256 devices in a mesh: group: 8 (over y, core), page: 32 (over x, z).
Axes of the slice: x: 4, y: 4, z: 8, core: 2. Of those that a mesh axis runs over, the one named last changes fastest.
Arguments:
- queries: bfloat16 [8, 2, 128, 576], P('group', None, 'page'), may hold values from -260 to 260
- cache: bfloat16 [8, 3072, 64, 576], P('group', 'page'), may hold values from -18 to 18
- slot_page: int32 [8, 3072], P('group', 'page'), may hold values from 0 to 3071, as said below
- lengths: int32 [8], P('group'), may hold values from 24576 to 196608, as said below
- w_uv: bfloat16 [128, 512, 128], P('page'), may hold values from -0.25 to 0.25
- w_out: bfloat16 [16384, 7168], P('page', 'group'), may hold values from -0.09375 to 0.09375
Outputs:
- output: bfloat16 [8, 2, 7168], P(None, None, ('group', 'page'))
The draws below stay inside these ranges and needn't reach their ends.
Inputs may be any that keep to these rules, and one draw needn't show every extreme that they name: `slot_page`: each request's row is a permutation; each index of page holds 96 consecutive logical pages. `lengths`: one request has exactly 196608 tokens.
All inputs are finite; a program needn't handle non-finite values.
Results may differ from the reference program's by a relative error of at most 0.015.
Values may be sent and summed in bfloat16 or wider, within the bound.
A program may use at most 64 MiB of HBM per device.

```python
import jax
import jax.numpy as jnp
from jax import lax

HEADS = 128
LAT = 512
ROPE = 64
VD = 128
D = 7168
PAGE = 64
QLEN = 2
PAGES_DEV = 96
REQS = 8
SLOTS = 3072
CONTEXT = 196608


def page_layout(key):
    base_key = jax.random.fold_in(key, 101)
    order_key, inner_key = jax.random.split(base_key)
    blocks = SLOTS // PAGES_DEV
    order = jax.vmap(lambda subkey: jax.random.permutation(subkey, blocks))(jax.random.split(order_key, REQS))
    inner = jax.vmap(lambda subkey: jax.random.permutation(subkey, PAGES_DEV))(jax.random.split(inner_key, REQS * blocks))
    layout = order.astype(jnp.int32)[:, :, None] * PAGES_DEV + inner.astype(jnp.int32).reshape(REQS, blocks, PAGES_DEV)
    return layout.reshape(REQS, SLOTS)


def drawn_pairs(key):
    planted_key = jax.random.fold_in(key, 202)
    return jnp.clip(jax.random.normal(planted_key, (REQS, 4, 2, LAT + ROPE), jnp.float32), -4.0, 4.0)


def strengths_and_mask():
    strengths = jnp.array([5.0, 8.0, 13.0, 20.0], jnp.float32)
    columns_idx = jnp.arange(LAT + ROPE)
    keep_mask = (columns_idx < LAT // 2) | (columns_idx >= LAT)
    return (strengths, keep_mask)


def drawn_gain():
    kept_count = LAT // 2 + ROPE
    return kept_count


def draw_slot_page(key, part):
    return page_layout(key)


def draw_lengths(key, part):
    key = jax.random.fold_in(key, 7)
    length_key, chosen_key = jax.random.split(key)
    drawn = jax.random.randint(length_key, (REQS,), CONTEXT // 8, CONTEXT + 1, jnp.int32)
    chosen = jax.random.randint(chosen_key, (), 0, REQS, jnp.int32)
    return jnp.where(jnp.arange(REQS, dtype=jnp.int32) == chosen, CONTEXT, drawn).astype(jnp.int32)


def draw_cache(key, part):
    layout = page_layout(key)
    pairs = drawn_pairs(key)
    key = jax.random.fold_in(key, 3)
    base_key, scale_key = jax.random.split(key)
    shape = (REQS, SLOTS, PAGE, LAT + ROPE)
    row_scale = jnp.exp(jax.random.uniform(scale_key, (REQS, SLOTS, PAGE, 1), jnp.float32, jnp.log(0.3), jnp.log(3.0)))
    base = jnp.clip(jax.random.normal(base_key, shape, jnp.float32), -6.0, 6.0) * row_scale
    strengths, keep_mask = strengths_and_mask()
    kept_count = drawn_gain()
    expected = strengths * kept_count * 192.0 ** (-0.5)
    epsilon = 2.0 / expected
    leading = pairs[:, :, 0]
    second = jnp.where(keep_mask[None, None, :], leading * (1.0 - epsilon[None, :, None]), pairs[:, :, 1])
    rows = jnp.stack([leading, second], axis=2).reshape(REQS, 8, LAT + ROPE)
    slot_first = jnp.argmax((layout == 0).astype(jnp.int32), axis=1).astype(jnp.int32)
    base = base.at[jnp.arange(REQS), slot_first, 0:8].set(rows)
    return base.astype(jnp.bfloat16)


def draw_queries(key, part):
    pairs = drawn_pairs(key)
    key = jax.random.fold_in(key, 5)
    base_key = jax.random.fold_in(key, 0)
    shape = (REQS, QLEN, HEADS, LAT + ROPE)
    base = jnp.clip(jax.random.normal(base_key, shape, jnp.float32), -6.0, 6.0) * 2.5
    strengths, keep_mask = strengths_and_mask()
    aligned = strengths[None, :, None] * jnp.where(keep_mask[None, None, :], pairs[:, :, 0], 0.0)
    filled = jnp.zeros(shape, jnp.float32).at[:, :, 0:4].set(jnp.broadcast_to(aligned[:, None], (REQS, QLEN, 4, LAT + ROPE)))
    head_index = jnp.arange(HEADS)[None, None, :, None]
    base = jnp.where(head_index < 4, filled, base)
    return base.astype(jnp.bfloat16)


def with_spikes(values, rng, source, target, parts, factor):
    owner, partner = [(jnp.arange(values.shape[dim]) // (values.shape[dim] // parts)).reshape([-1 if axis == dim else 1 for axis in range(values.ndim)]) for dim in (source, target)]
    chosen = jax.random.permutation(rng, parts)[partner]
    strong = (owner == chosen) | (owner == (partner + parts // 2) % parts)
    return jnp.where(strong, factor * values, values)


def levels(rng, shape, shards, smallest, top_value):
    factor_of, own = 1.0, jax.random.fold_in(rng, 6)
    for position, blocks in shards:
        heights = jnp.exp(jax.random.uniform(jax.random.fold_in(own, position), (blocks,), jnp.float32, smallest / len(shards), top_value / len(shards)))
        factor_of = factor_of * jnp.repeat(heights, shape[position] // blocks).reshape([-1 if axis == position else 1 for axis in range(len(shape))])
    return factor_of


def centred(own_key, extent, scale, reach, pieces=(), kind=jnp.bfloat16):
    values = jax.random.normal(own_key, extent, jnp.float32) * scale
    if len(pieces) > 0:
        values = levels(own_key, extent, pieces, -0.22, 0.18) * values
    return jnp.clip(values, min=-reach, max=reach).astype(kind)


def gaussian_with(rng, dims, deviation, most, cuts, heavy, kind=jnp.bfloat16):
    values = deviation * jax.random.normal(rng, dims, jnp.float32)
    if cuts:
        values = values * levels(rng, dims, cuts, -0.22, 0.18)
    return jnp.clip(with_spikes(values, jax.random.fold_in(rng, 3), *heavy), -most, most).astype(kind)


def setup_inputs(seed: int = 0) -> dict:
    seeds = jax.random.split(jax.random.key(seed), 7)
    queries = draw_queries(jax.random.fold_in(seeds[6], 71), 0)
    cache = draw_cache(jax.random.fold_in(seeds[6], 71), 0)
    slot_page = draw_slot_page(jax.random.fold_in(seeds[6], 71), 0)
    lengths = draw_lengths(jax.random.fold_in(seeds[6], 71), 0)
    w_uv = centred(seeds[4], (HEADS, LAT, VD), LAT ** -0.5, 0.25, ((0, 32),))
    w_out = gaussian_with(seeds[5], (HEADS * VD, D), (HEADS * VD) ** -0.5, 0.09375, ((0, 32), (1, 8)), (0, 1, 32, 2.75))
    return dict(queries=queries, cache=cache, slot_page=slot_page, lengths=lengths, w_uv=w_uv, w_out=w_out)


score_scale = 192.0 ** -0.5
masked_fill = -1.0e30


def one_request(inputs):
    query_rows, cache_rows, slot_rows, length = inputs
    width = cache_rows.shape[-1]
    key_rows = cache_rows.reshape(-1, width)
    positions = (slot_rows[:, None] * PAGE + jnp.arange(PAGE, dtype=jnp.int32)[None, :]).reshape(-1)
    limits = length - QLEN + jnp.arange(QLEN, dtype=jnp.int32)
    live_mask = positions[None, :] <= limits[:, None]
    live_mask = jnp.broadcast_to(live_mask[:, None, :], (QLEN, HEADS, positions.shape[0])).reshape(QLEN * HEADS, -1)
    scores = lax.dot_general(query_rows.reshape(-1, width), key_rows, (((1,), (1,)), ((), ())), preferred_element_type=jnp.float32) * score_scale
    masked = jnp.where(live_mask, scores, masked_fill)
    top_score = jnp.max(masked, axis=1)
    weights = jnp.where(live_mask, jnp.exp(masked - top_score[:, None]), 0.0).astype(jnp.bfloat16)
    total = jnp.sum(weights.astype(jnp.float32), axis=1)
    numerator = jnp.dot(weights, key_rows[:, :LAT], preferred_element_type=jnp.float32)
    attended = (numerator / total[:, None]).astype(jnp.bfloat16).reshape(QLEN, HEADS, LAT)
    return attended


def reference(queries, cache, slot_page, lengths, w_uv, w_out):
    attended = lax.map(one_request, (queries, cache, slot_page, lengths))
    values = jnp.einsum("rthl,hlv->rthv", attended.astype(jnp.float32), w_uv.astype(jnp.float32)).astype(jnp.bfloat16)
    flat_values = values.reshape(REQS * QLEN, HEADS * VD)
    output = jnp.dot(flat_values, w_out, preferred_element_type=jnp.float32).astype(jnp.bfloat16)
    return output.reshape(REQS, QLEN, D)
```

```python
import functools

import jax
import jax.numpy as jnp
from jax import lax
from jax.experimental import pallas as pl
from jax.experimental.pallas import tpu as pltpu
from jax.sharding import PartitionSpec as P

MESH = pl.DeviceIdType.MESH
F32 = jnp.float32
BF16 = jnp.bfloat16
score_scale = 192.0 ** (-0.5)
log2_e = 1.4426950408889634
masked_fill = -1e30
out_group = 32
step_keys = 1024
tile_keys = 256


def dot(a, b, contract_b=0):
    return lax.dot_general(a, b, (((1,), (contract_b,)), ((), ())), preferred_element_type=F32)


def kernel(
    sizes,
    q_hbm,
    k_hbm,
    page_hbm,
    length_hbm,
    up_hbm,
    out_hbm,
    result,
    q_in,
    q_rows,
    q_packed,
    q_all,
    keys,
    pages,
    length,
    w_up,
    w_out,
    w_placed,
    bias,
    scores,
    probs,
    peaks,
    sums,
    numer,
    num_send,
    num_recv,
    stat_send,
    stat_recv,
    low_stat_send,
    low_stat_recv,
    low_send,
    low_recv,
    head_values,
    term_send,
    term_recv,
    last_send,
    last_recv,
    local_sem,
    key_sem,
    qz_send,
    qz_recv,
    qx_send,
    qx_recv,
    st_send,
    st_recv,
    nx_send,
    nx_recv,
    ls_send,
    ls_recv,
    nz_send,
    nz_recv,
    v_send,
    v_recv,
    tx_send,
    tx_recv,
    tz_send,
    tz_recv,
):
    NX, NZ, NG, own_columns = sizes
    width = q_in.shape[-1]
    latent = w_up.shape[1]
    half = latent // 2
    key_rows = keys.shape[0]
    rows = q_all.shape[0]
    block = rows // NX
    steps = key_rows // step_keys
    tokens, heads = q_in.shape[1], q_in.shape[2]

    g = lax.axis_index("group")
    page = lax.axis_index("page")
    x, z = lax.div(page, NZ), lax.rem(page, NZ)

    def along_x(k):
        return {"page": lax.rem(x + k + NX, NX) * NZ + z}

    def along_z(k):
        return {"page": x * NZ + lax.rem(z + k + NZ, NZ)}

    def along_g(k):
        return {"group": lax.rem(g + k + NG, NG)}

    def send(source, target, send_sem, recv_sem, device):
        copy = pltpu.make_async_remote_copy(
            src_ref=source,
            dst_ref=target,
            send_sem=send_sem,
            recv_sem=recv_sem,
            device_id=device,
            device_id_type=MESH,
        )
        copy.start()
        return copy

    sent = []
    far_z = sorted(range(1, NZ), key=lambda k: -min(k, NZ - k))
    far_x = sorted(range(1, NX), key=lambda k: -min(k, NX - k))

    barrier = pltpu.get_barrier_semaphore()
    for k in range(1, NX):
        pl.semaphore_signal(barrier, inc=1, device_id=along_x(k), device_id_type=MESH)
    for k in range(1, NZ):
        pl.semaphore_signal(barrier, inc=1, device_id=along_z(k), device_id_type=MESH)
    for k in range(1, NG):
        pl.semaphore_signal(barrier, inc=1, device_id=along_g(k), device_id_type=MESH)

    def local(source, target, sem):
        copy = pltpu.make_async_copy(source, target, sem)
        copy.start()
        return copy

    q_copy = local(q_hbm, q_in, local_sem.at[0])
    page_copy = local(page_hbm, pages, local_sem.at[1])
    length_copy = local(length_hbm, length, local_sem.at[2])
    out_copy = local(out_hbm, w_out, local_sem.at[3])
    key_copies = [
        local(
            k_hbm.at[pl.ds(c * step_keys, step_keys)],
            keys.at[pl.ds(c * step_keys, step_keys)],
            key_sem.at[c],
        )
        for c in range(steps)
    ]
    up_copy = local(up_hbm, w_up, local_sem.at[4])

    q_copy.wait()
    q_rows[:, 512:768] = jnp.zeros((8, 256), F32)
    for t in range(tokens):
        q_rows[t * heads : (t + 1) * heads, 0:width] = q_in[0, t].astype(F32)
    q_packed[0, :, 0:128] = jnp.concatenate(
        [q_rows[:, 0:128], q_rows[:, 128:256]], axis=0
    ).astype(BF16)
    q_packed[0, :, 128:384] = jnp.concatenate(
        [q_rows[:, 256:512], q_rows[:, 512:768]], axis=0
    ).astype(BF16)
    pl.semaphore_wait(barrier, NX + NZ + NG - 3)
    parts = ((0, 128), (128, 384))
    places = ((0, 256), (256, 640))
    q_z = [{}, {}]
    for c, (low, high) in enumerate(parts):
        for k in far_z:
            q_z[c][k] = send(
                q_packed.at[0, :, low:high],
                q_packed.at[k, :, low:high],
                qz_send.at[c, k],
                qz_recv.at[c, k],
                along_z(k),
            )

    page_copy.wait()
    length_copy.wait()
    lane = lax.broadcasted_iota(jnp.int32, (8, 128), 1)
    token = lax.broadcasted_iota(jnp.int32, (8, 128), 0) // heads
    limit = length[0] - tokens + token
    for i in range(key_rows // 128):
        held = jnp.where(lane < 64, pages[0, 2 * i], pages[0, 2 * i + 1])
        position = held * 64 + lax.rem(lane, 64)
        bias[:, i * 128 : (i + 1) * 128] = jnp.where(position <= limit, 0.0, masked_fill)
    x_columns = own_columns * NZ
    x_lanes = out_group * NZ

    def place_columns():
        out_copy.wait()
        place = lax.broadcasted_iota(jnp.int32, (1, x_lanes), 1)
        inside = lax.rem(place, out_group)
        wanted = lax.div(place, out_group) * own_columns + inside
        wanted = jnp.where(inside < own_columns, wanted, -(2**20))
        for i in range(NX):
            low = i * x_columns // 128 * 128
            high = min(-(-(i + 1) * x_columns // 128) * 128, w_out.shape[1])
            column = lax.broadcasted_iota(jnp.int32, (high - low, x_lanes), 0)
            pick = jnp.where(column == wanted + (i * x_columns - low), 1.0, 0.0).astype(BF16)
            w_placed[:, i * x_lanes : (i + 1) * x_lanes] = dot(w_out[:, low:high], pick).astype(BF16)

    q_x = [{}, {}]
    relayed = [{}, {}]

    def q_block(c, first, target, count, k, sem):
        low, high = places[c]
        return send(
            q_all.at[pl.ds(first, count), low:high],
            q_all.at[pl.ds(target, count), low:high],
            qx_send.at[c, sem],
            qx_recv.at[c, sem],
            along_x(k),
        )

    for c in range(2):
        for k in far_z[::-1]:
            q_z[c][k].wait_recv()
        for k in range(0, NZ, 2):
            pair = []
            for j in (k, k + 1):
                part = q_packed[j, :, parts[c][0] : parts[c][1]].astype(F32)
                pair.append(
                    jnp.concatenate([part[0:8], part[8:16, 0:128]], axis=1)
                )
            q_all[k * 8 : k * 8 + 16, places[c][0] : places[c][1]] = jnp.concatenate(
                pair, axis=0
            ).astype(BF16)
        for k in far_x:
            if NX != 4 or k != 2:
                q_x[c][k] = q_block(c, 0, k * block, block, k, k)
        if c == 0:
            place_columns()
    if NX == 4:
        part = block // 2
        for c in range(2):
            q_x[c][1].wait_recv()
            relayed[c][1] = q_block(c, block, 2 * block, part, 1, 0)
            q_x[c][3].wait_recv()
            relayed[c][3] = q_block(c, 3 * block + part, 2 * block + part, part, -1, 2)
    for copy in key_copies:
        copy.wait()

    def wait_queries(c):
        for copy in (relayed[c] if NX == 4 else q_x[c]).values():
            copy.wait_recv()

    wait_queries(0)

    @pl.loop(0, steps)
    def _(c):
        for n in range(step_keys // tile_keys):
            at = pl.ds(pl.multiple_of(c * step_keys + n * tile_keys, tile_keys), tile_keys)
            scores[:, at] = dot(q_all[:, 0:256], keys[at, 0:256], 1)

    wait_queries(1)
    peaks[...] = jnp.full(peaks.shape, masked_fill, F32)

    @pl.loop(0, steps)
    def _(c):
        largest = peaks[...]
        for n in range(step_keys // tile_keys):
            at = pl.ds(pl.multiple_of(c * step_keys + n * tile_keys, tile_keys), tile_keys)
            s = scores[:, at] + dot(q_all[:, 256:width], keys[at, 256:width], 1)
            s = (s * (score_scale * log2_e)).reshape(rows // 8, 8, tile_keys) + bias[:, at][None]
            s = s.reshape(rows, tile_keys)
            scores[:, at] = s
            for j in range(0, tile_keys, 128):
                largest = jnp.maximum(largest, s[:, j : j + 128])
        peaks[...] = largest

    top = jnp.max(peaks[...], axis=1, keepdims=True)
    peaks[...] = jnp.broadcast_to(top, peaks.shape)
    sums[...] = jnp.zeros(sums.shape, F32)
    numer[...] = jnp.zeros(numer.shape, F32)

    @pl.loop(0, steps)
    def _(c):
        total = sums[...]
        top_here = peaks[...]
        pieces = []
        for n in range(step_keys // 128):
            at = pl.ds(pl.multiple_of(c * step_keys + n * 128, 128), 128)
            p = jnp.exp2(scores[:, at] - top_here)
            total = total + p
            p = p.astype(BF16)
            probs[:, at] = p
            pieces.append(p)
        sums[...] = total
        here = pl.ds(pl.multiple_of(c * step_keys, step_keys), step_keys)
        numer[0] += dot(jnp.concatenate(pieces, axis=1), keys[here, 0:half])

    total = jnp.broadcast_to(jnp.sum(sums[...], axis=1, keepdims=True), (rows, 128))
    sums[...] = total
    owner = lax.div(lax.broadcasted_iota(jnp.int32, (8, 128), 1), 8)
    for i in range(NX):
        tile = jnp.zeros((8, 128), F32)
        for v in range(NZ):
            at = pl.ds(i * block + v * 8, 8)
            tile = jnp.where(owner == v, peaks[at, :], tile)
            tile = jnp.where(owner == v + 8, sums[at, :], tile)
        stat_send[i] = tile
    stats = {}
    for k in far_x:
        stats[k] = send(
            stat_send.at[k], stat_recv.at[k], st_send.at[k], st_recv.at[k], along_x(-k)
        )

    num_x = [{}, {}]

    def send_half(h):
        num_send[h] = numer[h].astype(BF16)
        for k in far_x:
            num_x[h][k] = send(
                num_send.at[h, pl.ds(k * block, block)],
                num_recv.at[h, k],
                nx_send.at[h, k],
                nx_recv.at[h, k],
                along_x(-k),
            )

    send_half(0)

    @pl.loop(0, steps)
    def _(c):
        here = pl.ds(pl.multiple_of(c * step_keys, step_keys), step_keys)
        numer[1] += dot(probs[:, here], keys[here, half:latent])

    send_half(1)

    for k in far_x[::-1]:
        stats[k].wait_recv()
    found = [stat_send[0]] + [stat_recv[k] for k in range(1, NX)]
    factors = [[] for _ in found]
    for v in range(NZ):
        tops = [jnp.broadcast_to(f[:, 8 * v : 8 * v + 1], (8, 128)) for f in found]
        top_x = functools.reduce(jnp.maximum, tops)
        total_x = jnp.zeros((8, 128), F32)
        for f, t, held in zip(found, tops, factors):
            held.append(jnp.exp2(t - top_x))
            total_x = total_x + f[:, 64 + 8 * v : 64 + 8 * v + 1] * held[v]
        low_stat_send[v] = jnp.where(lane < 64, top_x, total_x)
    factors = [
        jnp.concatenate([jnp.concatenate(held, axis=0)] * (half // 128), axis=1) for held in factors
    ]
    low_stats = {}
    for k in far_z:
        low_stats[k] = send(
            low_stat_send.at[k],
            low_stat_recv.at[k],
            ls_send.at[k],
            ls_recv.at[k],
            along_z(-k),
        )

    num_z = [{}, {}]
    own_half = []
    for h in range(2):
        for k in far_x[::-1]:
            num_x[h][k].wait_recv()
        merged = numer[h, 0:block, :] * factors[0]
        for k in range(1, NX):
            merged = merged + num_recv[h, k].astype(F32) * factors[k]
        own_half.append(
            [merged[0:8, j : j + 128] for j in range(0, half, 128)]
        )
        for k in far_z:
            part = merged[k * 8 : (k + 1) * 8]
            low_send[h, k] = jnp.concatenate([part[:, 0:128], part[:, 128:256]], axis=0).astype(BF16)
            num_z[h][k] = send(
                low_send.at[h, k],
                low_recv.at[h, k],
                nz_send.at[h, k],
                nz_recv.at[h, k],
                along_z(-k),
            )

    for k in far_z[::-1]:
        low_stats[k].wait_recv()
    found = [low_stat_send[0]] + [low_stat_recv[k] for k in range(1, NZ)]
    tops = [f[:, 0:1] for f in found]
    top_z = functools.reduce(jnp.maximum, tops)
    factors = [jnp.broadcast_to(jnp.exp2(t - top_z), (8, 128)) for t in tops]
    total_z = sum(f[:, 64:65] * w for f, w in zip(found, factors))
    attended = []
    for h in range(2):
        for k in far_z[::-1]:
            num_z[h][k].wait_recv()
        for j in range(2):
            merged = own_half[h][j] * factors[0]
            for k in range(1, NZ):
                merged = merged + low_recv[h, k].astype(F32)[j * 8 : (j + 1) * 8] * factors[k]
            attended.append(merged / total_z)
    attended = jnp.concatenate(attended, axis=1)
    head = lax.rem(lax.broadcasted_iota(jnp.int32, attended.shape, 0), heads)
    spread = [jnp.where(head == i, attended, 0.0) for i in range(heads)]
    up_copy.wait()
    values = dot(
        jnp.concatenate(spread, axis=1).astype(BF16), w_up[...].reshape(heads * latent, -1)
    )

    own = pl.ds(pl.multiple_of(g * 8, 8), 8)
    head_values[own, :] = values.astype(BF16).astype(F32)
    moved = {}
    for k in range(1, NG):
        moved[k] = send(
            head_values.at[own], head_values.at[own], v_send.at[k], v_recv.at[k], along_g(k)
        )
    for k in range(1, NG):
        moved[k].wait_recv()
    wide = [head_values[pl.ds(i, tokens * NG, stride=heads), :] for i in range(heads)]
    terms = dot(jnp.concatenate(wide, axis=1).astype(BF16), w_placed[...])

    for i in range(NX):
        term_send[i] = terms[:, i * x_lanes : (i + 1) * x_lanes].astype(BF16)
    tx = {}
    for k in far_x:
        tx[k] = send(
            term_send.at[lax.rem(x + k, NX)],
            term_recv.at[k],
            tx_send.at[k],
            tx_recv.at[k],
            along_x(k),
        )
    summed = term_send[x].astype(F32)
    for k in far_x[::-1]:
        tx[k].wait_recv()
    for k in range(1, NX):
        summed = summed + term_recv[k].astype(F32)
    for i in range(x_lanes // 128):
        last_send[i] = summed[:, i * 128 : (i + 1) * 128].astype(BF16)
    per_tile = 128 // out_group
    tz = {}
    for k in far_z:
        tz[k] = send(
            last_send.at[lax.div(lax.rem(z + k, NZ), per_tile)],
            last_recv.at[k],
            tz_send.at[k],
            tz_recv.at[k],
            along_z(k),
        )
    final = last_send[lax.div(z, per_tile)].astype(F32)
    for k in far_z[::-1]:
        tz[k].wait_recv()
    for k in range(1, NZ):
        final = final + last_recv[k].astype(F32)
    place = lax.rem(z, per_tile)
    chosen = final
    for i in range(1, per_tile):
        chosen = jnp.where(place == i, pltpu.roll(final, 128 - i * out_group, 1), chosen)
    result[...] = chosen

    for group in (*q_z, *q_x, *relayed, stats, num_x[0], num_x[1], low_stats, num_z[0], num_z[1], moved, tx, tz):
        for copy in group.values():
            copy.wait_send()


def body(sizes, queries, cache, slot_page, lengths, w_uv, w_out):
    NX, NZ, NG, own_columns = sizes
    tokens, heads, width = queries.shape[1:]
    latent = w_uv.shape[1]
    half = latent // 2
    key_rows = cache.shape[1] * cache.shape[2]
    rows = NX * NZ * 8
    block = NZ * 8
    x_lanes = NZ * out_group
    sem = pltpu.SemaphoreType.DMA
    scratch = [
        pltpu.VMEM(queries.shape, BF16),
        pltpu.VMEM((8, 768), F32),
        pltpu.VMEM((NZ, 16, 384), BF16),
        pltpu.VMEM((rows, 640), BF16),
        pltpu.VMEM((key_rows, width), BF16),
        pltpu.SMEM(slot_page.shape, jnp.int32),
        pltpu.SMEM(lengths.shape, jnp.int32),
        pltpu.VMEM(w_uv.shape, BF16),
        pltpu.VMEM(w_out.shape, BF16),
        pltpu.VMEM((w_out.shape[0], NX * x_lanes), BF16),
        pltpu.VMEM((8, key_rows), F32),
        pltpu.VMEM((rows, key_rows), F32),
        pltpu.VMEM((rows, key_rows), BF16),
        pltpu.VMEM((rows, 128), F32),
        pltpu.VMEM((rows, 128), F32),
        pltpu.VMEM((2, rows, half), F32),
        pltpu.VMEM((2, rows, half), BF16),
        pltpu.VMEM((2, NX, block, half), BF16),
        pltpu.VMEM((NX, 8, 128), F32),
        pltpu.VMEM((NX, 8, 128), F32),
        pltpu.VMEM((NZ, 8, 128), F32),
        pltpu.VMEM((NZ, 8, 128), F32),
        pltpu.VMEM((2, NZ, 16, 128), BF16),
        pltpu.VMEM((2, NZ, 16, 128), BF16),
        pltpu.VMEM((NG * 8, 128), F32),
        pltpu.VMEM((NX, tokens * NG, x_lanes), BF16),
        pltpu.VMEM((NX, tokens * NG, x_lanes), BF16),
        pltpu.VMEM((x_lanes // 128, tokens * NG, 128), BF16),
        pltpu.VMEM((NZ, tokens * NG, 128), BF16),
        sem((5,)),
        sem((key_rows // step_keys,)),
        sem((2, NZ)),
        sem((2, NZ)),
        sem((2, NX)),
        sem((2, NX)),
        sem((NX,)),
        sem((NX,)),
        sem((2, NX)),
        sem((2, NX)),
        sem((NZ,)),
        sem((NZ,)),
        sem((2, NZ)),
        sem((2, NZ)),
        sem((NG,)),
        sem((NG,)),
        sem((NX,)),
        sem((NX,)),
        sem((NZ,)),
        sem((NZ,)),
    ]
    result = pl.pallas_call(
        functools.partial(kernel, sizes),
        out_shape=jax.ShapeDtypeStruct((tokens * NG, 128), F32),
        in_specs=[pl.BlockSpec(memory_space=pltpu.HBM)] * 6,
        out_specs=pl.BlockSpec(memory_space=pltpu.VMEM),
        scratch_shapes=scratch,
        compiler_params=pltpu.CompilerParams(
            collective_id=0, has_side_effects=True, vmem_limit_bytes=56 * 1024 * 1024
        ),
    )(queries, cache.reshape(key_rows, width), slot_page, lengths, w_uv, w_out)
    return result[:, 0:own_columns].astype(BF16).reshape(NG, tokens, own_columns)


def solution(mesh, NX=4):
    NG, pages = mesh.shape["group"], mesh.shape["page"]
    in_specs = (
        P("group", None, "page", None),
        P("group", "page", None, None),
        P("group", "page"),
        P("group"),
        P("page", None, None),
        P("page", "group"),
    )
    out_specs = P(None, None, ("group", "page"))

    def step(queries, cache, slot_page, lengths, w_uv, w_out):
        sizes = (NX, pages // NX, NG, w_out.shape[1] // pages)
        return body(sizes, queries, cache, slot_page, lengths, w_uv, w_out)

    return jax.shard_map(step, mesh=mesh, in_specs=in_specs, out_specs=out_specs, check_vma=False)
```

```python
import functools

import jax
import jax.numpy as jnp
from jax import lax
from jax.experimental import pallas as pl
from jax.experimental.pallas import tpu as pltpu
from jax.sharding import PartitionSpec as P

MESH = pl.DeviceIdType.MESH
F32 = jnp.float32
BF16 = jnp.bfloat16
score_scale = 192.0 ** (-0.5)
log2_e = 1.4426950408889634
masked_fill = -(2.0**99)
out_group = 32
step_keys = 1024
tile_keys = 256


def dot(a, b, contract_b=0):
    return lax.dot_general(a, b, (((1,), (contract_b,)), ((), ())), preferred_element_type=F32)


def kernel(
    sizes,
    q_hbm,
    k_hbm,
    page_hbm,
    length_hbm,
    up_hbm,
    out_hbm,
    result,
    q_in,
    q_rows,
    q_packed,
    q_all,
    keys,
    pages,
    length,
    w_up,
    w_out,
    w_placed,
    bias,
    scores,
    probs,
    peaks,
    sums,
    numer,
    num_send,
    num_recv,
    stat_send,
    stat_recv,
    low_send,
    low_recv,
    head_values,
    term_send,
    term_recv,
    last_send,
    last_recv,
    local_sem,
    key_sem,
    qz_send,
    qz_recv,
    qx_send,
    qx_recv,
    st_send,
    st_recv,
    nx_send,
    nx_recv,
    nz_send,
    nz_recv,
    v_send,
    v_recv,
    tx_send,
    tx_recv,
    tz_send,
    tz_recv,
):
    NX, NZ, NG, own_columns = sizes
    width = q_in.shape[-1]
    latent = w_up.shape[1]
    half = latent // 2
    key_rows = keys.shape[0]
    rows = q_all.shape[0]
    block = rows // NX
    steps = key_rows // step_keys
    tokens, heads = q_in.shape[1], q_in.shape[2]

    g = lax.axis_index("group")
    page = lax.axis_index("page")
    x, z = lax.div(page, NZ), lax.rem(page, NZ)

    def along_x(k):
        return {"page": lax.rem(x + k + NX, NX) * NZ + z}

    def along_z(k):
        return {"page": x * NZ + lax.rem(z + k + NZ, NZ)}

    def along_g(k):
        return {"group": lax.rem(g + k + NG, NG)}

    def send(source, target, send_sem, recv_sem, device):
        copy = pltpu.make_async_remote_copy(
            src_ref=source,
            dst_ref=target,
            send_sem=send_sem,
            recv_sem=recv_sem,
            device_id=device,
            device_id_type=MESH,
        )
        copy.start()
        return copy

    def done(region, sem):
        pltpu.make_async_copy(region, region, sem).wait()

    far_z = sorted(range(1, NZ), key=lambda k: -min(k, NZ - k))
    far_x = sorted(range(1, NX), key=lambda k: -min(k, NX - k))

    barrier = pltpu.get_barrier_semaphore()
    for k in range(1, NX):
        pl.semaphore_signal(barrier, inc=1, device_id=along_x(k), device_id_type=MESH)
    for k in range(1, NZ):
        pl.semaphore_signal(barrier, inc=1, device_id=along_z(k), device_id_type=MESH)
    for k in range(1, NG):
        pl.semaphore_signal(barrier, inc=1, device_id=along_g(k), device_id_type=MESH)

    def local(source, target, sem):
        copy = pltpu.make_async_copy(source, target, sem)
        copy.start()
        return copy

    q_copy = local(q_hbm, q_in, local_sem.at[0])
    page_copy = local(page_hbm, pages, local_sem.at[1])
    length_copy = local(length_hbm, length, local_sem.at[2])
    out_copy = local(out_hbm, w_out, local_sem.at[3])
    key_copies = [
        local(
            k_hbm.at[pl.ds(c * step_keys, step_keys)],
            keys.at[pl.ds(c * step_keys, step_keys)],
            key_sem.at[c],
        )
        for c in range(steps)
    ]
    up_copy = local(up_hbm, w_up, local_sem.at[4])

    q_copy.wait()
    q_rows[:, 512:768] = jnp.zeros((8, 256), F32)
    for t in range(tokens):
        q_rows[t * heads : (t + 1) * heads, 0:width] = q_in[0, t].astype(F32)
    q_packed[0] = jnp.concatenate([q_rows[:, 0:384], q_rows[:, 384:768]], axis=0).astype(BF16)
    pl.semaphore_wait(barrier, NX + NZ + NG - 3)
    for k in far_z:
        send(q_packed.at[0], q_packed.at[k], qz_send, qz_recv, along_z(k))

    page_copy.wait()
    length_copy.wait()
    lane = lax.broadcasted_iota(jnp.int32, (8, 128), 1)
    token = lax.broadcasted_iota(jnp.int32, (8, 128), 0) // heads
    limit = length[0] - tokens + token
    for i in range(key_rows // 128):
        held = jnp.where(lane < 64, pages[0, 2 * i], pages[0, 2 * i + 1])
        position = held * 64 + lax.rem(lane, 64)
        bias[:, i * 128 : (i + 1) * 128] = jnp.where(position <= limit, 0.0, masked_fill)
    done(q_packed.at[pl.ds(1, NZ - 1)], qz_recv)
    for k in range(0, NZ, 2):
        pair = []
        for j in (k, k + 1):
            part = q_packed[j].astype(F32)
            pair.append(jnp.concatenate([part[0:8], part[8:16, 0:256]], axis=1))
        q_all[k * 8 : k * 8 + 16, :] = jnp.concatenate(pair, axis=0).astype(BF16)
    for k in far_x:
        send(
            q_all.at[pl.ds(0, block)],
            q_all.at[pl.ds(k * block, block)],
            qx_send,
            qx_recv,
            along_x(k),
        )

    x_columns = own_columns * NZ
    x_lanes = out_group * NZ
    out_copy.wait()
    place = lax.broadcasted_iota(jnp.int32, (1, x_lanes), 1)
    inside = lax.rem(place, out_group)
    wanted = lax.div(place, out_group) * own_columns + inside
    wanted = jnp.where(inside < own_columns, wanted, -(2**20))
    for i in range(NX):
        low = i * x_columns // 128 * 128
        high = min(-(-(i + 1) * x_columns // 128) * 128, w_out.shape[1])
        column = lax.broadcasted_iota(jnp.int32, (high - low, x_lanes), 0)
        pick = jnp.where(column == wanted + (i * x_columns - low), 1.0, 0.0).astype(BF16)
        w_placed[:, i * x_lanes : (i + 1) * x_lanes] = dot(w_out[:, low:high], pick).astype(BF16)
    done(q_packed.at[pl.ds(1, NZ - 1)], qz_send)
    for copy in key_copies:
        copy.wait()
    done(q_all.at[pl.ds(block, rows - block)], qx_recv)

    peaks[...] = jnp.full(peaks.shape, masked_fill, F32)

    @pl.loop(0, steps)
    def _(c):
        largest = peaks[...]
        for n in range(step_keys // tile_keys):
            at = pl.ds(pl.multiple_of(c * step_keys + n * tile_keys, tile_keys), tile_keys)
            s = dot(q_all[:, 0:width], keys[at, :], 1) * (score_scale * log2_e)
            s = s.reshape(rows // 8, 8, tile_keys) + bias[:, at][None]
            s = s.reshape(rows, tile_keys)
            scores[:, at] = s
            for j in range(0, tile_keys, 128):
                largest = jnp.maximum(largest, s[:, j : j + 128])
        peaks[...] = largest

    top = jnp.max(peaks[...], axis=1, keepdims=True)
    peaks[...] = jnp.broadcast_to(top, peaks.shape)
    sums[...] = jnp.zeros(sums.shape, F32)
    numer[...] = jnp.zeros(numer.shape, F32)

    @pl.loop(0, steps)
    def _(c):
        total = sums[...]
        top_here = peaks[...]
        pieces = []
        for n in range(step_keys // 128):
            at = pl.ds(pl.multiple_of(c * step_keys + n * 128, 128), 128)
            p = jnp.exp2(scores[:, at] - top_here)
            total = total + p
            p = p.astype(BF16)
            probs[:, at] = p
            pieces.append(p)
        sums[...] = total
        here = pl.ds(pl.multiple_of(c * step_keys, step_keys), step_keys)
        numer[0] += dot(jnp.concatenate(pieces, axis=1), keys[here, 0:half])

    total = jnp.broadcast_to(jnp.sum(sums[...], axis=1, keepdims=True), (rows, 128))
    sums[...] = total
    owner = lax.div(lax.broadcasted_iota(jnp.int32, (8, 128), 1), 8)
    for i in range(NX):
        tile = jnp.zeros((8, 128), F32)
        for v in range(NZ):
            at = pl.ds(i * block + v * 8, 8)
            tile = jnp.where(owner == v, peaks[at, :], tile)
            tile = jnp.where(owner == v + 8, sums[at, :], tile)
        stat_send[i] = tile
    for k in far_x:
        send(stat_send.at[k], stat_recv.at[k], st_send, st_recv, along_x(-k))

    def send_half(h):
        num_send[h] = numer[h].astype(BF16)
        for k in far_x:
            send(
                num_send.at[h, pl.ds(k * block, block)],
                num_recv.at[h, k],
                nx_send.at[h],
                nx_recv.at[h],
                along_x(-k),
            )

    send_half(0)

    @pl.loop(0, steps)
    def _(c):
        here = pl.ds(pl.multiple_of(c * step_keys, step_keys), step_keys)
        numer[1] += dot(probs[:, here], keys[here, half:latent])

    send_half(1)
    done(q_all.at[pl.ds(block, rows - block)], qx_send)

    done(stat_recv.at[pl.ds(1, NX - 1)], st_recv)
    found = [stat_send[0]] + [stat_recv[k] for k in range(1, NX)]
    factors = [[] for _ in found]
    z_stats = []
    for v in range(NZ):
        tops = [jnp.broadcast_to(f[:, 8 * v : 8 * v + 1], (8, 128)) for f in found]
        top_x = functools.reduce(jnp.maximum, tops)
        coarse = top_x.astype(BF16).astype(F32)
        top_x = coarse + (top_x - coarse).astype(BF16).astype(F32)
        total_x = jnp.zeros((8, 128), F32)
        for f, t, held in zip(found, tops, factors):
            held.append(jnp.exp2(t - top_x))
            total_x = total_x + f[:, 64 + 8 * v : 64 + 8 * v + 1] * held[v]
        z_stats.append(jnp.where(lane < 64, top_x, total_x))
        if v > 0:
            coarse = z_stats[v].astype(BF16).astype(F32)
            low_send[v, :, 128:256] = jnp.concatenate(
                [coarse, z_stats[v] - coarse], axis=0
            ).astype(BF16)
    factors = [
        jnp.concatenate([jnp.concatenate(held, axis=0)] * (half // 128), axis=1) for held in factors
    ]

    spans = ((0, 256), (256, 384))
    own_half = []
    for h in range(2):
        done(num_recv.at[h, pl.ds(1, NX - 1)], nx_recv.at[h])
        merged = numer[h, 0:block, :] * factors[0]
        for k in range(1, NX):
            merged = merged + num_recv[h, k].astype(F32) * factors[k]
        own_half.append([merged[0:8, j : j + 128] for j in range(0, half, 128)])
        low, high = spans[h]
        for k in far_z:
            part = merged[k * 8 : (k + 1) * 8]
            low_send[k, :, low : low + 128] = jnp.concatenate(
                [part[:, 0:128], part[:, 128:256]], axis=0
            ).astype(BF16)
            send(
                low_send.at[k, :, low:high],
                low_recv.at[k, :, low:high],
                nz_send.at[h],
                nz_recv.at[h],
                along_z(-k),
            )
    done(stat_recv.at[pl.ds(1, NX - 1)], st_send)
    for h in range(2):
        done(num_recv.at[h, pl.ds(1, NX - 1)], nx_send.at[h])

    done(low_recv.at[pl.ds(1, NZ - 1), :, 0:256], nz_recv.at[0])
    found = [z_stats[0]]
    for k in range(1, NZ):
        held = low_recv[k, :, 128:256].astype(F32)
        found.append(held[0:8] + held[8:16])
    tops = [jnp.broadcast_to(f[:, 0:1], (8, 128)) for f in found]
    top_z = functools.reduce(jnp.maximum, tops)
    factors = [jnp.exp2(t - top_z) for t in tops]
    total_z = sum(f[:, 64:65] * w for f, w in zip(found, factors))
    attended = []
    for h in range(2):
        if h == 1:
            done(low_recv.at[pl.ds(1, NZ - 1), :, 256:384], nz_recv.at[1])
        merged = [own * factors[0] for own in own_half[h]]
        for k in range(1, NZ):
            held = low_recv[k, :, spans[h][0] : spans[h][0] + 128].astype(F32)
            for j in range(2):
                merged[j] = merged[j] + held[j * 8 : (j + 1) * 8] * factors[k]
        attended += [m / total_z for m in merged]
    attended = jnp.concatenate(attended, axis=1)
    head = lax.rem(lax.broadcasted_iota(jnp.int32, attended.shape, 0), heads)
    spread = [jnp.where(head == i, attended, 0.0) for i in range(heads)]
    up_copy.wait()
    values = dot(
        jnp.concatenate(spread, axis=1).astype(BF16), w_up[...].reshape(heads * latent, -1)
    )

    own = pl.ds(pl.multiple_of(g * 8, 8), 8)
    head_values[own, :] = values.astype(BF16).astype(F32)
    for k in range(1, NG):
        send(head_values.at[own], head_values.at[own], v_send, v_recv, along_g(k))
    others = head_values.at[pl.ds(0, (NG - 1) * 8)]
    done(low_recv.at[pl.ds(1, NZ - 1), :, 0:256], nz_send.at[0])
    done(low_recv.at[pl.ds(1, NZ - 1), :, 256:384], nz_send.at[1])
    done(others, v_recv)
    wide = [head_values[pl.ds(i, tokens * NG, stride=heads), :] for i in range(heads)]
    terms = dot(jnp.concatenate(wide, axis=1).astype(BF16), w_placed[...])

    for i in range(NX):
        term_send[i] = terms[:, i * x_lanes : (i + 1) * x_lanes].astype(BF16)
    for k in far_x:
        send(term_send.at[lax.rem(x + k, NX)], term_recv.at[k], tx_send, tx_recv, along_x(k))
    done(others, v_send)
    summed = term_send[x].astype(F32)
    done(term_recv.at[pl.ds(1, NX - 1)], tx_recv)
    for k in range(1, NX):
        summed = summed + term_recv[k].astype(F32)
    for i in range(x_lanes // 128):
        last_send[i] = summed[:, i * 128 : (i + 1) * 128].astype(BF16)
    per_tile = 128 // out_group
    for k in far_z:
        send(
            last_send.at[lax.div(lax.rem(z + k, NZ), per_tile)],
            last_recv.at[k],
            tz_send,
            tz_recv,
            along_z(k),
        )
    done(term_recv.at[pl.ds(1, NX - 1)], tx_send)
    final = last_send[lax.div(z, per_tile)].astype(F32)
    done(last_recv.at[pl.ds(1, NZ - 1)], tz_recv)
    for k in range(1, NZ):
        final = final + last_recv[k].astype(F32)
    place = lax.rem(z, per_tile)
    chosen = final
    for i in range(1, per_tile):
        chosen = jnp.where(place == i, pltpu.roll(final, 128 - i * out_group, 1), chosen)
    result[...] = chosen
    done(last_recv.at[pl.ds(1, NZ - 1)], tz_send)


def body(sizes, queries, cache, slot_page, lengths, w_uv, w_out):
    NX, NZ, NG, own_columns = sizes
    tokens, heads, width = queries.shape[1:]
    latent = w_uv.shape[1]
    half = latent // 2
    key_rows = cache.shape[1] * cache.shape[2]
    rows = NX * NZ * 8
    block = NZ * 8
    x_lanes = NZ * out_group
    sem = pltpu.SemaphoreType.DMA
    scratch = [
        pltpu.VMEM(queries.shape, BF16),
        pltpu.VMEM((8, 768), F32),
        pltpu.VMEM((NZ, 16, 384), BF16),
        pltpu.VMEM((rows, 640), BF16),
        pltpu.VMEM((key_rows, width), BF16),
        pltpu.SMEM(slot_page.shape, jnp.int32),
        pltpu.SMEM(lengths.shape, jnp.int32),
        pltpu.VMEM(w_uv.shape, BF16),
        pltpu.VMEM(w_out.shape, BF16),
        pltpu.VMEM((w_out.shape[0], NX * x_lanes), BF16),
        pltpu.VMEM((8, key_rows), F32),
        pltpu.VMEM((rows, key_rows), F32),
        pltpu.VMEM((rows, key_rows), BF16),
        pltpu.VMEM((rows, 128), F32),
        pltpu.VMEM((rows, 128), F32),
        pltpu.VMEM((2, rows, half), F32),
        pltpu.VMEM((2, rows, half), BF16),
        pltpu.VMEM((2, NX, block, half), BF16),
        pltpu.VMEM((NX, 8, 128), F32),
        pltpu.VMEM((NX, 8, 128), F32),
        pltpu.VMEM((NZ, 16, 384), BF16),
        pltpu.VMEM((NZ, 16, 384), BF16),
        pltpu.VMEM((NG * 8, 128), F32),
        pltpu.VMEM((NX, tokens * NG, x_lanes), BF16),
        pltpu.VMEM((NX, tokens * NG, x_lanes), BF16),
        pltpu.VMEM((x_lanes // 128, tokens * NG, 128), BF16),
        pltpu.VMEM((NZ, tokens * NG, 128), BF16),
        sem((5,)),
        sem((key_rows // step_keys,)),
        sem,
        sem,
        sem,
        sem,
        sem,
        sem,
        sem((2,)),
        sem((2,)),
        sem((2,)),
        sem((2,)),
        sem,
        sem,
        sem,
        sem,
        sem,
        sem,
    ]
    result = pl.pallas_call(
        functools.partial(kernel, sizes),
        out_shape=jax.ShapeDtypeStruct((tokens * NG, 128), F32),
        in_specs=[pl.BlockSpec(memory_space=pltpu.HBM)] * 6,
        out_specs=pl.BlockSpec(memory_space=pltpu.VMEM),
        scratch_shapes=scratch,
        compiler_params=pltpu.CompilerParams(
            collective_id=0, has_side_effects=True, vmem_limit_bytes=56 * 1024 * 1024
        ),
    )(queries, cache.reshape(key_rows, width), slot_page, lengths, w_uv, w_out)
    return result[:, 0:own_columns].astype(BF16).reshape(NG, tokens, own_columns)


def solution(mesh, NX=4):
    NG, pages = mesh.shape["group"], mesh.shape["page"]
    in_specs = (
        P("group", None, "page", None),
        P("group", "page", None, None),
        P("group", "page"),
        P("group"),
        P("page", None, None),
        P("page", "group"),
    )
    out_specs = P(None, None, ("group", "page"))

    def step(queries, cache, slot_page, lengths, w_uv, w_out):
        sizes = (NX, pages // NX, NG, w_out.shape[1] // pages)
        return body(sizes, queries, cache, slot_page, lengths, w_uv, w_out)

    return jax.shard_map(step, mesh=mesh, in_specs=in_specs, out_specs=out_specs, check_vma=False)
```

```python
import functools

import jax
import jax.numpy as jnp
from jax import lax
from jax.experimental import pallas as pl
from jax.experimental.pallas import tpu as pltpu
from jax.sharding import PartitionSpec as P

MESH = pl.DeviceIdType.MESH
F32 = jnp.float32
BF16 = jnp.bfloat16
score_scale = 192.0 ** (-0.5)
log2_e = 1.4426950408889634
masked_fill = -(2.0**99)
out_group = 32
step_keys = 1024
tile_keys = 256


def dot(a, b, contract_b=0):
    return lax.dot_general(a, b, (((1,), (contract_b,)), ((), ())), preferred_element_type=F32)


def kernel(
    sizes,
    q_hbm,
    k_hbm,
    page_hbm,
    length_hbm,
    up_hbm,
    out_hbm,
    result,
    q_in,
    q_rows,
    q_packed,
    q_all,
    keys,
    pages,
    length,
    w_up,
    w_out,
    w_placed,
    bias,
    scores,
    probs,
    numer,
    num_send,
    num_recv,
    stat_send,
    stat_recv,
    low_send,
    low_recv,
    head_values,
    term_send,
    term_recv,
    last_send,
    last_recv,
    local_sem,
    key_sem,
    qz_send,
    qz_recv,
    qx_send,
    qx_recv,
    st_send,
    st_recv,
    nx_send,
    nx_recv,
    nz_send,
    nz_recv,
    v_send,
    v_recv,
    tx_send,
    tx_recv,
    tz_send,
    tz_recv,
):
    NX, NZ, NG, own_columns = sizes
    width = q_in.shape[-1]
    latent = w_up.shape[1]
    half = latent // 2
    key_rows = keys.shape[0]
    rows = q_all.shape[0]
    block = rows // NX
    steps = key_rows // step_keys
    tokens, heads = q_in.shape[1], q_in.shape[2]

    g = lax.axis_index("group")
    page = lax.axis_index("page")
    x, z = lax.div(page, NZ), lax.rem(page, NZ)

    def along_x(k):
        return {"page": lax.rem(x + k + NX, NX) * NZ + z}

    def along_z(k):
        return {"page": x * NZ + lax.rem(z + k + NZ, NZ)}

    def along_g(k):
        return {"group": lax.rem(g + k + NG, NG)}

    def send(source, target, send_sem, recv_sem, device):
        copy = pltpu.make_async_remote_copy(
            src_ref=source,
            dst_ref=target,
            send_sem=send_sem,
            recv_sem=recv_sem,
            device_id=device,
            device_id_type=MESH,
        )
        copy.start()
        return copy

    def done(region, sem):
        pltpu.make_async_copy(region, region, sem).wait()

    far_z = sorted(range(1, NZ), key=lambda k: -min(k, NZ - k))
    far_x = sorted(range(1, NX), key=lambda k: -min(k, NX - k))

    barrier = pltpu.get_barrier_semaphore()
    for k in range(1, NX):
        pl.semaphore_signal(barrier, inc=1, device_id=along_x(k), device_id_type=MESH)
    for k in range(1, NZ):
        pl.semaphore_signal(barrier, inc=1, device_id=along_z(k), device_id_type=MESH)
    for k in range(1, NG):
        pl.semaphore_signal(barrier, inc=1, device_id=along_g(k), device_id_type=MESH)

    def local(source, target, sem):
        copy = pltpu.make_async_copy(source, target, sem)
        copy.start()
        return copy

    q_copy = local(q_hbm, q_in, local_sem.at[0])
    page_copy = local(page_hbm, pages, local_sem.at[1])
    length_copy = local(length_hbm, length, local_sem.at[2])
    out_copy = local(out_hbm, w_out, local_sem.at[3])
    key_copies = [
        local(
            k_hbm.at[pl.ds(c * step_keys, step_keys)],
            keys.at[pl.ds(c * step_keys, step_keys)],
            key_sem.at[c],
        )
        for c in range(steps)
    ]
    up_copy = local(up_hbm, w_up, local_sem.at[4])

    q_copy.wait()
    q_rows[:, 512:768] = jnp.zeros((8, 256), F32)
    for t in range(tokens):
        q_rows[t * heads : (t + 1) * heads, 0:width] = q_in[0, t].astype(F32)
    q_packed[0, 0] = jnp.concatenate([q_rows[:, 0:384], q_rows[:, 384:768]], axis=0).astype(BF16)
    pl.semaphore_wait(barrier, NX + NZ + NG - 3)
    for k in far_z:
        send(q_packed.at[0, 0], q_packed.at[0, k], qz_send, qz_recv.at[k], along_z(k))

    def forward(j):
        for k in far_x:
            send(q_packed.at[0, j], q_packed.at[k, j], qx_send, qx_recv, along_x(k))

    forward(0)

    page_copy.wait()
    length_copy.wait()
    lane = lax.broadcasted_iota(jnp.int32, (8, 128), 1)
    spot = lax.broadcasted_iota(jnp.int32, (64, 128), 0)
    token = lax.rem(lax.broadcasted_iota(jnp.int32, (64, 128), 1), 8) // heads
    last = length[0] - tokens + token - spot

    @pl.loop(0, key_rows // 64)
    def _(i):
        at = pl.ds(pl.multiple_of(i * 64, 64), 64)
        bias[at, :] = jnp.where(pages[0, i] * 64 <= last, 0.0, masked_fill)

    for k in far_z[::-1]:
        done(q_packed.at[0, k], qz_recv.at[k])
        forward(k)

    x_columns = own_columns * NZ
    x_lanes = out_group * NZ
    out_copy.wait()
    place = lax.broadcasted_iota(jnp.int32, (1, x_lanes), 1)
    inside = lax.rem(place, out_group)
    wanted = lax.div(place, out_group) * own_columns + inside
    wanted = jnp.where(inside < own_columns, wanted, -(2**20))
    for i in range(NX):
        low = i * x_columns // 128 * 128
        high = min(-(-(i + 1) * x_columns // 128) * 128, w_out.shape[1])
        column = lax.broadcasted_iota(jnp.int32, (high - low, x_lanes), 0)
        pick = jnp.where(column == wanted + (i * x_columns - low), 1.0, 0.0).astype(BF16)
        w_placed[:, i * x_lanes : (i + 1) * x_lanes] = dot(w_out[:, low:high], pick).astype(BF16)
    done(q_packed.at[0, pl.ds(1, NZ - 1)], qz_send)
    done(q_packed.at[pl.ds(1, NX - 1)], qx_recv)
    for i in range(NX):
        for j in range(0, NZ, 2):
            pair = []
            for part in (q_packed[i, j].astype(F32), q_packed[i, j + 1].astype(F32)):
                pair.append(jnp.concatenate([part[0:8], part[8:16, 0:256]], axis=1))
            first = i * block + j * 8
            q_all[first : first + 16, :] = jnp.concatenate(pair, axis=0).astype(BF16)

    def as_column(row):
        return jnp.broadcast_to(row, (128, rows)).T

    def scaled(value, row):
        return value * jnp.concatenate([as_column(row)] * (value.shape[1] // 128), axis=1)

    def score_tile(c, n):
        at = pl.ds(c * step_keys + n * tile_keys, tile_keys)
        s = dot(keys[at, :], q_all[:, 0:width], 1) * (score_scale * log2_e)
        s = s + jnp.concatenate([bias[at, :]] * (rows // 128), axis=1)
        scores[c % 2, n * tile_keys : (n + 1) * tile_keys, :] = s
        return jnp.max(s.reshape(-1, 8, rows), axis=0)

    tiles = step_keys // tile_keys
    key_copies[0].wait()
    largest = functools.reduce(jnp.maximum, [score_tile(0, n) for n in range(tiles)])
    tops = []
    total = jnp.zeros((8, rows), F32)
    for c in range(steps):
        top = jnp.max(largest, axis=0, keepdims=True)
        if c > 0:
            top = jnp.maximum(top, tops[-1])
            shrink = jnp.exp2(tops[-1] - top)
            total = total * shrink
        tops.append(top)
        if c + 1 < steps:
            key_copies[c + 1].wait()
        found, pieces = [], []
        for n in range(tiles):
            if c + 1 < steps:
                found.append(score_tile(c + 1, n))
            p = jnp.exp2(scores[c % 2, n * tile_keys : (n + 1) * tile_keys, :] - top)
            total = total + jnp.sum(p.reshape(-1, 8, rows), axis=0)
            p = p.astype(BF16).T
            probs[:, c * step_keys + n * tile_keys : c * step_keys + (n + 1) * tile_keys] = p
            pieces.append(p)
        if found:
            largest = functools.reduce(jnp.maximum, found)
        part = dot(jnp.concatenate(pieces, axis=1), keys[pl.ds(c * step_keys, step_keys), 0:half])
        numer[0] = part if c == 0 else scaled(numer[0], shrink) + part

    top_column = as_column(top)
    sum_column = as_column(jnp.sum(total, axis=0, keepdims=True))
    owner = lax.div(lax.broadcasted_iota(jnp.int32, (8, 128), 1), 8)
    for i in range(NX):
        tile = jnp.zeros((8, 128), F32)
        for v in range(NZ):
            first = i * block + v * 8
            tile = jnp.where(owner == v, top_column[first : first + 8], tile)
            tile = jnp.where(owner == v + 8, sum_column[first : first + 8], tile)
        stat_send[i] = tile
    for k in far_x:
        send(stat_send.at[k], stat_recv.at[k], st_send, st_recv, along_x(-k))

    def send_half(h):
        num_send[h] = numer[h].astype(BF16)
        for k in far_x:
            send(
                num_send.at[h, pl.ds(k * block, block)],
                num_recv.at[h, k],
                nx_send.at[h],
                nx_recv.at[h],
                along_x(-k),
            )

    send_half(0)

    for c in range(steps):
        here = pl.ds(c * step_keys, step_keys)
        part = dot(probs[:, here], keys[here, half:latent])
        if c + 1 < steps:
            part = scaled(part, jnp.exp2(tops[c] - top))
        numer[1] = part if c == 0 else numer[1] + part

    send_half(1)
    done(q_packed.at[pl.ds(1, NX - 1)], qx_send)

    done(stat_recv.at[pl.ds(1, NX - 1)], st_recv)
    found = [stat_send[0]] + [stat_recv[k] for k in range(1, NX)]
    factors = [[] for _ in found]
    z_stats = []
    for v in range(NZ):
        tops = [jnp.broadcast_to(f[:, 8 * v : 8 * v + 1], (8, 128)) for f in found]
        top_x = functools.reduce(jnp.maximum, tops)
        coarse = top_x.astype(BF16).astype(F32)
        top_x = coarse + (top_x - coarse).astype(BF16).astype(F32)
        total_x = jnp.zeros((8, 128), F32)
        for f, t, held in zip(found, tops, factors):
            held.append(jnp.exp2(t - top_x))
            total_x = total_x + f[:, 64 + 8 * v : 64 + 8 * v + 1] * held[v]
        z_stats.append(jnp.where(lane < 64, top_x, total_x))
        if v > 0:
            coarse = z_stats[v].astype(BF16).astype(F32)
            low_send[v, :, 128:256] = jnp.concatenate(
                [coarse, z_stats[v] - coarse], axis=0
            ).astype(BF16)
    factors = [
        jnp.concatenate([jnp.concatenate(held, axis=0)] * (half // 128), axis=1) for held in factors
    ]

    spans = ((0, 256), (256, 384))
    own_half = []
    for h in range(2):
        done(num_recv.at[h, pl.ds(1, NX - 1)], nx_recv.at[h])
        merged = numer[h, 0:block, :] * factors[0]
        for k in range(1, NX):
            merged = merged + num_recv[h, k].astype(F32) * factors[k]
        own_half.append([merged[0:8, j : j + 128] for j in range(0, half, 128)])
        low, high = spans[h]
        for k in far_z:
            part = merged[k * 8 : (k + 1) * 8]
            low_send[k, :, low : low + 128] = jnp.concatenate(
                [part[:, 0:128], part[:, 128:256]], axis=0
            ).astype(BF16)
            send(
                low_send.at[k, :, low:high],
                low_recv.at[k, :, low:high],
                nz_send.at[h],
                nz_recv.at[h],
                along_z(-k),
            )
    done(stat_recv.at[pl.ds(1, NX - 1)], st_send)
    for h in range(2):
        done(num_recv.at[h, pl.ds(1, NX - 1)], nx_send.at[h])

    done(low_recv.at[pl.ds(1, NZ - 1), :, 0:256], nz_recv.at[0])
    found = [z_stats[0]]
    for k in range(1, NZ):
        held = low_recv[k, :, 128:256].astype(F32)
        found.append(held[0:8] + held[8:16])
    tops = [jnp.broadcast_to(f[:, 0:1], (8, 128)) for f in found]
    top_z = functools.reduce(jnp.maximum, tops)
    factors = [jnp.exp2(t - top_z) for t in tops]
    total_z = sum(f[:, 64:65] * w for f, w in zip(found, factors))
    attended = []
    for h in range(2):
        if h == 1:
            done(low_recv.at[pl.ds(1, NZ - 1), :, 256:384], nz_recv.at[1])
        merged = [own * factors[0] for own in own_half[h]]
        for k in range(1, NZ):
            held = low_recv[k, :, spans[h][0] : spans[h][0] + 128].astype(F32)
            for j in range(2):
                merged[j] = merged[j] + held[j * 8 : (j + 1) * 8] * factors[k]
        attended += [m / total_z for m in merged]
    attended = jnp.concatenate(attended, axis=1)
    head = lax.rem(lax.broadcasted_iota(jnp.int32, attended.shape, 0), heads)
    spread = [jnp.where(head == i, attended, 0.0) for i in range(heads)]
    up_copy.wait()
    values = dot(
        jnp.concatenate(spread, axis=1).astype(BF16), w_up[...].reshape(heads * latent, -1)
    )

    own = pl.ds(pl.multiple_of(g * 8, 8), 8)
    head_values[own, :] = values.astype(BF16).astype(F32)
    for k in range(1, NG):
        send(head_values.at[own], head_values.at[own], v_send, v_recv, along_g(k))
    others = head_values.at[pl.ds(0, (NG - 1) * 8)]
    done(low_recv.at[pl.ds(1, NZ - 1), :, 0:256], nz_send.at[0])
    done(low_recv.at[pl.ds(1, NZ - 1), :, 256:384], nz_send.at[1])
    done(others, v_recv)
    wide = [head_values[pl.ds(i, tokens * NG, stride=heads), :] for i in range(heads)]
    terms = dot(jnp.concatenate(wide, axis=1).astype(BF16), w_placed[...])

    for i in range(NX):
        term_send[i] = terms[:, i * x_lanes : (i + 1) * x_lanes].astype(BF16)
    for k in far_x:
        send(term_send.at[lax.rem(x + k, NX)], term_recv.at[k], tx_send, tx_recv, along_x(k))
    done(others, v_send)
    summed = term_send[x].astype(F32)
    done(term_recv.at[pl.ds(1, NX - 1)], tx_recv)
    for k in range(1, NX):
        summed = summed + term_recv[k].astype(F32)
    for i in range(x_lanes // 128):
        last_send[i] = summed[:, i * 128 : (i + 1) * 128].astype(BF16)
    per_tile = 128 // out_group
    for k in far_z:
        send(
            last_send.at[lax.div(lax.rem(z + k, NZ), per_tile)],
            last_recv.at[k],
            tz_send,
            tz_recv,
            along_z(k),
        )
    done(term_recv.at[pl.ds(1, NX - 1)], tx_send)
    final = last_send[lax.div(z, per_tile)].astype(F32)
    done(last_recv.at[pl.ds(1, NZ - 1)], tz_recv)
    for k in range(1, NZ):
        final = final + last_recv[k].astype(F32)
    place = lax.rem(z, per_tile)
    chosen = final
    for i in range(1, per_tile):
        chosen = jnp.where(place == i, pltpu.roll(final, 128 - i * out_group, 1), chosen)
    result[...] = chosen
    done(last_recv.at[pl.ds(1, NZ - 1)], tz_send)


def body(sizes, queries, cache, slot_page, lengths, w_uv, w_out):
    NX, NZ, NG, own_columns = sizes
    tokens, heads, width = queries.shape[1:]
    latent = w_uv.shape[1]
    half = latent // 2
    key_rows = cache.shape[1] * cache.shape[2]
    rows = NX * NZ * 8
    block = NZ * 8
    x_lanes = NZ * out_group
    sem = pltpu.SemaphoreType.DMA
    scratch = [
        pltpu.VMEM(queries.shape, BF16),
        pltpu.VMEM((8, 768), F32),
        pltpu.VMEM((NX, NZ, 16, 384), BF16),
        pltpu.VMEM((rows, 640), BF16),
        pltpu.VMEM((key_rows, width), BF16),
        pltpu.SMEM(slot_page.shape, jnp.int32),
        pltpu.SMEM(lengths.shape, jnp.int32),
        pltpu.VMEM(w_uv.shape, BF16),
        pltpu.VMEM(w_out.shape, BF16),
        pltpu.VMEM((w_out.shape[0], NX * x_lanes), BF16),
        pltpu.VMEM((key_rows, 128), F32),
        pltpu.VMEM((2, step_keys, rows), F32),
        pltpu.VMEM((rows, key_rows), BF16),
        pltpu.VMEM((2, rows, half), F32),
        pltpu.VMEM((2, rows, half), BF16),
        pltpu.VMEM((2, NX, block, half), BF16),
        pltpu.VMEM((NX, 8, 128), F32),
        pltpu.VMEM((NX, 8, 128), F32),
        pltpu.VMEM((NZ, 16, 384), BF16),
        pltpu.VMEM((NZ, 16, 384), BF16),
        pltpu.VMEM((NG * 8, 128), F32),
        pltpu.VMEM((NX, tokens * NG, x_lanes), BF16),
        pltpu.VMEM((NX, tokens * NG, x_lanes), BF16),
        pltpu.VMEM((x_lanes // 128, tokens * NG, 128), BF16),
        pltpu.VMEM((NZ, tokens * NG, 128), BF16),
        sem((5,)),
        sem((key_rows // step_keys,)),
        sem,
        sem((NZ,)),
        sem,
        sem,
        sem,
        sem,
        sem((2,)),
        sem((2,)),
        sem((2,)),
        sem((2,)),
        sem,
        sem,
        sem,
        sem,
        sem,
        sem,
    ]
    result = pl.pallas_call(
        functools.partial(kernel, sizes),
        out_shape=jax.ShapeDtypeStruct((tokens * NG, 128), F32),
        in_specs=[pl.BlockSpec(memory_space=pltpu.HBM)] * 6,
        out_specs=pl.BlockSpec(memory_space=pltpu.VMEM),
        scratch_shapes=scratch,
        compiler_params=pltpu.CompilerParams(
            collective_id=0, has_side_effects=True, vmem_limit_bytes=56 * 1024 * 1024
        ),
    )(queries, cache.reshape(key_rows, width), slot_page, lengths, w_uv, w_out)
    return result[:, 0:own_columns].astype(BF16).reshape(NG, tokens, own_columns)


def solution(mesh, NX=4):
    NG, pages = mesh.shape["group"], mesh.shape["page"]
    in_specs = (
        P("group", None, "page", None),
        P("group", "page", None, None),
        P("group", "page"),
        P("group"),
        P("page", None, None),
        P("page", "group"),
    )
    out_specs = P(None, None, ("group", "page"))

    def step(queries, cache, slot_page, lengths, w_uv, w_out):
        sizes = (NX, pages // NX, NG, w_out.shape[1] // pages)
        return body(sizes, queries, cache, slot_page, lengths, w_uv, w_out)

    return jax.shard_map(step, mesh=mesh, in_specs=in_specs, out_specs=out_specs, check_vma=False)
```

```python
import functools

import jax
import jax.numpy as jnp
from jax import lax
from jax.experimental import pallas as pl
from jax.experimental.pallas import tpu as pltpu
from jax.sharding import PartitionSpec as P

MESH = pl.DeviceIdType.MESH
F32 = jnp.float32
BF16 = jnp.bfloat16
score_scale = 192.0 ** (-0.5)
log2_e = 1.4426950408889634
masked_fill = -(2.0**99)
lowest_top = -(2.0**20)
out_group = 32
step_keys = 1024
tile_keys = 512


def dot(a, b, contract_b=0):
    return lax.dot_general(a, b, (((1,), (contract_b,)), ((), ())), preferred_element_type=F32)


def kernel(
    sizes,
    q_hbm,
    k_hbm,
    page_hbm,
    length_hbm,
    up_hbm,
    out_hbm,
    result,
    q_in,
    q_rows,
    q_packed,
    q_all,
    keys,
    pages,
    length,
    w_up,
    w_out,
    w_placed,
    tails,
    scores,
    probs,
    numer,
    num_send,
    num_recv,
    stat_send,
    stat_recv,
    low_send,
    low_recv,
    head_values,
    term_send,
    term_recv,
    last_send,
    last_recv,
    local_sem,
    key_sem,
    qz_send,
    qz_recv,
    qx_send,
    qx_recv,
    st_send,
    st_recv,
    nx_send,
    nx_recv,
    nz_send,
    nz_recv,
    v_send,
    v_recv,
    tx_send,
    tx_recv,
    tz_send,
    tz_recv,
):
    NX, NZ, NG, own_columns = sizes
    width = q_in.shape[-1]
    latent = w_up.shape[1]
    half = latent // 2
    key_rows = keys.shape[0]
    rows = q_all.shape[0]
    block = rows // NX
    steps = key_rows // step_keys
    tokens, heads = q_in.shape[1], q_in.shape[2]

    g = lax.axis_index("group")
    page = lax.axis_index("page")
    x, z = lax.div(page, NZ), lax.rem(page, NZ)

    def along_x(k):
        return {"page": lax.rem(x + k + NX, NX) * NZ + z}

    def along_z(k):
        return {"page": x * NZ + lax.rem(z + k + NZ, NZ)}

    def along_g(k):
        return {"group": lax.rem(g + k + NG, NG)}

    def send(source, target, send_sem, recv_sem, device):
        copy = pltpu.make_async_remote_copy(
            src_ref=source,
            dst_ref=target,
            send_sem=send_sem,
            recv_sem=recv_sem,
            device_id=device,
            device_id_type=MESH,
        )
        copy.start()
        return copy

    def done(region, sem):
        pltpu.make_async_copy(region, region, sem).wait()

    far_z = sorted(range(1, NZ), key=lambda k: -min(k, NZ - k))
    far_x = sorted(range(1, NX), key=lambda k: -min(k, NX - k))

    barrier = pltpu.get_barrier_semaphore()
    for k in range(1, NX):
        pl.semaphore_signal(barrier, inc=1, device_id=along_x(k), device_id_type=MESH)
    for k in range(1, NZ):
        pl.semaphore_signal(barrier, inc=1, device_id=along_z(k), device_id_type=MESH)
    for k in range(1, NG):
        pl.semaphore_signal(barrier, inc=1, device_id=along_g(k), device_id_type=MESH)

    def local(source, target, sem):
        copy = pltpu.make_async_copy(source, target, sem)
        copy.start()
        return copy

    q_copy = local(q_hbm, q_in, local_sem.at[0])
    page_copy = local(page_hbm, pages, local_sem.at[1])
    length_copy = local(length_hbm, length, local_sem.at[2])
    out_copy = local(out_hbm, w_out, local_sem.at[3])
    key_copies = [
        local(
            k_hbm.at[pl.ds(c * step_keys, step_keys)],
            keys.at[pl.ds(c * step_keys, step_keys)],
            key_sem.at[c],
        )
        for c in range(steps)
    ]
    up_copy = local(up_hbm, w_up, local_sem.at[4])

    q_copy.wait()
    place = lax.broadcasted_iota(jnp.int32, (8, 256), 1) + 512
    owner = lax.broadcasted_iota(jnp.int32, (8, 256), 0) // heads
    q_rows[:, 512:768] = jnp.where(place == width + owner, 1.0, 0.0)
    for t in range(tokens):
        q_rows[t * heads : (t + 1) * heads, 0:width] = q_in[0, t].astype(F32)
    q_packed[0, 0] = jnp.concatenate([q_rows[:, 0:384], q_rows[:, 384:768]], axis=0).astype(BF16)
    pl.semaphore_wait(barrier, NX + NZ + NG - 3)
    for k in far_z:
        send(q_packed.at[0, 0], q_packed.at[0, k], qz_send, qz_recv.at[k], along_z(k))

    def forward(j):
        for k in far_x:
            send(q_packed.at[0, j], q_packed.at[k, j], qx_send, qx_recv, along_x(k))

    forward(0)

    page_copy.wait()
    length_copy.wait()
    lane = lax.broadcasted_iota(jnp.int32, (8, 128), 1)
    spot = lax.broadcasted_iota(jnp.int32, (64, 64), 0)
    token = lax.broadcasted_iota(jnp.int32, (64, 64), 1)
    last = jnp.where(token < tokens, length[0] - tokens + token - spot, 2**30)

    for k in far_z[::-1]:
        done(q_packed.at[0, k], qz_recv.at[k])
        forward(k)

    x_columns = own_columns * NZ
    x_lanes = out_group * NZ
    out_copy.wait()
    place = lax.broadcasted_iota(jnp.int32, (1, x_lanes), 1)
    inside = lax.rem(place, out_group)
    wanted = lax.div(place, out_group) * own_columns + inside
    wanted = jnp.where(inside < own_columns, wanted, -(2**20))
    for i in range(NX):
        low = i * x_columns // 128 * 128
        high = min(-(-(i + 1) * x_columns // 128) * 128, w_out.shape[1])
        column = lax.broadcasted_iota(jnp.int32, (high - low, x_lanes), 0)
        pick = jnp.where(column == wanted + (i * x_columns - low), 1.0, 0.0).astype(BF16)
        w_placed[:, i * x_lanes : (i + 1) * x_lanes] = dot(w_out[:, low:high], pick).astype(BF16)
    done(q_packed.at[0, pl.ds(1, NZ - 1)], qz_send)
    for c, copy in enumerate(key_copies):
        copy.wait()

        @pl.loop(c * step_keys // 64, (c + 1) * step_keys // 64)
        def _(i):
            at = pl.ds(pl.multiple_of(i * 64, 64), 64)
            mask = jnp.where(pages[0, i] * 64 <= last, 0.0, masked_fill).astype(BF16)
            tails[at, :] = jnp.concatenate([keys[at, latent:width], mask], axis=1)

    done(q_packed.at[pl.ds(1, NX - 1)], qx_recv)
    for i in range(NX):
        for j in range(0, NZ, 2):
            pair = []
            for part in (q_packed[i, j].astype(F32), q_packed[i, j + 1].astype(F32)):
                pair.append(jnp.concatenate([part[0:8], part[8:16, 0:256]], axis=1))
            first = i * block + j * 8
            q_all[first : first + 16, :] = jnp.concatenate(pair, axis=0).astype(BF16)

    def as_column(row):
        return jnp.broadcast_to(row, (128, rows)).T

    def scaled(value, row):
        return value * jnp.concatenate([as_column(row)] * (value.shape[1] // 128), axis=1)

    def score_tile(c, n):
        at = pl.ds(c * step_keys + n * tile_keys, tile_keys)
        wide = jnp.concatenate([keys[at, 0:latent], tails[at, :]], axis=1)
        s = dot(wide, q_all[...], 1) * (score_scale * log2_e)
        scores[c % 2, n * tile_keys : (n + 1) * tile_keys, :] = s
        return jnp.max(s.reshape(-1, 8, rows), axis=0)

    tiles = step_keys // tile_keys
    largest = functools.reduce(jnp.maximum, [score_tile(0, n) for n in range(tiles)])
    tops = [jnp.full((1, rows), lowest_top, F32)]
    total = jnp.zeros((8, rows), F32)
    for c in range(steps):
        top = jnp.maximum(jnp.max(largest, axis=0, keepdims=True), tops[-1])
        shrink = jnp.exp2(tops[-1] - top)
        total = total * shrink
        tops.append(top)
        found, pieces = [], []
        for n in range(tiles):
            if c + 1 < steps:
                found.append(score_tile(c + 1, n))
            for low in range(n * tile_keys, (n + 1) * tile_keys, 256):
                p = jnp.exp2(scores[c % 2, low : low + 256, :] - top)
                total = total + jnp.sum(p.reshape(-1, 8, rows), axis=0)
                p = p.astype(BF16).T
                probs[:, c * step_keys + low : c * step_keys + low + 256] = p
                pieces.append(p)
        if found:
            largest = functools.reduce(jnp.maximum, found)
        part = dot(jnp.concatenate(pieces, axis=1), keys[pl.ds(c * step_keys, step_keys), 0:half])
        numer[0] = part if c == 0 else scaled(numer[0], shrink) + part

    top_column = as_column(top)
    sum_column = as_column(jnp.sum(total, axis=0, keepdims=True))
    owner = lax.div(lax.broadcasted_iota(jnp.int32, (8, 128), 1), 8)
    for i in range(NX):
        tile = jnp.zeros((8, 128), F32)
        for v in range(NZ):
            first = i * block + v * 8
            tile = jnp.where(owner == v, top_column[first : first + 8], tile)
            tile = jnp.where(owner == v + 8, sum_column[first : first + 8], tile)
        stat_send[i] = tile
    for k in far_x:
        send(stat_send.at[k], stat_recv.at[k], st_send, st_recv, along_x(-k))

    def send_half(h):
        num_send[h] = numer[h].astype(BF16)
        for k in far_x:
            send(
                num_send.at[h, pl.ds(k * block, block)],
                num_recv.at[h, k],
                nx_send.at[h],
                nx_recv.at[h],
                along_x(-k),
            )

    send_half(0)

    for c in range(steps):
        here = pl.ds(c * step_keys, step_keys)
        part = dot(probs[:, here], keys[here, half:latent])
        if c + 1 < steps:
            part = scaled(part, jnp.exp2(tops[c + 1] - top))
        numer[1] = part if c == 0 else numer[1] + part

    send_half(1)
    done(q_packed.at[pl.ds(1, NX - 1)], qx_send)

    done(stat_recv.at[pl.ds(1, NX - 1)], st_recv)
    found = [stat_send[0]] + [stat_recv[k] for k in range(1, NX)]
    factors = [[] for _ in found]
    z_stats = []
    for v in range(NZ):
        tops = [jnp.broadcast_to(f[:, 8 * v : 8 * v + 1], (8, 128)) for f in found]
        top_x = functools.reduce(jnp.maximum, tops)
        coarse = top_x.astype(BF16).astype(F32)
        top_x = coarse + (top_x - coarse).astype(BF16).astype(F32)
        total_x = jnp.zeros((8, 128), F32)
        for f, t, held in zip(found, tops, factors):
            held.append(jnp.exp2(t - top_x))
            total_x = total_x + f[:, 64 + 8 * v : 64 + 8 * v + 1] * held[v]
        z_stats.append(jnp.where(lane < 64, top_x, total_x))
        if v > 0:
            coarse = z_stats[v].astype(BF16).astype(F32)
            low_send[v, :, 128:256] = jnp.concatenate(
                [coarse, z_stats[v] - coarse], axis=0
            ).astype(BF16)
    factors = [
        jnp.concatenate([jnp.concatenate(held, axis=0)] * (half // 128), axis=1) for held in factors
    ]

    spans = ((0, 256), (256, 384))
    own_half = []
    for h in range(2):
        done(num_recv.at[h, pl.ds(1, NX - 1)], nx_recv.at[h])
        merged = numer[h, 0:block, :] * factors[0]
        for k in range(1, NX):
            merged = merged + num_recv[h, k].astype(F32) * factors[k]
        own_half.append([merged[0:8, j : j + 128] for j in range(0, half, 128)])
        low, high = spans[h]
        for k in far_z:
            part = merged[k * 8 : (k + 1) * 8]
            low_send[k, :, low : low + 128] = jnp.concatenate(
                [part[:, 0:128], part[:, 128:256]], axis=0
            ).astype(BF16)
            send(
                low_send.at[k, :, low:high],
                low_recv.at[k, :, low:high],
                nz_send.at[h],
                nz_recv.at[h],
                along_z(-k),
            )
    done(stat_recv.at[pl.ds(1, NX - 1)], st_send)
    for h in range(2):
        done(num_recv.at[h, pl.ds(1, NX - 1)], nx_send.at[h])

    done(low_recv.at[pl.ds(1, NZ - 1), :, 0:256], nz_recv.at[0])
    found = [z_stats[0]]
    for k in range(1, NZ):
        held = low_recv[k, :, 128:256].astype(F32)
        found.append(held[0:8] + held[8:16])
    tops = [jnp.broadcast_to(f[:, 0:1], (8, 128)) for f in found]
    top_z = functools.reduce(jnp.maximum, tops)
    factors = [jnp.exp2(t - top_z) for t in tops]
    total_z = sum(f[:, 64:65] * w for f, w in zip(found, factors))
    attended = []
    for h in range(2):
        if h == 1:
            done(low_recv.at[pl.ds(1, NZ - 1), :, 256:384], nz_recv.at[1])
        merged = [own * factors[0] for own in own_half[h]]
        for k in range(1, NZ):
            held = low_recv[k, :, spans[h][0] : spans[h][0] + 128].astype(F32)
            for j in range(2):
                merged[j] = merged[j] + held[j * 8 : (j + 1) * 8] * factors[k]
        attended += [m / total_z for m in merged]
    attended = jnp.concatenate(attended, axis=1)
    head = lax.rem(lax.broadcasted_iota(jnp.int32, attended.shape, 0), heads)
    spread = [jnp.where(head == i, attended, 0.0) for i in range(heads)]
    up_copy.wait()
    values = dot(
        jnp.concatenate(spread, axis=1).astype(BF16), w_up[...].reshape(heads * latent, -1)
    )

    own = pl.ds(pl.multiple_of(g * 8, 8), 8)
    head_values[own, :] = values.astype(BF16).astype(F32)
    for k in range(1, NG):
        send(head_values.at[own], head_values.at[own], v_send, v_recv, along_g(k))
    others = head_values.at[pl.ds(0, (NG - 1) * 8)]
    done(low_recv.at[pl.ds(1, NZ - 1), :, 0:256], nz_send.at[0])
    done(low_recv.at[pl.ds(1, NZ - 1), :, 256:384], nz_send.at[1])
    done(others, v_recv)
    wide = [head_values[pl.ds(i, tokens * NG, stride=heads), :] for i in range(heads)]
    terms = dot(jnp.concatenate(wide, axis=1).astype(BF16), w_placed[...])

    for i in range(NX):
        term_send[i] = terms[:, i * x_lanes : (i + 1) * x_lanes].astype(BF16)
    for k in far_x:
        send(term_send.at[lax.rem(x + k, NX)], term_recv.at[k], tx_send, tx_recv, along_x(k))
    done(others, v_send)
    summed = term_send[x].astype(F32)
    done(term_recv.at[pl.ds(1, NX - 1)], tx_recv)
    for k in range(1, NX):
        summed = summed + term_recv[k].astype(F32)
    for i in range(x_lanes // 128):
        last_send[i] = summed[:, i * 128 : (i + 1) * 128].astype(BF16)
    per_tile = 128 // out_group
    for k in far_z:
        send(
            last_send.at[lax.div(lax.rem(z + k, NZ), per_tile)],
            last_recv.at[k],
            tz_send,
            tz_recv,
            along_z(k),
        )
    done(term_recv.at[pl.ds(1, NX - 1)], tx_send)
    final = last_send[lax.div(z, per_tile)].astype(F32)
    done(last_recv.at[pl.ds(1, NZ - 1)], tz_recv)
    for k in range(1, NZ):
        final = final + last_recv[k].astype(F32)
    place = lax.rem(z, per_tile)
    chosen = final
    for i in range(1, per_tile):
        chosen = jnp.where(place == i, pltpu.roll(final, 128 - i * out_group, 1), chosen)
    result[...] = chosen
    done(last_recv.at[pl.ds(1, NZ - 1)], tz_send)


def body(sizes, queries, cache, slot_page, lengths, w_uv, w_out):
    NX, NZ, NG, own_columns = sizes
    tokens, heads, width = queries.shape[1:]
    latent = w_uv.shape[1]
    half = latent // 2
    key_rows = cache.shape[1] * cache.shape[2]
    rows = NX * NZ * 8
    block = NZ * 8
    x_lanes = NZ * out_group
    sem = pltpu.SemaphoreType.DMA
    scratch = [
        pltpu.VMEM(queries.shape, BF16),
        pltpu.VMEM((8, 768), F32),
        pltpu.VMEM((NX, NZ, 16, 384), BF16),
        pltpu.VMEM((rows, 640), BF16),
        pltpu.VMEM((key_rows, width), BF16),
        pltpu.SMEM(slot_page.shape, jnp.int32),
        pltpu.SMEM(lengths.shape, jnp.int32),
        pltpu.VMEM(w_uv.shape, BF16),
        pltpu.VMEM(w_out.shape, BF16),
        pltpu.VMEM((w_out.shape[0], NX * x_lanes), BF16),
        pltpu.VMEM((key_rows, 128), BF16),
        pltpu.VMEM((2, step_keys, rows), F32),
        pltpu.VMEM((rows, key_rows), BF16),
        pltpu.VMEM((2, rows, half), F32),
        pltpu.VMEM((2, rows, half), BF16),
        pltpu.VMEM((2, NX, block, half), BF16),
        pltpu.VMEM((NX, 8, 128), F32),
        pltpu.VMEM((NX, 8, 128), F32),
        pltpu.VMEM((NZ, 16, 384), BF16),
        pltpu.VMEM((NZ, 16, 384), BF16),
        pltpu.VMEM((NG * 8, 128), F32),
        pltpu.VMEM((NX, tokens * NG, x_lanes), BF16),
        pltpu.VMEM((NX, tokens * NG, x_lanes), BF16),
        pltpu.VMEM((x_lanes // 128, tokens * NG, 128), BF16),
        pltpu.VMEM((NZ, tokens * NG, 128), BF16),
        sem((5,)),
        sem((key_rows // step_keys,)),
        sem,
        sem((NZ,)),
        sem,
        sem,
        sem,
        sem,
        sem((2,)),
        sem((2,)),
        sem((2,)),
        sem((2,)),
        sem,
        sem,
        sem,
        sem,
        sem,
        sem,
    ]
    result = pl.pallas_call(
        functools.partial(kernel, sizes),
        out_shape=jax.ShapeDtypeStruct((tokens * NG, 128), F32),
        in_specs=[pl.BlockSpec(memory_space=pltpu.HBM)] * 6,
        out_specs=pl.BlockSpec(memory_space=pltpu.VMEM),
        scratch_shapes=scratch,
        compiler_params=pltpu.CompilerParams(
            collective_id=0, has_side_effects=True, vmem_limit_bytes=56 * 1024 * 1024
        ),
    )(queries, cache.reshape(key_rows, width), slot_page, lengths, w_uv, w_out)
    return result[:, 0:own_columns].astype(BF16).reshape(NG, tokens, own_columns)


def solution(mesh, NX=4):
    NG, pages = mesh.shape["group"], mesh.shape["page"]
    in_specs = (
        P("group", None, "page", None),
        P("group", "page", None, None),
        P("group", "page"),
        P("group"),
        P("page", None, None),
        P("page", "group"),
    )
    out_specs = P(None, None, ("group", "page"))

    def step(queries, cache, slot_page, lengths, w_uv, w_out):
        sizes = (NX, pages // NX, NG, w_out.shape[1] // pages)
        return body(sizes, queries, cache, slot_page, lengths, w_uv, w_out)

    return jax.shard_map(step, mesh=mesh, in_specs=in_specs, out_specs=out_specs, check_vma=False)
```

```python
import functools

import jax
import jax.numpy as jnp
from jax import lax
from jax.experimental import pallas as pl
from jax.experimental.pallas import tpu as pltpu
from jax.sharding import PartitionSpec as P

MESH = pl.DeviceIdType.MESH
F32 = jnp.float32
BF16 = jnp.bfloat16
score_scale = 192.0 ** (-0.5)
log2_e = 1.4426950408889634
masked_fill = -(2.0**99)
lowest_top = -(2.0**20)
out_group = 32
step_keys = 1024
tile_keys = 512


def dot(a, b, contract_b=0):
    return lax.dot_general(a, b, (((1,), (contract_b,)), ((), ())), preferred_element_type=F32)


def kernel(
    sizes,
    q_hbm,
    k_hbm,
    page_hbm,
    length_hbm,
    up_hbm,
    out_hbm,
    result,
    q_in,
    q_rows,
    q_packed,
    q_all,
    keys,
    pages,
    length,
    w_up,
    w_out,
    w_placed,
    tails,
    scores,
    probs,
    numer,
    num_send,
    num_recv,
    stat_send,
    stat_recv,
    low_send,
    low_recv,
    head_values,
    term_send,
    term_recv,
    last_send,
    last_recv,
    local_sem,
    key_sem,
    qz_send,
    qz_recv,
    qx_send,
    qx_recv,
    st_send,
    st_recv,
    nx_send,
    nx_recv,
    nz_send,
    nz_recv,
    v_send,
    v_recv,
    tx_send,
    tx_recv,
    tz_send,
    tz_recv,
):
    NX, NZ, NG, own_columns = sizes
    width = q_in.shape[-1]
    latent = w_up.shape[1]
    half = latent // 2
    key_rows = keys.shape[0]
    rows = q_all.shape[0]
    block = rows // NX
    steps = key_rows // step_keys
    tokens, heads = q_in.shape[1], q_in.shape[2]

    g = lax.axis_index("group")
    page = lax.axis_index("page")
    x, z = lax.div(page, NZ), lax.rem(page, NZ)

    def along_x(k):
        return {"page": lax.rem(x + k + NX, NX) * NZ + z}

    def along_z(k):
        return {"page": x * NZ + lax.rem(z + k + NZ, NZ)}

    def along_g(k):
        return {"group": lax.rem(g + k + NG, NG)}

    def send(source, target, send_sem, recv_sem, device):
        copy = pltpu.make_async_remote_copy(
            src_ref=source,
            dst_ref=target,
            send_sem=send_sem,
            recv_sem=recv_sem,
            device_id=device,
            device_id_type=MESH,
        )
        copy.start()
        return copy

    def done(region, sem):
        pltpu.make_async_copy(region, region, sem).wait()

    far_z = sorted(range(1, NZ), key=lambda k: -min(k, NZ - k))
    far_x = sorted(range(1, NX), key=lambda k: -min(k, NX - k))

    barrier = pltpu.get_barrier_semaphore()
    for k in range(1, NX):
        pl.semaphore_signal(barrier, inc=1, device_id=along_x(k), device_id_type=MESH)
    for k in range(1, NZ):
        pl.semaphore_signal(barrier, inc=1, device_id=along_z(k), device_id_type=MESH)
    for k in range(1, NG):
        pl.semaphore_signal(barrier, inc=1, device_id=along_g(k), device_id_type=MESH)

    def local(source, target, sem):
        copy = pltpu.make_async_copy(source, target, sem)
        copy.start()
        return copy

    q_copy = local(q_hbm, q_in, local_sem.at[0])
    page_copy = local(page_hbm, pages, local_sem.at[1])
    length_copy = local(length_hbm, length, local_sem.at[2])
    out_copy = local(out_hbm, w_out, local_sem.at[3])
    key_copies = [
        local(
            k_hbm.at[pl.ds(c * step_keys, step_keys)],
            keys.at[pl.ds(c * step_keys, step_keys)],
            key_sem.at[c],
        )
        for c in range(steps)
    ]
    up_copy = local(up_hbm, w_up, local_sem.at[4])

    q_copy.wait()
    place = lax.broadcasted_iota(jnp.int32, (8, 256), 1) + 512
    owner = lax.broadcasted_iota(jnp.int32, (8, 256), 0) // heads
    q_rows[:, 512:768] = jnp.where(place == width + owner, 1.0, 0.0)
    for t in range(tokens):
        q_rows[t * heads : (t + 1) * heads, 0:width] = q_in[0, t].astype(F32)
    q_packed[0, 0] = jnp.concatenate([q_rows[:, 0:384], q_rows[:, 384:768]], axis=0).astype(BF16)
    pl.semaphore_wait(barrier, NX + NZ + NG - 3)
    for k in far_z:
        send(q_packed.at[0, 0], q_packed.at[0, k], qz_send, qz_recv.at[k], along_z(k))

    def forward(j):
        for k in far_x:
            send(q_packed.at[0, j], q_packed.at[k, j], qx_send, qx_recv, along_x(k))

    forward(0)

    page_copy.wait()
    length_copy.wait()
    lane = lax.broadcasted_iota(jnp.int32, (8, 128), 1)
    spot = lax.broadcasted_iota(jnp.int32, (64, 64), 0)
    token = lax.broadcasted_iota(jnp.int32, (64, 64), 1)
    last = jnp.where(token < tokens, length[0] - tokens + token - spot, 2**30)

    x_columns = own_columns * NZ
    x_lanes = out_group * NZ
    out_copy.wait()
    place = lax.broadcasted_iota(jnp.int32, (1, x_lanes), 1)
    inside = lax.rem(place, out_group)
    wanted = lax.div(place, out_group) * own_columns + inside
    wanted = jnp.where(inside < own_columns, wanted, -(2**20))
    for i in range(NX):
        low = i * x_columns // 128 * 128
        high = min(-(-(i + 1) * x_columns // 128) * 128, w_out.shape[1])
        column = lax.broadcasted_iota(jnp.int32, (high - low, x_lanes), 0)
        pick = jnp.where(column == wanted + (i * x_columns - low), 1.0, 0.0).astype(BF16)
        w_placed[:, i * x_lanes : (i + 1) * x_lanes] = dot(w_out[:, low:high], pick).astype(BF16)

    for k in far_z[::-1]:
        done(q_packed.at[0, k], qz_recv.at[k])
        forward(k)

    done(q_packed.at[0, pl.ds(1, NZ - 1)], qz_send)
    for c, copy in enumerate(key_copies):
        copy.wait()

        @pl.loop(c * step_keys // 64, (c + 1) * step_keys // 64, unroll=8)
        def _(i):
            at = pl.ds(pl.multiple_of(i * 64, 64), 64)
            mask = jnp.where(pages[0, i] * 64 <= last, 0.0, masked_fill).astype(BF16)
            tails[at, :] = jnp.concatenate([keys[at, latent:width], mask], axis=1)

    done(q_packed.at[pl.ds(1, NX - 1)], qx_recv)
    for i in range(NX):
        for j in range(0, NZ, 2):
            pair = []
            for part in (q_packed[i, j].astype(F32), q_packed[i, j + 1].astype(F32)):
                pair.append(jnp.concatenate([part[0:8], part[8:16, 0:256]], axis=1))
            first = i * block + j * 8
            q_all[first : first + 16, :] = jnp.concatenate(pair, axis=0).astype(BF16)

    def as_column(row):
        return jnp.broadcast_to(row, (128, rows)).T

    def scaled(value, row):
        return value * jnp.concatenate([as_column(row)] * (value.shape[1] // 128), axis=1)

    def score_tile(c, n):
        at = pl.ds(c * step_keys + n * tile_keys, tile_keys)
        wide = jnp.concatenate([keys[at, 0:latent], tails[at, :]], axis=1)
        s = dot(wide, q_all[...], 1) * (score_scale * log2_e)
        scores[c % 2, n * tile_keys : (n + 1) * tile_keys, :] = s
        return jnp.max(s.reshape(-1, 8, rows), axis=0)

    tiles = step_keys // tile_keys
    largest = functools.reduce(jnp.maximum, [score_tile(0, n) for n in range(tiles)])
    tops = [jnp.full((1, rows), lowest_top, F32)]
    total = jnp.zeros((8, rows), F32)
    for c in range(steps):
        top = jnp.maximum(jnp.max(largest, axis=0, keepdims=True), tops[-1])
        shrink = jnp.exp2(tops[-1] - top)
        total = total * shrink
        tops.append(top)
        found, pieces = [], []
        for n in range(tiles):
            if c + 1 < steps:
                found.append(score_tile(c + 1, n))
            for low in range(n * tile_keys, (n + 1) * tile_keys, 256):
                p = jnp.exp2(scores[c % 2, low : low + 256, :] - top)
                total = total + jnp.sum(p.reshape(-1, 8, rows), axis=0)
                p = p.astype(BF16).T
                probs[:, c * step_keys + low : c * step_keys + low + 256] = p
                pieces.append(p)
        if found:
            largest = functools.reduce(jnp.maximum, found)
        part = dot(jnp.concatenate(pieces, axis=1), keys[pl.ds(c * step_keys, step_keys), 0:half])
        numer[0] = part if c == 0 else scaled(numer[0], shrink) + part

    top_column = as_column(top)
    sum_column = as_column(jnp.sum(total, axis=0, keepdims=True))
    owner = lax.div(lax.broadcasted_iota(jnp.int32, (8, 128), 1), 8)
    for i in range(NX):
        tile = jnp.zeros((8, 128), F32)
        for v in range(NZ):
            first = i * block + v * 8
            tile = jnp.where(owner == v, top_column[first : first + 8], tile)
            tile = jnp.where(owner == v + 8, sum_column[first : first + 8], tile)
        stat_send[i] = tile
    for k in far_x:
        send(stat_send.at[k], stat_recv.at[k], st_send, st_recv, along_x(-k))

    def send_half(h):
        num_send[h] = numer[h].astype(BF16)
        for k in far_x:
            send(
                num_send.at[h, pl.ds(k * block, block)],
                num_recv.at[h, k],
                nx_send.at[h],
                nx_recv.at[h],
                along_x(-k),
            )

    send_half(0)

    for c in range(steps):
        here = pl.ds(c * step_keys, step_keys)
        part = dot(probs[:, here], keys[here, half:latent])
        if c + 1 < steps:
            part = scaled(part, jnp.exp2(tops[c + 1] - top))
        numer[1] = part if c == 0 else numer[1] + part

    send_half(1)
    done(q_packed.at[pl.ds(1, NX - 1)], qx_send)

    done(stat_recv.at[pl.ds(1, NX - 1)], st_recv)
    found = [stat_send[0]] + [stat_recv[k] for k in range(1, NX)]
    factors = [[] for _ in found]
    z_stats = []
    for v in range(NZ):
        tops = [jnp.broadcast_to(f[:, 8 * v : 8 * v + 1], (8, 128)) for f in found]
        top_x = functools.reduce(jnp.maximum, tops)
        coarse = top_x.astype(BF16).astype(F32)
        top_x = coarse + (top_x - coarse).astype(BF16).astype(F32)
        total_x = jnp.zeros((8, 128), F32)
        for f, t, held in zip(found, tops, factors):
            held.append(jnp.exp2(t - top_x))
            total_x = total_x + f[:, 64 + 8 * v : 64 + 8 * v + 1] * held[v]
        z_stats.append(jnp.where(lane < 64, top_x, total_x))
        if v > 0:
            coarse = z_stats[v].astype(BF16).astype(F32)
            low_send[v, :, 128:256] = jnp.concatenate(
                [coarse, z_stats[v] - coarse], axis=0
            ).astype(BF16)
    factors = [
        jnp.concatenate([jnp.concatenate(held, axis=0)] * (half // 128), axis=1) for held in factors
    ]

    spans = ((0, 256), (256, 384))
    own_half = []
    for h in range(2):
        done(num_recv.at[h, pl.ds(1, NX - 1)], nx_recv.at[h])
        merged = numer[h, 0:block, :] * factors[0]
        for k in range(1, NX):
            merged = merged + num_recv[h, k].astype(F32) * factors[k]
        own_half.append([merged[0:8, j : j + 128] for j in range(0, half, 128)])
        low, high = spans[h]
        for k in far_z:
            part = merged[k * 8 : (k + 1) * 8]
            low_send[k, :, low : low + 128] = jnp.concatenate(
                [part[:, 0:128], part[:, 128:256]], axis=0
            ).astype(BF16)
            send(
                low_send.at[k, :, low:high],
                low_recv.at[k, :, low:high],
                nz_send.at[h],
                nz_recv.at[h],
                along_z(-k),
            )
    done(stat_recv.at[pl.ds(1, NX - 1)], st_send)
    for h in range(2):
        done(num_recv.at[h, pl.ds(1, NX - 1)], nx_send.at[h])

    done(low_recv.at[pl.ds(1, NZ - 1), :, 0:256], nz_recv.at[0])
    found = [z_stats[0]]
    for k in range(1, NZ):
        held = low_recv[k, :, 128:256].astype(F32)
        found.append(held[0:8] + held[8:16])
    tops = [jnp.broadcast_to(f[:, 0:1], (8, 128)) for f in found]
    top_z = functools.reduce(jnp.maximum, tops)
    factors = [jnp.exp2(t - top_z) for t in tops]
    total_z = sum(f[:, 64:65] * w for f, w in zip(found, factors))
    attended = []
    for h in range(2):
        if h == 1:
            done(low_recv.at[pl.ds(1, NZ - 1), :, 256:384], nz_recv.at[1])
        merged = [own * factors[0] for own in own_half[h]]
        for k in range(1, NZ):
            held = low_recv[k, :, spans[h][0] : spans[h][0] + 128].astype(F32)
            for j in range(2):
                merged[j] = merged[j] + held[j * 8 : (j + 1) * 8] * factors[k]
        attended += [m / total_z for m in merged]
    attended = jnp.concatenate(attended, axis=1)
    head = lax.rem(lax.broadcasted_iota(jnp.int32, attended.shape, 0), heads)
    spread = [jnp.where(head == i, attended, 0.0) for i in range(heads)]
    up_copy.wait()
    values = dot(
        jnp.concatenate(spread, axis=1).astype(BF16), w_up[...].reshape(heads * latent, -1)
    )

    own = pl.ds(pl.multiple_of(g * 8, 8), 8)
    head_values[own, :] = values.astype(BF16).astype(F32)
    for k in range(1, NG):
        send(head_values.at[own], head_values.at[own], v_send, v_recv, along_g(k))
    others = head_values.at[pl.ds(0, (NG - 1) * 8)]
    done(low_recv.at[pl.ds(1, NZ - 1), :, 0:256], nz_send.at[0])
    done(low_recv.at[pl.ds(1, NZ - 1), :, 256:384], nz_send.at[1])
    done(others, v_recv)
    wide = [head_values[pl.ds(i, tokens * NG, stride=heads), :] for i in range(heads)]
    terms = dot(jnp.concatenate(wide, axis=1).astype(BF16), w_placed[...])

    for i in range(NX):
        term_send[i] = terms[:, i * x_lanes : (i + 1) * x_lanes].astype(BF16)
    for k in far_x:
        send(term_send.at[lax.rem(x + k, NX)], term_recv.at[k], tx_send, tx_recv, along_x(k))
    done(others, v_send)
    summed = term_send[x].astype(F32)
    done(term_recv.at[pl.ds(1, NX - 1)], tx_recv)
    for k in range(1, NX):
        summed = summed + term_recv[k].astype(F32)
    for i in range(x_lanes // 128):
        last_send[i] = summed[:, i * 128 : (i + 1) * 128].astype(BF16)
    per_tile = 128 // out_group
    for k in far_z:
        send(
            last_send.at[lax.div(lax.rem(z + k, NZ), per_tile)],
            last_recv.at[k],
            tz_send,
            tz_recv,
            along_z(k),
        )
    done(term_recv.at[pl.ds(1, NX - 1)], tx_send)
    final = last_send[lax.div(z, per_tile)].astype(F32)
    done(last_recv.at[pl.ds(1, NZ - 1)], tz_recv)
    for k in range(1, NZ):
        final = final + last_recv[k].astype(F32)
    place = lax.rem(z, per_tile)
    chosen = final
    for i in range(1, per_tile):
        chosen = jnp.where(place == i, pltpu.roll(final, 128 - i * out_group, 1), chosen)
    result[...] = chosen
    done(last_recv.at[pl.ds(1, NZ - 1)], tz_send)


def body(sizes, queries, cache, slot_page, lengths, w_uv, w_out):
    NX, NZ, NG, own_columns = sizes
    tokens, heads, width = queries.shape[1:]
    latent = w_uv.shape[1]
    half = latent // 2
    key_rows = cache.shape[1] * cache.shape[2]
    rows = NX * NZ * 8
    block = NZ * 8
    x_lanes = NZ * out_group
    sem = pltpu.SemaphoreType.DMA
    scratch = [
        pltpu.VMEM(queries.shape, BF16),
        pltpu.VMEM((8, 768), F32),
        pltpu.VMEM((NX, NZ, 16, 384), BF16),
        pltpu.VMEM((rows, 640), BF16),
        pltpu.VMEM((key_rows, width), BF16),
        pltpu.SMEM(slot_page.shape, jnp.int32),
        pltpu.SMEM(lengths.shape, jnp.int32),
        pltpu.VMEM(w_uv.shape, BF16),
        pltpu.VMEM(w_out.shape, BF16),
        pltpu.VMEM((w_out.shape[0], NX * x_lanes), BF16),
        pltpu.VMEM((key_rows, 128), BF16),
        pltpu.VMEM((2, step_keys, rows), F32),
        pltpu.VMEM((rows, key_rows), BF16),
        pltpu.VMEM((2, rows, half), F32),
        pltpu.VMEM((2, rows, half), BF16),
        pltpu.VMEM((2, NX, block, half), BF16),
        pltpu.VMEM((NX, 8, 128), F32),
        pltpu.VMEM((NX, 8, 128), F32),
        pltpu.VMEM((NZ, 16, 384), BF16),
        pltpu.VMEM((NZ, 16, 384), BF16),
        pltpu.VMEM((NG * 8, 128), F32),
        pltpu.VMEM((NX, tokens * NG, x_lanes), BF16),
        pltpu.VMEM((NX, tokens * NG, x_lanes), BF16),
        pltpu.VMEM((x_lanes // 128, tokens * NG, 128), BF16),
        pltpu.VMEM((NZ, tokens * NG, 128), BF16),
        sem((5,)),
        sem((key_rows // step_keys,)),
        sem,
        sem((NZ,)),
        sem,
        sem,
        sem,
        sem,
        sem((2,)),
        sem((2,)),
        sem((2,)),
        sem((2,)),
        sem,
        sem,
        sem,
        sem,
        sem,
        sem,
    ]
    result = pl.pallas_call(
        functools.partial(kernel, sizes),
        out_shape=jax.ShapeDtypeStruct((tokens * NG, 128), F32),
        in_specs=[pl.BlockSpec(memory_space=pltpu.HBM)] * 6,
        out_specs=pl.BlockSpec(memory_space=pltpu.VMEM),
        scratch_shapes=scratch,
        compiler_params=pltpu.CompilerParams(
            collective_id=0, has_side_effects=True, vmem_limit_bytes=56 * 1024 * 1024
        ),
    )(queries, cache.reshape(key_rows, width), slot_page, lengths, w_uv, w_out)
    return result[:, 0:own_columns].astype(BF16).reshape(NG, tokens, own_columns)


def solution(mesh, NX=4):
    NG, pages = mesh.shape["group"], mesh.shape["page"]
    in_specs = (
        P("group", None, "page", None),
        P("group", "page", None, None),
        P("group", "page"),
        P("group"),
        P("page", None, None),
        P("page", "group"),
    )
    out_specs = P(None, None, ("group", "page"))

    def step(queries, cache, slot_page, lengths, w_uv, w_out):
        sizes = (NX, pages // NX, NG, w_out.shape[1] // pages)
        return body(sizes, queries, cache, slot_page, lengths, w_uv, w_out)

    return jax.shard_map(step, mesh=mesh, in_specs=in_specs, out_specs=out_specs, check_vma=False)
```

```python
import functools

import jax
import jax.numpy as jnp
from jax import lax
from jax.experimental import pallas as pl
from jax.experimental.pallas import tpu as pltpu
from jax.sharding import PartitionSpec as P

MESH = pl.DeviceIdType.MESH
F32 = jnp.float32
BF16 = jnp.bfloat16
score_scale = 192.0 ** (-0.5)
log2_e = 1.4426950408889634
masked_fill = -(2.0**99)
lowest_top = -(2.0**20)
out_group = 32
step_keys = 1024
tile_keys = 512
turned_early = 3


def dot(a, b, contract_b=0):
    return lax.dot_general(a, b, (((1,), (contract_b,)), ((), ())), preferred_element_type=F32)


def kernel(
    sizes,
    q_hbm,
    k_hbm,
    page_hbm,
    length_hbm,
    up_hbm,
    out_hbm,
    result,
    q_in,
    q_rows,
    q_packed,
    q_all,
    keys,
    pages,
    length,
    w_up,
    w_out,
    w_placed,
    tails,
    scores,
    probs,
    numer,
    turned,
    num_send,
    num_recv,
    stat_send,
    stat_recv,
    low_send,
    low_recv,
    head_values,
    term_send,
    term_recv,
    last_send,
    last_recv,
    local_sem,
    key_sem,
    qz_send,
    qz_recv,
    qx_send,
    qx_recv,
    st_send,
    st_recv,
    nx_send,
    nx_recv,
    nz_send,
    nz_recv,
    v_send,
    v_recv,
    tx_send,
    tx_recv,
    tz_send,
    tz_recv,
):
    NX, NZ, NG, own_columns = sizes
    width = q_in.shape[-1]
    latent = w_up.shape[1]
    half = latent // 2
    key_rows = keys.shape[0]
    rows = q_all.shape[0]
    block = rows // NX
    steps = key_rows // step_keys
    tokens, heads = q_in.shape[1], q_in.shape[2]

    g = lax.axis_index("group")
    page = lax.axis_index("page")
    x, z = lax.div(page, NZ), lax.rem(page, NZ)

    def along_x(k):
        return {"page": lax.rem(x + k + NX, NX) * NZ + z}

    def along_z(k):
        return {"page": x * NZ + lax.rem(z + k + NZ, NZ)}

    def along_g(k):
        return {"group": lax.rem(g + k + NG, NG)}

    def send(source, target, send_sem, recv_sem, device):
        copy = pltpu.make_async_remote_copy(
            src_ref=source,
            dst_ref=target,
            send_sem=send_sem,
            recv_sem=recv_sem,
            device_id=device,
            device_id_type=MESH,
        )
        copy.start()
        return copy

    def done(region, sem):
        pltpu.make_async_copy(region, region, sem).wait()

    far_z = sorted(range(1, NZ), key=lambda k: -min(k, NZ - k))
    far_x = sorted(range(1, NX), key=lambda k: -min(k, NX - k))

    barrier = pltpu.get_barrier_semaphore()
    for k in range(1, NX):
        pl.semaphore_signal(barrier, inc=1, device_id=along_x(k), device_id_type=MESH)
    for k in range(1, NZ):
        pl.semaphore_signal(barrier, inc=1, device_id=along_z(k), device_id_type=MESH)
    for k in range(1, NG):
        pl.semaphore_signal(barrier, inc=1, device_id=along_g(k), device_id_type=MESH)

    def local(source, target, sem):
        copy = pltpu.make_async_copy(source, target, sem)
        copy.start()
        return copy

    q_copy = local(q_hbm, q_in, local_sem.at[0])
    page_copy = local(page_hbm, pages, local_sem.at[1])
    length_copy = local(length_hbm, length, local_sem.at[2])
    out_copy = local(out_hbm, w_out, local_sem.at[3])
    key_copies = [
        local(
            k_hbm.at[pl.ds(c * step_keys, step_keys)],
            keys.at[pl.ds(c * step_keys, step_keys)],
            key_sem.at[c],
        )
        for c in range(steps)
    ]
    up_copy = local(up_hbm, w_up, local_sem.at[4])

    q_copy.wait()
    place = lax.broadcasted_iota(jnp.int32, (8, 256), 1) + 512
    owner = lax.broadcasted_iota(jnp.int32, (8, 256), 0) // heads
    q_rows[:, 512:768] = jnp.where(place == width + owner, 1.0, 0.0)
    for t in range(tokens):
        q_rows[t * heads : (t + 1) * heads, 0:width] = q_in[0, t].astype(F32)
    q_packed[0, 0] = jnp.concatenate([q_rows[:, 0:384], q_rows[:, 384:768]], axis=0).astype(BF16)
    pl.semaphore_wait(barrier, NX + NZ + NG - 3)
    for k in far_z:
        send(q_packed.at[0, 0], q_packed.at[0, k], qz_send, qz_recv.at[k], along_z(k))

    def forward(j):
        for k in far_x:
            send(q_packed.at[0, j], q_packed.at[k, j], qx_send, qx_recv, along_x(k))

    forward(0)

    page_copy.wait()
    length_copy.wait()
    lane = lax.broadcasted_iota(jnp.int32, (8, 128), 1)
    spot = lax.broadcasted_iota(jnp.int32, (64, 64), 0)
    token = lax.broadcasted_iota(jnp.int32, (64, 64), 1)
    last = jnp.where(token < tokens, length[0] - tokens + token - spot, 2**30)

    for k in far_z[::-1]:
        done(q_packed.at[0, k], qz_recv.at[k])
        forward(k)

    done(q_packed.at[0, pl.ds(1, NZ - 1)], qz_send)
    for c, copy in enumerate(key_copies):
        copy.wait()

        @pl.loop(c * step_keys // 64, (c + 1) * step_keys // 64, unroll=8)
        def _(i):
            at = pl.ds(pl.multiple_of(i * 64, 64), 64)
            mask = jnp.where(pages[0, i] * 64 <= last, 0.0, masked_fill).astype(BF16)
            tails[at, :] = jnp.concatenate([keys[at, latent:width], mask], axis=1)

    def turn(c):
        here = pl.ds(c * step_keys, step_keys)
        turned[:, here] = keys[here, 0:latent].T

    for c in range(turned_early):
        turn(c)
    done(q_packed.at[pl.ds(1, NX - 1)], qx_recv)
    for i in range(NX):
        for j in range(0, NZ, 2):
            pair = []
            for part in (q_packed[i, j].astype(F32), q_packed[i, j + 1].astype(F32)):
                pair.append(jnp.concatenate([part[0:8], part[8:16, 0:256]], axis=1))
            first = i * block + j * 8
            q_all[first : first + 16, :] = jnp.concatenate(pair, axis=0).astype(BF16)

    def as_column(row):
        return jnp.broadcast_to(row, (128, rows)).T

    def score_tile(c, n):
        at = pl.ds(c * step_keys + n * tile_keys, tile_keys)
        wide = jnp.concatenate([keys[at, 0:latent], tails[at, :]], axis=1)
        s = dot(wide, q_all[...], 1) * (score_scale * log2_e)
        scores[c % 2, n * tile_keys : (n + 1) * tile_keys, :] = s
        return jnp.max(s.reshape(-1, 8, rows), axis=0)

    tiles = step_keys // tile_keys
    largest = functools.reduce(jnp.maximum, [score_tile(0, n) for n in range(tiles)])
    tops = [jnp.full((1, rows), lowest_top, F32)]
    total = jnp.zeros((8, rows), F32)
    for c in range(steps):
        top = jnp.maximum(jnp.max(largest, axis=0, keepdims=True), tops[-1])
        shrink = jnp.exp2(tops[-1] - top)
        total = total * shrink
        tops.append(top)
        found, pieces = [], []
        for n in range(tiles):
            if c + 1 < steps:
                found.append(score_tile(c + 1, n))
            for low in range(n * tile_keys, (n + 1) * tile_keys, 256):
                p = jnp.exp2(scores[c % 2, low : low + 256, :] - top)
                total = total + jnp.sum(p.reshape(-1, 8, rows), axis=0)
                p = p.astype(BF16)
                probs[c * step_keys + low : c * step_keys + low + 256, :] = p
                pieces.append(p)
        if found:
            largest = functools.reduce(jnp.maximum, found)
        if turned_early <= c + 1 < steps:
            turn(c + 1)
        here = pl.ds(c * step_keys, step_keys)
        part = dot(turned[0:half, here], jnp.concatenate(pieces, axis=0))
        numer[0] = part if c == 0 else numer[0] * shrink + part

    top_column = as_column(top)
    sum_column = as_column(jnp.sum(total, axis=0, keepdims=True))
    owner = lax.div(lax.broadcasted_iota(jnp.int32, (8, 128), 1), 8)
    for i in range(NX):
        tile = jnp.zeros((8, 128), F32)
        for v in range(NZ):
            first = i * block + v * 8
            tile = jnp.where(owner == v, top_column[first : first + 8], tile)
            tile = jnp.where(owner == v + 8, sum_column[first : first + 8], tile)
        stat_send[i] = tile
    for k in far_x:
        send(stat_send.at[k], stat_recv.at[k], st_send, st_recv, along_x(-k))

    def send_half(h):
        num_send[h] = numer[h].astype(BF16).T
        for k in far_x:
            send(
                num_send.at[h, pl.ds(k * block, block)],
                num_recv.at[h, k],
                nx_send.at[h],
                nx_recv.at[h],
                along_x(-k),
            )

    send_half(0)

    for c in range(steps):
        here = pl.ds(c * step_keys, step_keys)
        part = dot(turned[half:latent, here], probs[here, :])
        if c + 1 < steps:
            part = part * jnp.exp2(tops[c + 1] - top)
        numer[1] = part if c == 0 else numer[1] + part

    send_half(1)
    done(q_packed.at[pl.ds(1, NX - 1)], qx_send)

    done(stat_recv.at[pl.ds(1, NX - 1)], st_recv)
    found = [stat_send[0]] + [stat_recv[k] for k in range(1, NX)]
    factors = [[] for _ in found]
    z_stats = []
    for v in range(NZ):
        tops = [jnp.broadcast_to(f[:, 8 * v : 8 * v + 1], (8, 128)) for f in found]
        top_x = functools.reduce(jnp.maximum, tops)
        coarse = top_x.astype(BF16).astype(F32)
        top_x = coarse + (top_x - coarse).astype(BF16).astype(F32)
        total_x = jnp.zeros((8, 128), F32)
        for f, t, held in zip(found, tops, factors):
            held.append(jnp.exp2(t - top_x))
            total_x = total_x + f[:, 64 + 8 * v : 64 + 8 * v + 1] * held[v]
        z_stats.append(jnp.where(lane < 64, top_x, total_x))
        if v > 0:
            coarse = z_stats[v].astype(BF16).astype(F32)
            low_send[v, :, 128:256] = jnp.concatenate(
                [coarse, z_stats[v] - coarse], axis=0
            ).astype(BF16)
    factors = [
        jnp.concatenate([jnp.concatenate(held, axis=0)] * (half // 128), axis=1) for held in factors
    ]

    spans = ((0, 256), (256, 384))
    own_half = []
    for h in range(2):
        done(num_recv.at[h, pl.ds(1, NX - 1)], nx_recv.at[h])
        merged = num_send[h, 0:block, :].astype(F32) * factors[0]
        for k in range(1, NX):
            merged = merged + num_recv[h, k].astype(F32) * factors[k]
        own_half.append([merged[0:8, j : j + 128] for j in range(0, half, 128)])
        low, high = spans[h]
        for k in far_z:
            part = merged[k * 8 : (k + 1) * 8]
            low_send[k, :, low : low + 128] = jnp.concatenate(
                [part[:, 0:128], part[:, 128:256]], axis=0
            ).astype(BF16)
            send(
                low_send.at[k, :, low:high],
                low_recv.at[k, :, low:high],
                nz_send.at[h],
                nz_recv.at[h],
                along_z(-k),
            )
    x_columns = own_columns * NZ
    x_lanes = out_group * NZ
    out_copy.wait()
    place = lax.broadcasted_iota(jnp.int32, (1, x_lanes), 1)
    inside = lax.rem(place, out_group)
    wanted = lax.div(place, out_group) * own_columns + inside
    wanted = jnp.where(inside < own_columns, wanted, -(2**20))
    for i in range(NX):
        low = i * x_columns // 128 * 128
        high = min(-(-(i + 1) * x_columns // 128) * 128, w_out.shape[1])
        column = lax.broadcasted_iota(jnp.int32, (high - low, x_lanes), 0)
        pick = jnp.where(column == wanted + (i * x_columns - low), 1.0, 0.0).astype(BF16)
        w_placed[:, i * x_lanes : (i + 1) * x_lanes] = dot(w_out[:, low:high], pick).astype(BF16)

    done(stat_recv.at[pl.ds(1, NX - 1)], st_send)
    for h in range(2):
        done(num_recv.at[h, pl.ds(1, NX - 1)], nx_send.at[h])

    done(low_recv.at[pl.ds(1, NZ - 1), :, 0:256], nz_recv.at[0])
    found = [z_stats[0]]
    for k in range(1, NZ):
        held = low_recv[k, :, 128:256].astype(F32)
        found.append(held[0:8] + held[8:16])
    tops = [jnp.broadcast_to(f[:, 0:1], (8, 128)) for f in found]
    top_z = functools.reduce(jnp.maximum, tops)
    factors = [jnp.exp2(t - top_z) for t in tops]
    total_z = sum(f[:, 64:65] * w for f, w in zip(found, factors))
    attended = []
    for h in range(2):
        if h == 1:
            done(low_recv.at[pl.ds(1, NZ - 1), :, 256:384], nz_recv.at[1])
        merged = [own * factors[0] for own in own_half[h]]
        for k in range(1, NZ):
            held = low_recv[k, :, spans[h][0] : spans[h][0] + 128].astype(F32)
            for j in range(2):
                merged[j] = merged[j] + held[j * 8 : (j + 1) * 8] * factors[k]
        attended += [m / total_z for m in merged]
    attended = jnp.concatenate(attended, axis=1)
    head = lax.rem(lax.broadcasted_iota(jnp.int32, attended.shape, 0), heads)
    spread = [jnp.where(head == i, attended, 0.0) for i in range(heads)]
    up_copy.wait()
    values = dot(
        jnp.concatenate(spread, axis=1).astype(BF16), w_up[...].reshape(heads * latent, -1)
    )

    own = pl.ds(pl.multiple_of(g * 8, 8), 8)
    head_values[own, :] = values.astype(BF16).astype(F32)
    for k in range(1, NG):
        send(head_values.at[own], head_values.at[own], v_send, v_recv, along_g(k))
    others = head_values.at[pl.ds(0, (NG - 1) * 8)]
    done(low_recv.at[pl.ds(1, NZ - 1), :, 0:256], nz_send.at[0])
    done(low_recv.at[pl.ds(1, NZ - 1), :, 256:384], nz_send.at[1])
    done(others, v_recv)
    wide = [head_values[pl.ds(i, tokens * NG, stride=heads), :] for i in range(heads)]
    terms = dot(jnp.concatenate(wide, axis=1).astype(BF16), w_placed[...])

    for i in range(NX):
        term_send[i] = terms[:, i * x_lanes : (i + 1) * x_lanes].astype(BF16)
    for k in far_x:
        send(term_send.at[lax.rem(x + k, NX)], term_recv.at[k], tx_send, tx_recv, along_x(k))
    done(others, v_send)
    summed = term_send[x].astype(F32)
    done(term_recv.at[pl.ds(1, NX - 1)], tx_recv)
    for k in range(1, NX):
        summed = summed + term_recv[k].astype(F32)
    for i in range(x_lanes // 128):
        last_send[i] = summed[:, i * 128 : (i + 1) * 128].astype(BF16)
    per_tile = 128 // out_group
    for k in far_z:
        send(
            last_send.at[lax.div(lax.rem(z + k, NZ), per_tile)],
            last_recv.at[k],
            tz_send,
            tz_recv,
            along_z(k),
        )
    done(term_recv.at[pl.ds(1, NX - 1)], tx_send)
    final = last_send[lax.div(z, per_tile)].astype(F32)
    done(last_recv.at[pl.ds(1, NZ - 1)], tz_recv)
    for k in range(1, NZ):
        final = final + last_recv[k].astype(F32)
    place = lax.rem(z, per_tile)
    chosen = final
    for i in range(1, per_tile):
        chosen = jnp.where(place == i, pltpu.roll(final, 128 - i * out_group, 1), chosen)
    result[...] = chosen
    done(last_recv.at[pl.ds(1, NZ - 1)], tz_send)


def body(sizes, queries, cache, slot_page, lengths, w_uv, w_out):
    NX, NZ, NG, own_columns = sizes
    tokens, heads, width = queries.shape[1:]
    latent = w_uv.shape[1]
    half = latent // 2
    key_rows = cache.shape[1] * cache.shape[2]
    rows = NX * NZ * 8
    block = NZ * 8
    x_lanes = NZ * out_group
    sem = pltpu.SemaphoreType.DMA
    scratch = [
        pltpu.VMEM(queries.shape, BF16),
        pltpu.VMEM((8, 768), F32),
        pltpu.VMEM((NX, NZ, 16, 384), BF16),
        pltpu.VMEM((rows, 640), BF16),
        pltpu.VMEM((key_rows, width), BF16),
        pltpu.SMEM(slot_page.shape, jnp.int32),
        pltpu.SMEM(lengths.shape, jnp.int32),
        pltpu.VMEM(w_uv.shape, BF16),
        pltpu.VMEM(w_out.shape, BF16),
        pltpu.VMEM((w_out.shape[0], NX * x_lanes), BF16),
        pltpu.VMEM((key_rows, 128), BF16),
        pltpu.VMEM((2, step_keys, rows), F32),
        pltpu.VMEM((key_rows, rows), BF16),
        pltpu.VMEM((2, half, rows), F32),
        pltpu.VMEM((latent, key_rows), BF16),
        pltpu.VMEM((2, rows, half), BF16),
        pltpu.VMEM((2, NX, block, half), BF16),
        pltpu.VMEM((NX, 8, 128), F32),
        pltpu.VMEM((NX, 8, 128), F32),
        pltpu.VMEM((NZ, 16, 384), BF16),
        pltpu.VMEM((NZ, 16, 384), BF16),
        pltpu.VMEM((NG * 8, 128), F32),
        pltpu.VMEM((NX, tokens * NG, x_lanes), BF16),
        pltpu.VMEM((NX, tokens * NG, x_lanes), BF16),
        pltpu.VMEM((x_lanes // 128, tokens * NG, 128), BF16),
        pltpu.VMEM((NZ, tokens * NG, 128), BF16),
        sem((5,)),
        sem((key_rows // step_keys,)),
        sem,
        sem((NZ,)),
        sem,
        sem,
        sem,
        sem,
        sem((2,)),
        sem((2,)),
        sem((2,)),
        sem((2,)),
        sem,
        sem,
        sem,
        sem,
        sem,
        sem,
    ]
    result = pl.pallas_call(
        functools.partial(kernel, sizes),
        out_shape=jax.ShapeDtypeStruct((tokens * NG, 128), F32),
        in_specs=[pl.BlockSpec(memory_space=pltpu.HBM)] * 6,
        out_specs=pl.BlockSpec(memory_space=pltpu.VMEM),
        scratch_shapes=scratch,
        compiler_params=pltpu.CompilerParams(
            collective_id=0, has_side_effects=True, vmem_limit_bytes=56 * 1024 * 1024
        ),
    )(queries, cache.reshape(key_rows, width), slot_page, lengths, w_uv, w_out)
    return result[:, 0:own_columns].astype(BF16).reshape(NG, tokens, own_columns)


def solution(mesh, NX=4):
    NG, pages = mesh.shape["group"], mesh.shape["page"]
    in_specs = (
        P("group", None, "page", None),
        P("group", "page", None, None),
        P("group", "page"),
        P("group"),
        P("page", None, None),
        P("page", "group"),
    )
    out_specs = P(None, None, ("group", "page"))

    def step(queries, cache, slot_page, lengths, w_uv, w_out):
        sizes = (NX, pages // NX, NG, w_out.shape[1] // pages)
        return body(sizes, queries, cache, slot_page, lengths, w_uv, w_out)

    return jax.shard_map(step, mesh=mesh, in_specs=in_specs, out_specs=out_specs, check_vma=False)
```

```python
import functools

import jax
import jax.numpy as jnp
from jax import lax
from jax.experimental import pallas as pl
from jax.experimental.pallas import tpu as pltpu
from jax.sharding import PartitionSpec as P

MESH = pl.DeviceIdType.MESH
F32 = jnp.float32
BF16 = jnp.bfloat16
score_scale = 192.0 ** (-0.5)
log2_e = 1.4426950408889634
masked_fill = -(2.0**99)
lowest_top = -(2.0**20)
out_group = 32
step_keys = 1024
tile_keys = 512


def dot(a, b, contract_b=0):
    return lax.dot_general(a, b, (((1,), (contract_b,)), ((), ())), preferred_element_type=F32)


def kernel(
    sizes,
    q_hbm,
    k_hbm,
    page_hbm,
    length_hbm,
    up_hbm,
    out_hbm,
    result,
    q_in,
    q_rows,
    q_packed,
    q_all,
    keys,
    pages,
    length,
    w_up,
    w_out,
    w_placed,
    tails,
    scores,
    probs,
    numer,
    num_send,
    num_recv,
    stat_send,
    stat_recv,
    low_send,
    low_recv,
    head_values,
    term_send,
    term_recv,
    last_send,
    last_recv,
    local_sem,
    key_sem,
    qz_send,
    qz_recv,
    qx_send,
    qx_recv,
    st_send,
    st_recv,
    nx_send,
    nx_recv,
    nz_send,
    nz_recv,
    v_send,
    v_recv,
    tx_send,
    tx_recv,
    tz_send,
    tz_recv,
):
    NX, NZ, NG, own_columns = sizes
    width = q_in.shape[-1]
    latent = w_up.shape[1]
    half = latent // 2
    key_rows = keys.shape[0]
    rows = q_all.shape[0]
    block = rows // NX
    steps = key_rows // step_keys
    tokens, heads = q_in.shape[1], q_in.shape[2]

    g = lax.axis_index("group")
    page = lax.axis_index("page")
    x, z = lax.div(page, NZ), lax.rem(page, NZ)

    def along_x(k):
        return {"page": lax.rem(x + k + NX, NX) * NZ + z}

    def along_z(k):
        return {"page": x * NZ + lax.rem(z + k + NZ, NZ)}

    def along_g(k):
        return {"group": lax.rem(g + k + NG, NG)}

    def send(source, target, send_sem, recv_sem, device):
        copy = pltpu.make_async_remote_copy(
            src_ref=source,
            dst_ref=target,
            send_sem=send_sem,
            recv_sem=recv_sem,
            device_id=device,
            device_id_type=MESH,
        )
        copy.start()
        return copy

    def done(region, sem):
        pltpu.make_async_copy(region, region, sem).wait()

    far_z = sorted(range(1, NZ), key=lambda k: -min(k, NZ - k))
    order = [0] + far_z[::-1]
    far_g = sorted(range(1, NG), key=lambda k: -min(k, NG - k))
    far_x = sorted(range(1, NX), key=lambda k: -min(k, NX - k))

    def local(source, target, sem):
        copy = pltpu.make_async_copy(source, target, sem)
        copy.start()
        return copy

    q_copy = local(q_hbm, q_in, local_sem.at[0])
    barrier = pltpu.get_barrier_semaphore()
    peers = [along_z(k) for k in far_z] + [along_x(k) for k in far_x] + [along_g(k) for k in far_g]
    for peer in peers:
        pl.semaphore_signal(barrier, inc=1, device_id=peer, device_id_type=MESH)
    page_copy = local(page_hbm, pages, local_sem.at[1])
    length_copy = local(length_hbm, length, local_sem.at[2])
    out_copy = local(out_hbm, w_out, local_sem.at[3])
    key_copies = [
        local(
            k_hbm.at[pl.ds(c * step_keys, step_keys)],
            keys.at[pl.ds(c * step_keys, step_keys)],
            key_sem.at[c],
        )
        for c in range(steps)
    ]
    up_copy = local(up_hbm, w_up, local_sem.at[4])

    q_copy.wait()
    place = lax.broadcasted_iota(jnp.int32, (8, 256), 1) + 512
    owner = lax.broadcasted_iota(jnp.int32, (8, 256), 0) // heads
    q_rows[:, 512:768] = jnp.where(place == width + owner, 1.0, 0.0)
    for t in range(tokens):
        q_rows[t * heads : (t + 1) * heads, 0:width] = q_in[0, t].astype(F32)
    q_packed[0] = jnp.concatenate([q_rows[:, 0:384], q_rows[:, 384:768]], axis=0).astype(BF16)
    pl.semaphore_wait(barrier, len(peers))
    for k in far_z:
        send(q_packed.at[0], q_packed.at[k], qz_send, qz_recv.at[k], along_z(k))

    page_copy.wait()
    length_copy.wait()
    lane = lax.broadcasted_iota(jnp.int32, (8, 128), 1)
    spot = lax.broadcasted_iota(jnp.int32, (64, 64), 0)
    token = lax.broadcasted_iota(jnp.int32, (64, 64), 1)
    last = jnp.where(token < tokens, length[0] - tokens + token - spot, 2**30)

    for c, copy in enumerate(key_copies):
        copy.wait()

        @pl.loop(c * step_keys // 64, (c + 1) * step_keys // 64, unroll=8)
        def _(i):
            at = pl.ds(pl.multiple_of(i * 64, 64), 64)
            mask = jnp.where(pages[0, i] * 64 <= last, 0.0, masked_fill).astype(BF16)
            tails[at, :] = jnp.concatenate([keys[at, latent:width], mask], axis=1)

    for n in range(0, NZ, 2):
        pair = []
        for j in order[n : n + 2]:
            if j > 0:
                done(q_packed.at[j], qz_recv.at[j])
            part = q_packed[j].astype(F32)
            pair.append(jnp.concatenate([part[0:8], part[8:16, 0:256]], axis=1))
        q_all[n * 8 : n * 8 + 16, :] = jnp.concatenate(pair, axis=0).astype(BF16)
        for k in far_x:
            send(
                q_all.at[pl.ds(n * 8, 16)],
                q_all.at[pl.ds(k * block + n * 8, 16)],
                qx_send,
                qx_recv,
                along_x(k),
            )
    done(q_packed.at[pl.ds(1, NZ - 1)], qz_send)

    done(q_all.at[pl.ds(block, rows - block)], qx_recv)

    def as_column(row):
        return jnp.broadcast_to(row, (128, rows)).T

    def scaled(value, row):
        return value * jnp.concatenate([as_column(row)] * (value.shape[1] // 128), axis=1)

    def score_tile(c, n):
        at = pl.ds(c * step_keys + n * tile_keys, tile_keys)
        wide = jnp.concatenate([keys[at, 0:latent], tails[at, :]], axis=1)
        s = dot(wide, q_all[...], 1) * (score_scale * log2_e)
        scores[c % 2, n * tile_keys : (n + 1) * tile_keys, :] = s
        return jnp.max(s.reshape(-1, 8, rows), axis=0)

    tiles = step_keys // tile_keys
    largest = functools.reduce(jnp.maximum, [score_tile(0, n) for n in range(tiles)])
    tops = [jnp.full((1, rows), lowest_top, F32)]
    total = jnp.zeros((8, rows), F32)
    for c in range(steps):
        top = jnp.maximum(jnp.max(largest, axis=0, keepdims=True), tops[-1])
        shrink = jnp.exp2(tops[-1] - top)
        total = total * shrink
        tops.append(top)
        found, pieces = [], []
        for n in range(tiles):
            if c + 1 < steps:
                found.append(score_tile(c + 1, n))
            for low in range(n * tile_keys, (n + 1) * tile_keys, 256):
                p = jnp.exp2(scores[c % 2, low : low + 256, :] - top)
                total = total + jnp.sum(p.reshape(-1, 8, rows), axis=0)
                p = p.astype(BF16).T
                probs[:, c * step_keys + low : c * step_keys + low + 256] = p
                pieces.append(p)
        if found:
            largest = functools.reduce(jnp.maximum, found)
        part = dot(jnp.concatenate(pieces, axis=1), keys[pl.ds(c * step_keys, step_keys), 0:half])
        numer[0] = part if c == 0 else scaled(numer[0], shrink) + part

    top_column = as_column(top)
    sum_column = as_column(jnp.sum(total, axis=0, keepdims=True))
    owner = lax.div(lax.broadcasted_iota(jnp.int32, (8, 128), 1), 8)
    for i in range(NX):
        tile = jnp.zeros((8, 128), F32)
        for v in range(NZ):
            first = i * block + v * 8
            tile = jnp.where(owner == v, top_column[first : first + 8], tile)
            tile = jnp.where(owner == v + 8, sum_column[first : first + 8], tile)
        stat_send[i] = tile
    for k in far_x:
        send(stat_send.at[k], stat_recv.at[k], st_send, st_recv, along_x(-k))

    def send_half(h):
        num_send[h] = numer[h].astype(BF16)
        for k in far_x:
            send(
                num_send.at[h, pl.ds(k * block, block)],
                num_recv.at[h, k],
                nx_send.at[h],
                nx_recv.at[h],
                along_x(-k),
            )

    send_half(0)

    for c in range(steps):
        here = pl.ds(c * step_keys, step_keys)
        part = dot(probs[:, here], keys[here, half:latent])
        if c + 1 < steps:
            part = scaled(part, jnp.exp2(tops[c + 1] - top))
        numer[1] = part if c == 0 else numer[1] + part

    send_half(1)
    done(q_all.at[pl.ds(block, rows - block)], qx_send)

    done(stat_recv.at[pl.ds(1, NX - 1)], st_recv)
    found = [stat_send[0]] + [stat_recv[k] for k in range(1, NX)]
    factors = [[] for _ in found]
    z_stats = []
    for v in range(NZ):
        tops = [jnp.broadcast_to(f[:, 8 * v : 8 * v + 1], (8, 128)) for f in found]
        top_x = functools.reduce(jnp.maximum, tops)
        coarse = top_x.astype(BF16).astype(F32)
        top_x = coarse + (top_x - coarse).astype(BF16).astype(F32)
        total_x = jnp.zeros((8, 128), F32)
        for f, t, held in zip(found, tops, factors):
            held.append(jnp.exp2(t - top_x))
            total_x = total_x + f[:, 64 + 8 * v : 64 + 8 * v + 1] * held[v]
        z_stats.append(jnp.where(lane < 64, top_x, total_x))
        if v > 0:
            coarse = z_stats[v].astype(BF16).astype(F32)
            low_send[order[v], :, 128:256] = jnp.concatenate(
                [coarse, z_stats[v] - coarse], axis=0
            ).astype(BF16)
    factors = [
        jnp.concatenate([jnp.concatenate(held, axis=0)] * (half // 128), axis=1) for held in factors
    ]

    spans = ((0, 256), (256, 384))
    own_half = []
    for h in range(2):
        done(num_recv.at[h, pl.ds(1, NX - 1)], nx_recv.at[h])
        merged = numer[h, 0:block, :] * factors[0]
        for k in range(1, NX):
            merged = merged + num_recv[h, k].astype(F32) * factors[k]
        own_half.append([merged[0:8, j : j + 128] for j in range(0, half, 128)])
        low, high = spans[h]
        for k in far_z:
            part = merged[order.index(k) * 8 : (order.index(k) + 1) * 8]
            low_send[k, :, low : low + 128] = jnp.concatenate(
                [part[:, 0:128], part[:, 128:256]], axis=0
            ).astype(BF16)
            send(
                low_send.at[k, :, low:high],
                low_recv.at[k, :, low:high],
                nz_send.at[h],
                nz_recv.at[h],
                along_z(-k),
            )
    x_columns = own_columns * NZ
    x_lanes = out_group * NZ
    out_copy.wait()
    place = lax.broadcasted_iota(jnp.int32, (1, x_lanes), 1)
    inside = lax.rem(place, out_group)
    wanted = lax.div(place, out_group) * own_columns + inside
    wanted = jnp.where(inside < own_columns, wanted, -(2**20))
    for i in range(NX):
        low = i * x_columns // 128 * 128
        high = min(-(-(i + 1) * x_columns // 128) * 128, w_out.shape[1])
        column = lax.broadcasted_iota(jnp.int32, (high - low, x_lanes), 0)
        pick = jnp.where(column == wanted + (i * x_columns - low), 1.0, 0.0).astype(BF16)
        w_placed[:, i * x_lanes : (i + 1) * x_lanes] = dot(w_out[:, low:high], pick).astype(BF16)

    done(stat_recv.at[pl.ds(1, NX - 1)], st_send)
    for h in range(2):
        done(num_recv.at[h, pl.ds(1, NX - 1)], nx_send.at[h])

    done(low_recv.at[pl.ds(1, NZ - 1), :, 0:256], nz_recv.at[0])
    found = [z_stats[0]]
    for k in range(1, NZ):
        held = low_recv[k, :, 128:256].astype(F32)
        found.append(held[0:8] + held[8:16])
    tops = [jnp.broadcast_to(f[:, 0:1], (8, 128)) for f in found]
    top_z = functools.reduce(jnp.maximum, tops)
    factors = [jnp.exp2(t - top_z) for t in tops]
    total_z = sum(f[:, 64:65] * w for f, w in zip(found, factors))
    attended = []
    for h in range(2):
        if h == 1:
            done(low_recv.at[pl.ds(1, NZ - 1), :, 256:384], nz_recv.at[1])
        merged = [own * factors[0] for own in own_half[h]]
        for k in range(1, NZ):
            held = low_recv[k, :, spans[h][0] : spans[h][0] + 128].astype(F32)
            for j in range(2):
                merged[j] = merged[j] + held[j * 8 : (j + 1) * 8] * factors[k]
        attended += [m / total_z for m in merged]
    attended = jnp.concatenate(attended, axis=1)
    head = lax.rem(lax.broadcasted_iota(jnp.int32, attended.shape, 0), heads)
    spread = [jnp.where(head == i, attended, 0.0) for i in range(heads)]
    up_copy.wait()
    values = dot(
        jnp.concatenate(spread, axis=1).astype(BF16), w_up[...].reshape(heads * latent, -1)
    )

    own = pl.ds(pl.multiple_of(g * 8, 8), 8)
    head_values[own, :] = values.astype(BF16).astype(F32)
    for k in far_g:
        send(head_values.at[own], head_values.at[own], v_send, v_recv, along_g(k))
    others = head_values.at[pl.ds(0, (NG - 1) * 8)]
    done(low_recv.at[pl.ds(1, NZ - 1), :, 0:256], nz_send.at[0])
    done(low_recv.at[pl.ds(1, NZ - 1), :, 256:384], nz_send.at[1])
    done(others, v_recv)
    wide = [head_values[pl.ds(i, tokens * NG, stride=heads), :] for i in range(heads)]
    terms = dot(jnp.concatenate(wide, axis=1).astype(BF16), w_placed[...])

    for i in range(NX):
        term_send[i] = terms[:, i * x_lanes : (i + 1) * x_lanes].astype(BF16)
    for k in far_x:
        send(term_send.at[lax.rem(x + k, NX)], term_recv.at[k], tx_send, tx_recv, along_x(k))
    done(others, v_send)
    summed = term_send[x].astype(F32)
    done(term_recv.at[pl.ds(1, NX - 1)], tx_recv)
    for k in range(1, NX):
        summed = summed + term_recv[k].astype(F32)
    for i in range(x_lanes // 128):
        last_send[i] = summed[:, i * 128 : (i + 1) * 128].astype(BF16)
    per_tile = 128 // out_group
    for k in far_z:
        send(
            last_send.at[lax.div(lax.rem(z + k, NZ), per_tile)],
            last_recv.at[k],
            tz_send,
            tz_recv,
            along_z(k),
        )
    done(term_recv.at[pl.ds(1, NX - 1)], tx_send)
    final = last_send[lax.div(z, per_tile)].astype(F32)
    done(last_recv.at[pl.ds(1, NZ - 1)], tz_recv)
    for k in range(1, NZ):
        final = final + last_recv[k].astype(F32)
    place = lax.rem(z, per_tile)
    chosen = final
    for i in range(1, per_tile):
        chosen = jnp.where(place == i, pltpu.roll(final, 128 - i * out_group, 1), chosen)
    result[...] = chosen
    done(last_recv.at[pl.ds(1, NZ - 1)], tz_send)


def body(sizes, queries, cache, slot_page, lengths, w_uv, w_out):
    NX, NZ, NG, own_columns = sizes
    tokens, heads, width = queries.shape[1:]
    latent = w_uv.shape[1]
    half = latent // 2
    key_rows = cache.shape[1] * cache.shape[2]
    rows = NX * NZ * 8
    block = NZ * 8
    x_lanes = NZ * out_group
    sem = pltpu.SemaphoreType.DMA
    scratch = [
        pltpu.VMEM(queries.shape, BF16),
        pltpu.VMEM((8, 768), F32),
        pltpu.VMEM((NZ, 16, 384), BF16),
        pltpu.VMEM((rows, 640), BF16),
        pltpu.VMEM((key_rows, width), BF16),
        pltpu.SMEM(slot_page.shape, jnp.int32),
        pltpu.SMEM(lengths.shape, jnp.int32),
        pltpu.VMEM(w_uv.shape, BF16),
        pltpu.VMEM(w_out.shape, BF16),
        pltpu.VMEM((w_out.shape[0], NX * x_lanes), BF16),
        pltpu.VMEM((key_rows, 128), BF16),
        pltpu.VMEM((2, step_keys, rows), F32),
        pltpu.VMEM((rows, key_rows), BF16),
        pltpu.VMEM((2, rows, half), F32),
        pltpu.VMEM((2, rows, half), BF16),
        pltpu.VMEM((2, NX, block, half), BF16),
        pltpu.VMEM((NX, 8, 128), F32),
        pltpu.VMEM((NX, 8, 128), F32),
        pltpu.VMEM((NZ, 16, 384), BF16),
        pltpu.VMEM((NZ, 16, 384), BF16),
        pltpu.VMEM((NG * 8, 128), F32),
        pltpu.VMEM((NX, tokens * NG, x_lanes), BF16),
        pltpu.VMEM((NX, tokens * NG, x_lanes), BF16),
        pltpu.VMEM((x_lanes // 128, tokens * NG, 128), BF16),
        pltpu.VMEM((NZ, tokens * NG, 128), BF16),
        sem((5,)),
        sem((key_rows // step_keys,)),
        sem,
        sem((NZ,)),
        sem,
        sem,
        sem,
        sem,
        sem((2,)),
        sem((2,)),
        sem((2,)),
        sem((2,)),
        sem,
        sem,
        sem,
        sem,
        sem,
        sem,
    ]
    result = pl.pallas_call(
        functools.partial(kernel, sizes),
        out_shape=jax.ShapeDtypeStruct((tokens * NG, 128), F32),
        in_specs=[pl.BlockSpec(memory_space=pltpu.HBM)] * 6,
        out_specs=pl.BlockSpec(memory_space=pltpu.VMEM),
        scratch_shapes=scratch,
        compiler_params=pltpu.CompilerParams(
            collective_id=0, has_side_effects=True, vmem_limit_bytes=56 * 1024 * 1024
        ),
    )(queries, cache.reshape(key_rows, width), slot_page, lengths, w_uv, w_out)
    return result[:, 0:own_columns].astype(BF16).reshape(NG, tokens, own_columns)


def solution(mesh, NX=4):
    NG, pages = mesh.shape["group"], mesh.shape["page"]
    in_specs = (
        P("group", None, "page", None),
        P("group", "page", None, None),
        P("group", "page"),
        P("group"),
        P("page", None, None),
        P("page", "group"),
    )
    out_specs = P(None, None, ("group", "page"))

    def step(queries, cache, slot_page, lengths, w_uv, w_out):
        sizes = (NX, pages // NX, NG, w_out.shape[1] // pages)
        return body(sizes, queries, cache, slot_page, lengths, w_uv, w_out)

    return jax.shard_map(step, mesh=mesh, in_specs=in_specs, out_specs=out_specs, check_vma=False)
```

```python
import functools

import jax
import jax.numpy as jnp
from jax import lax
from jax.experimental import pallas as pl
from jax.experimental.pallas import tpu as pltpu
from jax.sharding import PartitionSpec as P

MESH = pl.DeviceIdType.MESH
F32 = jnp.float32
BF16 = jnp.bfloat16
score_scale = 192.0 ** (-0.5)
log2_e = 1.4426950408889634
masked_fill = -(2.0**99)
lowest_top = -(2.0**20)
out_group = 32
step_keys = 1024
tile_keys = 256


def dot(a, b, contract_b=0):
    return lax.dot_general(a, b, (((1,), (contract_b,)), ((), ())), preferred_element_type=F32)


def kernel(
    sizes,
    q_hbm,
    k_hbm,
    page_hbm,
    length_hbm,
    up_hbm,
    out_hbm,
    result,
    q_in,
    q_rows,
    q_packed,
    q_all,
    keys,
    pages,
    length,
    w_up,
    w_out,
    w_placed,
    tails,
    scores,
    probs,
    tops,
    numer,
    num_send,
    num_recv,
    stat_send,
    stat_recv,
    low_send,
    low_recv,
    head_values,
    term_send,
    term_recv,
    last_send,
    last_recv,
    local_sem,
    key_sem,
    qz_send,
    qz_recv,
    qx_send,
    qx_recv,
    st_send,
    st_recv,
    nx_send,
    nx_recv,
    nz_send,
    nz_recv,
    v_send,
    v_recv,
    tx_send,
    tx_recv,
    tz_send,
    tz_recv,
):
    NX, NZ, NG, own_columns = sizes
    width = q_in.shape[-1]
    latent = w_up.shape[1]
    half = latent // 2
    key_rows = keys.shape[0]
    rows = q_all.shape[0]
    block = rows // NX
    steps = key_rows // step_keys
    tokens, heads = q_in.shape[1], q_in.shape[2]

    g = lax.axis_index("group")
    page = lax.axis_index("page")
    x, z = lax.div(page, NZ), lax.rem(page, NZ)

    def along_x(k):
        return {"page": lax.rem(x + k + NX, NX) * NZ + z}

    def along_z(k):
        return {"page": x * NZ + lax.rem(z + k + NZ, NZ)}

    def along_g(k):
        return {"group": lax.rem(g + k + NG, NG)}

    def send(source, target, send_sem, recv_sem, device):
        copy = pltpu.make_async_remote_copy(
            src_ref=source,
            dst_ref=target,
            send_sem=send_sem,
            recv_sem=recv_sem,
            device_id=device,
            device_id_type=MESH,
        )
        copy.start()
        return copy

    def done(region, sem):
        pltpu.make_async_copy(region, region, sem).wait()

    far_z = sorted(range(1, NZ), key=lambda k: -min(k, NZ - k))
    order = [0] + far_z[::-1]
    far_g = sorted(range(1, NG), key=lambda k: -min(k, NG - k))
    far_x = sorted(range(1, NX), key=lambda k: -min(k, NX - k))

    def local(source, target, sem):
        copy = pltpu.make_async_copy(source, target, sem)
        copy.start()
        return copy

    q_copy = local(q_hbm, q_in, local_sem.at[0])
    barrier = pltpu.get_barrier_semaphore()
    peers = [along_z(k) for k in far_z] + [along_x(k) for k in far_x] + [along_g(k) for k in far_g]
    for peer in peers:
        pl.semaphore_signal(barrier, inc=1, device_id=peer, device_id_type=MESH)
    page_copy = local(page_hbm, pages, local_sem.at[1])
    length_copy = local(length_hbm, length, local_sem.at[2])
    out_copy = local(out_hbm, w_out, local_sem.at[3])
    key_copies = [
        local(
            k_hbm.at[pl.ds(c * step_keys, step_keys)],
            keys.at[pl.ds(c * step_keys, step_keys)],
            key_sem.at[c],
        )
        for c in range(steps)
    ]
    up_copy = local(up_hbm, w_up, local_sem.at[4])

    q_copy.wait()
    place = lax.broadcasted_iota(jnp.int32, (8, 256), 1) + 512
    owner = lax.broadcasted_iota(jnp.int32, (8, 256), 0) // heads
    q_rows[:, 512:768] = jnp.where(place == width + owner, 1.0, 0.0)
    for t in range(tokens):
        q_rows[t * heads : (t + 1) * heads, 0:width] = q_in[0, t].astype(F32)
    q_packed[0] = jnp.concatenate([q_rows[:, 0:384], q_rows[:, 384:768]], axis=0).astype(BF16)
    pl.semaphore_wait(barrier, len(peers))
    for k in far_z:
        send(q_packed.at[0], q_packed.at[k], qz_send, qz_recv.at[k], along_z(k))

    page_copy.wait()
    length_copy.wait()
    lane = lax.broadcasted_iota(jnp.int32, (8, 128), 1)
    spot = lax.broadcasted_iota(jnp.int32, (64, 64), 0)
    token = lax.broadcasted_iota(jnp.int32, (64, 64), 1)
    last = jnp.where(token < tokens, length[0] - tokens + token - spot, 2**30)

    for c, copy in enumerate(key_copies):
        copy.wait()

        @pl.loop(c * step_keys // 64, (c + 1) * step_keys // 64, unroll=8)
        def _(i):
            at = pl.ds(pl.multiple_of(i * 64, 64), 64)
            mask = jnp.where(pages[0, i] * 64 <= last, 0.0, masked_fill).astype(BF16)
            tails[at, :] = jnp.concatenate([keys[at, latent:width], mask], axis=1)

    for n in range(0, NZ, 2):
        pair = []
        for j in order[n : n + 2]:
            if j > 0:
                done(q_packed.at[j], qz_recv.at[j])
            part = q_packed[j].astype(F32)
            pair.append(jnp.concatenate([part[0:8], part[8:16, 0:256]], axis=1))
        q_all[n * 8 : n * 8 + 16, :] = jnp.concatenate(pair, axis=0).astype(BF16)
        for k in far_x:
            send(
                q_all.at[pl.ds(n * 8, 16)],
                q_all.at[pl.ds(k * block + n * 8, 16)],
                qx_send,
                qx_recv,
                along_x(k),
            )
    done(q_packed.at[pl.ds(1, NZ - 1)], qz_send)

    done(q_all.at[pl.ds(block, rows - block)], qx_recv)

    def columns(value, width):
        return jnp.concatenate([value] * (width // 128), axis=1)

    def score_tile(c, n):
        at = pl.ds(c * step_keys + n * tile_keys, tile_keys)
        wide = jnp.concatenate([keys[at, 0:latent], tails[at, :]], axis=1)
        s = dot(q_all[...], wide, 1) * (score_scale * log2_e)
        scores[c % 2, :, n * tile_keys : (n + 1) * tile_keys] = s
        return functools.reduce(
            jnp.maximum, [s[:, j : j + 128] for j in range(0, tile_keys, 128)]
        )

    tiles = step_keys // tile_keys
    largest = functools.reduce(jnp.maximum, [score_tile(0, n) for n in range(tiles)])
    total = jnp.zeros((rows, 128), F32)
    for c in range(steps):
        top = jnp.broadcast_to(jnp.max(largest, axis=1, keepdims=True), (rows, 128))
        if c == 0:
            tops[c] = jnp.maximum(top, lowest_top)
        else:
            tops[c] = jnp.maximum(top, tops[c - 1])
            shrink = jnp.exp2(tops[c - 1] - tops[c])
            total = total * shrink
        found, pieces = [], []
        for n in range(tiles):
            if c + 1 < steps:
                found.append(score_tile(c + 1, n))
            for low in range(n * tile_keys, (n + 1) * tile_keys, 128):
                p = jnp.exp2(scores[c % 2, :, low : low + 128] - tops[c])
                total = total + p
                p = p.astype(BF16)
                probs[:, c * step_keys + low : c * step_keys + low + 128] = p
                pieces.append(p)
        if found:
            largest = functools.reduce(jnp.maximum, found)
        part = dot(jnp.concatenate(pieces, axis=1), keys[pl.ds(c * step_keys, step_keys), 0:half])
        numer[0] = part if c == 0 else numer[0] * columns(shrink, half) + part

    top_column = tops[steps - 1]
    sum_column = jnp.broadcast_to(jnp.sum(total, axis=1, keepdims=True), (rows, 128))
    owner = lax.div(lax.broadcasted_iota(jnp.int32, (8, 128), 1), 8)
    for i in range(NX):
        tile = jnp.zeros((8, 128), F32)
        for v in range(NZ):
            first = i * block + v * 8
            tile = jnp.where(owner == v, top_column[first : first + 8], tile)
            tile = jnp.where(owner == v + 8, sum_column[first : first + 8], tile)
        stat_send[i] = tile
    for k in far_x:
        send(stat_send.at[k], stat_recv.at[k], st_send, st_recv, along_x(-k))

    def send_half(h):
        num_send[h] = numer[h].astype(BF16)
        for k in far_x:
            send(
                num_send.at[h, pl.ds(k * block, block)],
                num_recv.at[h, k],
                nx_send.at[h],
                nx_recv.at[h],
                along_x(-k),
            )

    send_half(0)

    for c in range(steps):
        here = pl.ds(c * step_keys, step_keys)
        part = dot(probs[:, here], keys[here, half:latent])
        if c + 1 < steps:
            part = part * columns(jnp.exp2(tops[c] - tops[steps - 1]), half)
        numer[1] = part if c == 0 else numer[1] + part

    send_half(1)
    done(q_all.at[pl.ds(block, rows - block)], qx_send)

    done(stat_recv.at[pl.ds(1, NX - 1)], st_recv)
    found = [stat_send[0]] + [stat_recv[k] for k in range(1, NX)]
    factors = [[] for _ in found]
    z_stats = []
    for v in range(NZ):
        peaks = [jnp.broadcast_to(f[:, 8 * v : 8 * v + 1], (8, 128)) for f in found]
        top_x = functools.reduce(jnp.maximum, peaks)
        coarse = top_x.astype(BF16).astype(F32)
        top_x = coarse + (top_x - coarse).astype(BF16).astype(F32)
        total_x = jnp.zeros((8, 128), F32)
        for f, t, held in zip(found, peaks, factors):
            held.append(jnp.exp2(t - top_x))
            total_x = total_x + f[:, 64 + 8 * v : 64 + 8 * v + 1] * held[v]
        z_stats.append(jnp.where(lane < 64, top_x, total_x))
        if v > 0:
            coarse = z_stats[v].astype(BF16).astype(F32)
            low_send[order[v], :, 128:256] = jnp.concatenate(
                [coarse, z_stats[v] - coarse], axis=0
            ).astype(BF16)
    factors = [
        jnp.concatenate([jnp.concatenate(held, axis=0)] * (half // 128), axis=1) for held in factors
    ]

    spans = ((0, 256), (256, 384))
    own_half = []
    for h in range(2):
        done(num_recv.at[h, pl.ds(1, NX - 1)], nx_recv.at[h])
        merged = numer[h, 0:block, :] * factors[0]
        for k in range(1, NX):
            merged = merged + num_recv[h, k].astype(F32) * factors[k]
        own_half.append([merged[0:8, j : j + 128] for j in range(0, half, 128)])
        low, high = spans[h]
        for k in far_z:
            part = merged[order.index(k) * 8 : (order.index(k) + 1) * 8]
            low_send[k, :, low : low + 128] = jnp.concatenate(
                [part[:, 0:128], part[:, 128:256]], axis=0
            ).astype(BF16)
            send(
                low_send.at[k, :, low:high],
                low_recv.at[k, :, low:high],
                nz_send.at[h],
                nz_recv.at[h],
                along_z(-k),
            )
    x_columns = own_columns * NZ
    x_lanes = out_group * NZ
    out_copy.wait()
    place = lax.broadcasted_iota(jnp.int32, (1, x_lanes), 1)
    inside = lax.rem(place, out_group)
    wanted = lax.div(place, out_group) * own_columns + inside
    wanted = jnp.where(inside < own_columns, wanted, -(2**20))
    for i in range(NX):
        low = i * x_columns // 128 * 128
        high = min(-(-(i + 1) * x_columns // 128) * 128, w_out.shape[1])
        column = lax.broadcasted_iota(jnp.int32, (high - low, x_lanes), 0)
        pick = jnp.where(column == wanted + (i * x_columns - low), 1.0, 0.0).astype(BF16)
        w_placed[:, i * x_lanes : (i + 1) * x_lanes] = dot(w_out[:, low:high], pick).astype(BF16)

    done(stat_recv.at[pl.ds(1, NX - 1)], st_send)
    for h in range(2):
        done(num_recv.at[h, pl.ds(1, NX - 1)], nx_send.at[h])

    done(low_recv.at[pl.ds(1, NZ - 1), :, 0:256], nz_recv.at[0])
    found = [z_stats[0]]
    for k in range(1, NZ):
        held = low_recv[k, :, 128:256].astype(F32)
        found.append(held[0:8] + held[8:16])
    peaks = [jnp.broadcast_to(f[:, 0:1], (8, 128)) for f in found]
    top_z = functools.reduce(jnp.maximum, peaks)
    factors = [jnp.exp2(t - top_z) for t in peaks]
    total_z = sum(f[:, 64:65] * w for f, w in zip(found, factors))
    attended = []
    for h in range(2):
        if h == 1:
            done(low_recv.at[pl.ds(1, NZ - 1), :, 256:384], nz_recv.at[1])
        merged = [own * factors[0] for own in own_half[h]]
        for k in range(1, NZ):
            held = low_recv[k, :, spans[h][0] : spans[h][0] + 128].astype(F32)
            for j in range(2):
                merged[j] = merged[j] + held[j * 8 : (j + 1) * 8] * factors[k]
        attended += [m / total_z for m in merged]
    attended = jnp.concatenate(attended, axis=1)
    head = lax.rem(lax.broadcasted_iota(jnp.int32, attended.shape, 0), heads)
    spread = [jnp.where(head == i, attended, 0.0) for i in range(heads)]
    up_copy.wait()
    values = dot(
        jnp.concatenate(spread, axis=1).astype(BF16), w_up[...].reshape(heads * latent, -1)
    )

    own = pl.ds(pl.multiple_of(g * 8, 8), 8)
    head_values[own, :] = values.astype(BF16).astype(F32)
    for k in far_g:
        send(head_values.at[own], head_values.at[own], v_send, v_recv, along_g(k))
    others = head_values.at[pl.ds(0, (NG - 1) * 8)]
    done(low_recv.at[pl.ds(1, NZ - 1), :, 0:256], nz_send.at[0])
    done(low_recv.at[pl.ds(1, NZ - 1), :, 256:384], nz_send.at[1])
    done(others, v_recv)
    wide = [head_values[pl.ds(i, tokens * NG, stride=heads), :] for i in range(heads)]
    terms = dot(jnp.concatenate(wide, axis=1).astype(BF16), w_placed[...])

    for i in range(NX):
        term_send[i] = terms[:, i * x_lanes : (i + 1) * x_lanes].astype(BF16)
    for k in far_x:
        send(term_send.at[lax.rem(x + k, NX)], term_recv.at[k], tx_send, tx_recv, along_x(k))
    done(others, v_send)
    summed = term_send[x].astype(F32)
    done(term_recv.at[pl.ds(1, NX - 1)], tx_recv)
    for k in range(1, NX):
        summed = summed + term_recv[k].astype(F32)
    for i in range(x_lanes // 128):
        last_send[i] = summed[:, i * 128 : (i + 1) * 128].astype(BF16)
    per_tile = 128 // out_group
    for k in far_z:
        send(
            last_send.at[lax.div(lax.rem(z + k, NZ), per_tile)],
            last_recv.at[k],
            tz_send,
            tz_recv,
            along_z(k),
        )
    done(term_recv.at[pl.ds(1, NX - 1)], tx_send)
    final = last_send[lax.div(z, per_tile)].astype(F32)
    done(last_recv.at[pl.ds(1, NZ - 1)], tz_recv)
    for k in range(1, NZ):
        final = final + last_recv[k].astype(F32)
    place = lax.rem(z, per_tile)
    chosen = final
    for i in range(1, per_tile):
        chosen = jnp.where(place == i, pltpu.roll(final, 128 - i * out_group, 1), chosen)
    result[...] = chosen
    done(last_recv.at[pl.ds(1, NZ - 1)], tz_send)


def body(sizes, queries, cache, slot_page, lengths, w_uv, w_out):
    NX, NZ, NG, own_columns = sizes
    tokens, heads, width = queries.shape[1:]
    latent = w_uv.shape[1]
    half = latent // 2
    key_rows = cache.shape[1] * cache.shape[2]
    rows = NX * NZ * 8
    block = NZ * 8
    x_lanes = NZ * out_group
    sem = pltpu.SemaphoreType.DMA
    scratch = [
        pltpu.VMEM(queries.shape, BF16),
        pltpu.VMEM((8, 768), F32),
        pltpu.VMEM((NZ, 16, 384), BF16),
        pltpu.VMEM((rows, 640), BF16),
        pltpu.VMEM((key_rows, width), BF16),
        pltpu.SMEM(slot_page.shape, jnp.int32),
        pltpu.SMEM(lengths.shape, jnp.int32),
        pltpu.VMEM(w_uv.shape, BF16),
        pltpu.VMEM(w_out.shape, BF16),
        pltpu.VMEM((w_out.shape[0], NX * x_lanes), BF16),
        pltpu.VMEM((key_rows, 128), BF16),
        pltpu.VMEM((2, rows, step_keys), F32),
        pltpu.VMEM((rows, key_rows), BF16),
        pltpu.VMEM((key_rows // step_keys, rows, 128), F32),
        pltpu.VMEM((2, rows, half), F32),
        pltpu.VMEM((2, rows, half), BF16),
        pltpu.VMEM((2, NX, block, half), BF16),
        pltpu.VMEM((NX, 8, 128), F32),
        pltpu.VMEM((NX, 8, 128), F32),
        pltpu.VMEM((NZ, 16, 384), BF16),
        pltpu.VMEM((NZ, 16, 384), BF16),
        pltpu.VMEM((NG * 8, 128), F32),
        pltpu.VMEM((NX, tokens * NG, x_lanes), BF16),
        pltpu.VMEM((NX, tokens * NG, x_lanes), BF16),
        pltpu.VMEM((x_lanes // 128, tokens * NG, 128), BF16),
        pltpu.VMEM((NZ, tokens * NG, 128), BF16),
        sem((5,)),
        sem((key_rows // step_keys,)),
        sem,
        sem((NZ,)),
        sem,
        sem,
        sem,
        sem,
        sem((2,)),
        sem((2,)),
        sem((2,)),
        sem((2,)),
        sem,
        sem,
        sem,
        sem,
        sem,
        sem,
    ]
    result = pl.pallas_call(
        functools.partial(kernel, sizes),
        out_shape=jax.ShapeDtypeStruct((tokens * NG, 128), F32),
        in_specs=[pl.BlockSpec(memory_space=pltpu.HBM)] * 6,
        out_specs=pl.BlockSpec(memory_space=pltpu.VMEM),
        scratch_shapes=scratch,
        compiler_params=pltpu.CompilerParams(
            collective_id=0, has_side_effects=True, vmem_limit_bytes=56 * 1024 * 1024
        ),
    )(queries, cache.reshape(key_rows, width), slot_page, lengths, w_uv, w_out)
    return result[:, 0:own_columns].astype(BF16).reshape(NG, tokens, own_columns)


def solution(mesh, NX=4):
    NG, pages = mesh.shape["group"], mesh.shape["page"]
    in_specs = (
        P("group", None, "page", None),
        P("group", "page", None, None),
        P("group", "page"),
        P("group"),
        P("page", None, None),
        P("page", "group"),
    )
    out_specs = P(None, None, ("group", "page"))

    def step(queries, cache, slot_page, lengths, w_uv, w_out):
        sizes = (NX, pages // NX, NG, w_out.shape[1] // pages)
        return body(sizes, queries, cache, slot_page, lengths, w_uv, w_out)

    return jax.shard_map(step, mesh=mesh, in_specs=in_specs, out_specs=out_specs, check_vma=False)
```

```python
import functools

import jax
import jax.numpy as jnp
from jax import lax
from jax.experimental import pallas as pl
from jax.experimental.pallas import tpu as pltpu
from jax.sharding import PartitionSpec as P

MESH = pl.DeviceIdType.MESH
F32 = jnp.float32
BF16 = jnp.bfloat16
score_scale = 192.0 ** (-0.5)
log2_e = 1.4426950408889634
masked_fill = -(2.0**99)
lowest_top = -(2.0**20)
out_group = 32
step_keys = 512
tile_keys = 256


def dot(a, b, contract_b=0):
    return lax.dot_general(a, b, (((1,), (contract_b,)), ((), ())), preferred_element_type=F32)


def kernel(
    sizes,
    q_hbm,
    k_hbm,
    page_hbm,
    length_hbm,
    up_hbm,
    out_hbm,
    result,
    q_in,
    q_rows,
    q_packed,
    q_all,
    keys,
    pages,
    length,
    w_up,
    w_out,
    w_placed,
    tails,
    scores,
    probs,
    tops,
    numer,
    num_send,
    num_recv,
    stat_send,
    stat_recv,
    low_send,
    low_recv,
    head_values,
    term_send,
    term_recv,
    last_send,
    last_recv,
    local_sem,
    key_sem,
    qz_send,
    qz_recv,
    qx_send,
    qx_recv,
    st_send,
    st_recv,
    nx_send,
    nx_recv,
    nz_send,
    nz_recv,
    v_send,
    v_recv,
    tx_send,
    tx_recv,
    tz_send,
    tz_recv,
):
    NX, NZ, NG, own_columns = sizes
    width = q_in.shape[-1]
    latent = w_up.shape[1]
    half = latent // 2
    key_rows = keys.shape[0]
    rows = q_all.shape[0]
    block = rows // NX
    steps = key_rows // step_keys
    tokens, heads = q_in.shape[1], q_in.shape[2]

    g = lax.axis_index("group")
    page = lax.axis_index("page")
    x, z = lax.div(page, NZ), lax.rem(page, NZ)

    def along_x(k):
        return {"page": lax.rem(x + k + NX, NX) * NZ + z}

    def along_z(k):
        return {"page": x * NZ + lax.rem(z + k + NZ, NZ)}

    def along_g(k):
        return {"group": lax.rem(g + k + NG, NG)}

    def send(source, target, send_sem, recv_sem, device):
        copy = pltpu.make_async_remote_copy(
            src_ref=source,
            dst_ref=target,
            send_sem=send_sem,
            recv_sem=recv_sem,
            device_id=device,
            device_id_type=MESH,
        )
        copy.start()
        return copy

    def done(region, sem):
        pltpu.make_async_copy(region, region, sem).wait()

    far_z = sorted(range(1, NZ), key=lambda k: -min(k, NZ - k))
    order = [0] + far_z[::-1]
    far_g = sorted(range(1, NG), key=lambda k: -min(k, NG - k))
    far_x = sorted(range(1, NX), key=lambda k: -min(k, NX - k))

    def local(source, target, sem):
        copy = pltpu.make_async_copy(source, target, sem)
        copy.start()
        return copy

    q_copy = local(q_hbm, q_in, local_sem.at[0])
    barrier = pltpu.get_barrier_semaphore()
    peers = [along_z(k) for k in far_z] + [along_x(k) for k in far_x] + [along_g(k) for k in far_g]
    for peer in peers:
        pl.semaphore_signal(barrier, inc=1, device_id=peer, device_id_type=MESH)
    page_copy = local(page_hbm, pages, local_sem.at[1])
    length_copy = local(length_hbm, length, local_sem.at[2])
    out_copy = local(out_hbm, w_out, local_sem.at[3])
    key_copies = [
        local(
            k_hbm.at[pl.ds(c * step_keys, step_keys)],
            keys.at[pl.ds(c * step_keys, step_keys)],
            key_sem.at[c],
        )
        for c in range(steps)
    ]
    up_copy = local(up_hbm, w_up, local_sem.at[4])

    q_copy.wait()
    place = lax.broadcasted_iota(jnp.int32, (8, 256), 1) + 512
    owner = lax.broadcasted_iota(jnp.int32, (8, 256), 0) // heads
    q_rows[:, 512:768] = jnp.where(place == width + owner, 1.0, 0.0)
    for t in range(tokens):
        q_rows[t * heads : (t + 1) * heads, 0:width] = q_in[0, t].astype(F32)
    q_packed[0] = jnp.concatenate([q_rows[:, 0:384], q_rows[:, 384:768]], axis=0).astype(BF16)
    pl.semaphore_wait(barrier, len(peers))
    for k in far_z:
        send(q_packed.at[0], q_packed.at[k], qz_send, qz_recv.at[k], along_z(k))

    page_copy.wait()
    length_copy.wait()
    lane = lax.broadcasted_iota(jnp.int32, (8, 128), 1)
    spot = lax.broadcasted_iota(jnp.int32, (64, 64), 0)
    token = lax.broadcasted_iota(jnp.int32, (64, 64), 1)
    last = jnp.where(token < tokens, length[0] - tokens + token - spot, 2**30)

    for c, copy in enumerate(key_copies):
        copy.wait()

        @pl.loop(c * step_keys // 64, (c + 1) * step_keys // 64, unroll=8)
        def _(i):
            at = pl.ds(pl.multiple_of(i * 64, 64), 64)
            mask = jnp.where(pages[0, i] * 64 <= last, 0.0, masked_fill).astype(BF16)
            tails[at, :] = jnp.concatenate([keys[at, latent:width], mask], axis=1)

    for n in range(0, NZ, 2):
        pair = []
        for j in order[n : n + 2]:
            if j > 0:
                done(q_packed.at[j], qz_recv.at[j])
            part = q_packed[j].astype(F32)
            pair.append(jnp.concatenate([part[0:8], part[8:16, 0:256]], axis=1))
        q_all[n * 8 : n * 8 + 16, :] = jnp.concatenate(pair, axis=0).astype(BF16)
        for k in far_x:
            send(
                q_all.at[pl.ds(n * 8, 16)],
                q_all.at[pl.ds(k * block + n * 8, 16)],
                qx_send,
                qx_recv,
                along_x(k),
            )
    done(q_packed.at[pl.ds(1, NZ - 1)], qz_send)

    done(q_all.at[pl.ds(block, rows - block)], qx_recv)

    def columns(value, width):
        return jnp.concatenate([value] * (width // 128), axis=1)

    def score_tile(c, n):
        at = pl.ds(c * step_keys + n * tile_keys, tile_keys)
        wide = jnp.concatenate([keys[at, 0:latent], tails[at, :]], axis=1)
        s = dot(q_all[...], wide, 1) * (score_scale * log2_e)
        scores[c % 2, :, n * tile_keys : (n + 1) * tile_keys] = s
        return functools.reduce(
            jnp.maximum, [s[:, j : j + 128] for j in range(0, tile_keys, 128)]
        )

    tiles = step_keys // tile_keys
    largest = functools.reduce(jnp.maximum, [score_tile(0, n) for n in range(tiles)])
    total = jnp.zeros((rows, 128), F32)
    for c in range(steps):
        top = jnp.broadcast_to(jnp.max(largest, axis=1, keepdims=True), (rows, 128))
        if c == 0:
            tops[c] = jnp.maximum(top, lowest_top)
        else:
            tops[c] = jnp.maximum(top, tops[c - 1])
            shrink = jnp.exp2(tops[c - 1] - tops[c])
            total = total * shrink
        found, pieces = [], []
        for n in range(tiles):
            if c + 1 < steps:
                found.append(score_tile(c + 1, n))
            for low in range(n * tile_keys, (n + 1) * tile_keys, 128):
                p = jnp.exp2((scores[c % 2, :, low : low + 128] - tops[c]).astype(BF16))
                total = total + p.astype(F32)
                probs[:, c * step_keys + low : c * step_keys + low + 128] = p
                pieces.append(p)
        if found:
            largest = functools.reduce(jnp.maximum, found)
        part = dot(jnp.concatenate(pieces, axis=1), keys[pl.ds(c * step_keys, step_keys), 0:half])
        numer[0] = part if c == 0 else numer[0] * columns(shrink, half) + part

    top_column = tops[steps - 1]
    sum_column = jnp.broadcast_to(jnp.sum(total, axis=1, keepdims=True), (rows, 128))
    owner = lax.div(lax.broadcasted_iota(jnp.int32, (8, 128), 1), 8)
    for i in range(NX):
        tile = jnp.zeros((8, 128), F32)
        for v in range(NZ):
            first = i * block + v * 8
            tile = jnp.where(owner == v, top_column[first : first + 8], tile)
            tile = jnp.where(owner == v + 8, sum_column[first : first + 8], tile)
        stat_send[i] = tile
    for k in far_x:
        send(stat_send.at[k], stat_recv.at[k], st_send, st_recv, along_x(-k))

    def send_half(h):
        num_send[h] = numer[h].astype(BF16)
        for k in far_x:
            send(
                num_send.at[h, pl.ds(k * block, block)],
                num_recv.at[h, k],
                nx_send.at[h],
                nx_recv.at[h],
                along_x(-k),
            )

    send_half(0)

    for c in range(steps):
        here = pl.ds(c * step_keys, step_keys)
        part = dot(probs[:, here], keys[here, half:latent])
        if c + 1 < steps:
            part = part * columns(jnp.exp2(tops[c] - tops[steps - 1]), half)
        numer[1] = part if c == 0 else numer[1] + part

    send_half(1)
    done(q_all.at[pl.ds(block, rows - block)], qx_send)

    done(stat_recv.at[pl.ds(1, NX - 1)], st_recv)
    found = [stat_send[0]] + [stat_recv[k] for k in range(1, NX)]
    factors = [[] for _ in found]
    z_stats = []
    for v in range(NZ):
        peaks = [jnp.broadcast_to(f[:, 8 * v : 8 * v + 1], (8, 128)) for f in found]
        top_x = functools.reduce(jnp.maximum, peaks)
        coarse = top_x.astype(BF16).astype(F32)
        top_x = coarse + (top_x - coarse).astype(BF16).astype(F32)
        total_x = jnp.zeros((8, 128), F32)
        for f, t, held in zip(found, peaks, factors):
            held.append(jnp.exp2(t - top_x))
            total_x = total_x + f[:, 64 + 8 * v : 64 + 8 * v + 1] * held[v]
        z_stats.append(jnp.where(lane < 64, top_x, total_x))
        if v > 0:
            coarse = z_stats[v].astype(BF16).astype(F32)
            low_send[order[v], :, 128:256] = jnp.concatenate(
                [coarse, z_stats[v] - coarse], axis=0
            ).astype(BF16)
    factors = [
        jnp.concatenate([jnp.concatenate(held, axis=0)] * (half // 128), axis=1) for held in factors
    ]

    spans = ((0, 256), (256, 384))
    own_half = []
    for h in range(2):
        done(num_recv.at[h, pl.ds(1, NX - 1)], nx_recv.at[h])
        merged = numer[h, 0:block, :] * factors[0]
        for k in range(1, NX):
            merged = merged + num_recv[h, k].astype(F32) * factors[k]
        own_half.append([merged[0:8, j : j + 128] for j in range(0, half, 128)])
        low, high = spans[h]
        for k in far_z:
            part = merged[order.index(k) * 8 : (order.index(k) + 1) * 8]
            low_send[k, :, low : low + 128] = jnp.concatenate(
                [part[:, 0:128], part[:, 128:256]], axis=0
            ).astype(BF16)
            send(
                low_send.at[k, :, low:high],
                low_recv.at[k, :, low:high],
                nz_send.at[h],
                nz_recv.at[h],
                along_z(-k),
            )
    x_columns = own_columns * NZ
    x_lanes = out_group * NZ
    out_copy.wait()
    place = lax.broadcasted_iota(jnp.int32, (1, x_lanes), 1)
    inside = lax.rem(place, out_group)
    wanted = lax.div(place, out_group) * own_columns + inside
    wanted = jnp.where(inside < own_columns, wanted, -(2**20))
    for i in range(NX):
        low = i * x_columns // 128 * 128
        high = min(-(-(i + 1) * x_columns // 128) * 128, w_out.shape[1])
        column = lax.broadcasted_iota(jnp.int32, (high - low, x_lanes), 0)
        pick = jnp.where(column == wanted + (i * x_columns - low), 1.0, 0.0).astype(BF16)
        w_placed[:, i * x_lanes : (i + 1) * x_lanes] = dot(w_out[:, low:high], pick).astype(BF16)

    done(stat_recv.at[pl.ds(1, NX - 1)], st_send)
    for h in range(2):
        done(num_recv.at[h, pl.ds(1, NX - 1)], nx_send.at[h])

    done(low_recv.at[pl.ds(1, NZ - 1), :, 0:256], nz_recv.at[0])
    found = [z_stats[0]]
    for k in range(1, NZ):
        held = low_recv[k, :, 128:256].astype(F32)
        found.append(held[0:8] + held[8:16])
    peaks = [jnp.broadcast_to(f[:, 0:1], (8, 128)) for f in found]
    top_z = functools.reduce(jnp.maximum, peaks)
    factors = [jnp.exp2(t - top_z) for t in peaks]
    total_z = sum(f[:, 64:65] * w for f, w in zip(found, factors))
    attended = []
    for h in range(2):
        if h == 1:
            done(low_recv.at[pl.ds(1, NZ - 1), :, 256:384], nz_recv.at[1])
        merged = [own * factors[0] for own in own_half[h]]
        for k in range(1, NZ):
            held = low_recv[k, :, spans[h][0] : spans[h][0] + 128].astype(F32)
            for j in range(2):
                merged[j] = merged[j] + held[j * 8 : (j + 1) * 8] * factors[k]
        attended += [m / total_z for m in merged]
    attended = jnp.concatenate(attended, axis=1)
    head = lax.rem(lax.broadcasted_iota(jnp.int32, attended.shape, 0), heads)
    spread = [jnp.where(head == i, attended, 0.0) for i in range(heads)]
    up_copy.wait()
    values = dot(
        jnp.concatenate(spread, axis=1).astype(BF16), w_up[...].reshape(heads * latent, -1)
    )

    own = pl.ds(pl.multiple_of(g * 8, 8), 8)
    head_values[own, :] = values.astype(BF16).astype(F32)
    for k in far_g:
        send(head_values.at[own], head_values.at[own], v_send, v_recv, along_g(k))
    others = head_values.at[pl.ds(0, (NG - 1) * 8)]
    done(low_recv.at[pl.ds(1, NZ - 1), :, 0:256], nz_send.at[0])
    done(low_recv.at[pl.ds(1, NZ - 1), :, 256:384], nz_send.at[1])
    done(others, v_recv)
    wide = [head_values[pl.ds(i, tokens * NG, stride=heads), :] for i in range(heads)]
    terms = dot(jnp.concatenate(wide, axis=1).astype(BF16), w_placed[...])

    for i in range(NX):
        term_send[i] = terms[:, i * x_lanes : (i + 1) * x_lanes].astype(BF16)
    for k in far_x:
        send(term_send.at[lax.rem(x + k, NX)], term_recv.at[k], tx_send, tx_recv, along_x(k))
    done(others, v_send)
    summed = term_send[x].astype(F32)
    done(term_recv.at[pl.ds(1, NX - 1)], tx_recv)
    for k in range(1, NX):
        summed = summed + term_recv[k].astype(F32)
    for i in range(x_lanes // 128):
        last_send[i] = summed[:, i * 128 : (i + 1) * 128].astype(BF16)
    per_tile = 128 // out_group
    for k in far_z:
        send(
            last_send.at[lax.div(lax.rem(z + k, NZ), per_tile)],
            last_recv.at[k],
            tz_send,
            tz_recv,
            along_z(k),
        )
    done(term_recv.at[pl.ds(1, NX - 1)], tx_send)
    final = last_send[lax.div(z, per_tile)].astype(F32)
    done(last_recv.at[pl.ds(1, NZ - 1)], tz_recv)
    for k in range(1, NZ):
        final = final + last_recv[k].astype(F32)
    place = lax.rem(z, per_tile)
    chosen = final
    for i in range(1, per_tile):
        chosen = jnp.where(place == i, pltpu.roll(final, 128 - i * out_group, 1), chosen)
    result[...] = chosen
    done(last_recv.at[pl.ds(1, NZ - 1)], tz_send)


def body(sizes, queries, cache, slot_page, lengths, w_uv, w_out):
    NX, NZ, NG, own_columns = sizes
    tokens, heads, width = queries.shape[1:]
    latent = w_uv.shape[1]
    half = latent // 2
    key_rows = cache.shape[1] * cache.shape[2]
    rows = NX * NZ * 8
    block = NZ * 8
    x_lanes = NZ * out_group
    sem = pltpu.SemaphoreType.DMA
    scratch = [
        pltpu.VMEM(queries.shape, BF16),
        pltpu.VMEM((8, 768), F32),
        pltpu.VMEM((NZ, 16, 384), BF16),
        pltpu.VMEM((rows, 640), BF16),
        pltpu.VMEM((key_rows, width), BF16),
        pltpu.SMEM(slot_page.shape, jnp.int32),
        pltpu.SMEM(lengths.shape, jnp.int32),
        pltpu.VMEM(w_uv.shape, BF16),
        pltpu.VMEM(w_out.shape, BF16),
        pltpu.VMEM((w_out.shape[0], NX * x_lanes), BF16),
        pltpu.VMEM((key_rows, 128), BF16),
        pltpu.VMEM((2, rows, step_keys), F32),
        pltpu.VMEM((rows, key_rows), BF16),
        pltpu.VMEM((key_rows // step_keys, rows, 128), F32),
        pltpu.VMEM((2, rows, half), F32),
        pltpu.VMEM((2, rows, half), BF16),
        pltpu.VMEM((2, NX, block, half), BF16),
        pltpu.VMEM((NX, 8, 128), F32),
        pltpu.VMEM((NX, 8, 128), F32),
        pltpu.VMEM((NZ, 16, 384), BF16),
        pltpu.VMEM((NZ, 16, 384), BF16),
        pltpu.VMEM((NG * 8, 128), F32),
        pltpu.VMEM((NX, tokens * NG, x_lanes), BF16),
        pltpu.VMEM((NX, tokens * NG, x_lanes), BF16),
        pltpu.VMEM((x_lanes // 128, tokens * NG, 128), BF16),
        pltpu.VMEM((NZ, tokens * NG, 128), BF16),
        sem((5,)),
        sem((key_rows // step_keys,)),
        sem,
        sem((NZ,)),
        sem,
        sem,
        sem,
        sem,
        sem((2,)),
        sem((2,)),
        sem((2,)),
        sem((2,)),
        sem,
        sem,
        sem,
        sem,
        sem,
        sem,
    ]
    result = pl.pallas_call(
        functools.partial(kernel, sizes),
        out_shape=jax.ShapeDtypeStruct((tokens * NG, 128), F32),
        in_specs=[pl.BlockSpec(memory_space=pltpu.HBM)] * 6,
        out_specs=pl.BlockSpec(memory_space=pltpu.VMEM),
        scratch_shapes=scratch,
        compiler_params=pltpu.CompilerParams(
            collective_id=0, has_side_effects=True, vmem_limit_bytes=56 * 1024 * 1024
        ),
    )(queries, cache.reshape(key_rows, width), slot_page, lengths, w_uv, w_out)
    return result[:, 0:own_columns].astype(BF16).reshape(NG, tokens, own_columns)


def solution(mesh, NX=4):
    NG, pages = mesh.shape["group"], mesh.shape["page"]
    in_specs = (
        P("group", None, "page", None),
        P("group", "page", None, None),
        P("group", "page"),
        P("group"),
        P("page", None, None),
        P("page", "group"),
    )
    out_specs = P(None, None, ("group", "page"))

    def step(queries, cache, slot_page, lengths, w_uv, w_out):
        sizes = (NX, pages // NX, NG, w_out.shape[1] // pages)
        return body(sizes, queries, cache, slot_page, lengths, w_uv, w_out)

    return jax.shard_map(step, mesh=mesh, in_specs=in_specs, out_specs=out_specs, check_vma=False)
```

```python
import functools

import jax
import jax.numpy as jnp
from jax import lax
from jax.experimental import pallas as pl
from jax.experimental.pallas import tpu as pltpu
from jax.sharding import PartitionSpec as P

MESH = pl.DeviceIdType.MESH
F32 = jnp.float32
BF16 = jnp.bfloat16
score_scale = 192.0 ** (-0.5)
log2_e = 1.4426950408889634
masked_fill = -(2.0**99)
lowest_top = -(2.0**20)
out_group = 32
step_keys = 512
tile_keys = 256


def dot(a, b, contract_b=0):
    return lax.dot_general(a, b, (((1,), (contract_b,)), ((), ())), preferred_element_type=F32)


def kernel(
    sizes,
    q_hbm,
    k_hbm,
    page_hbm,
    length_hbm,
    up_hbm,
    out_hbm,
    result,
    q_in,
    q_rows,
    q_packed,
    q_all,
    keys,
    pages,
    length,
    w_up,
    w_out,
    w_placed,
    tails,
    scores,
    probs,
    tops,
    numer,
    num_send,
    num_recv,
    stat_send,
    stat_recv,
    low_send,
    low_recv,
    head_values,
    term_send,
    term_recv,
    last_send,
    last_recv,
    local_sem,
    key_sem,
    qz_send,
    qz_recv,
    qx_send,
    qx_recv,
    st_send,
    st_recv,
    nx_send,
    nx_recv,
    nz_send,
    nz_recv,
    v_send,
    v_recv,
    tx_send,
    tx_recv,
    tz_send,
    tz_recv,
):
    NX, NZ, NG, own_columns = sizes
    width = q_in.shape[-1]
    latent = w_up.shape[1]
    half = latent // 2
    key_rows = keys.shape[0]
    rows = q_all.shape[0]
    block = rows // NX
    steps = key_rows // step_keys
    tokens, heads = q_in.shape[1], q_in.shape[2]

    g = lax.axis_index("group")
    page = lax.axis_index("page")
    x, z = lax.div(page, NZ), lax.rem(page, NZ)

    def along_x(k):
        return {"page": lax.rem(x + k + NX, NX) * NZ + z}

    def along_z(k):
        return {"page": x * NZ + lax.rem(z + k + NZ, NZ)}

    def along_g(k):
        return {"group": lax.rem(g + k + NG, NG)}

    def send(source, target, send_sem, recv_sem, device):
        copy = pltpu.make_async_remote_copy(
            src_ref=source,
            dst_ref=target,
            send_sem=send_sem,
            recv_sem=recv_sem,
            device_id=device,
            device_id_type=MESH,
        )
        copy.start()
        return copy

    def done(region, sem):
        pltpu.make_async_copy(region, region, sem).wait()

    far_z = sorted(range(1, NZ), key=lambda k: -min(k, NZ - k))
    order = [0] + far_z[::-1]
    far_g = sorted(range(1, NG), key=lambda k: -min(k, NG - k))
    far_x = sorted(range(1, NX), key=lambda k: -min(k, NX - k))

    def local(source, target, sem):
        copy = pltpu.make_async_copy(source, target, sem)
        copy.start()
        return copy

    q_copy = local(q_hbm, q_in, local_sem.at[0])
    barrier = pltpu.get_barrier_semaphore()
    peers = [along_z(k) for k in far_z] + [along_x(k) for k in far_x] + [along_g(k) for k in far_g]
    for peer in peers:
        pl.semaphore_signal(barrier, inc=1, device_id=peer, device_id_type=MESH)
    page_copy = local(page_hbm, pages, local_sem.at[1])
    length_copy = local(length_hbm, length, local_sem.at[2])
    out_copy = local(out_hbm, w_out, local_sem.at[3])
    key_copies = [
        local(
            k_hbm.at[pl.ds(c * step_keys, step_keys)],
            keys.at[pl.ds(c * step_keys, step_keys)],
            key_sem.at[c],
        )
        for c in range(steps)
    ]
    up_copy = local(up_hbm, w_up, local_sem.at[4])

    q_copy.wait()
    place = lax.broadcasted_iota(jnp.int32, (8, 256), 1) + 512
    owner = lax.broadcasted_iota(jnp.int32, (8, 256), 0) // heads
    q_rows[:, 512:768] = jnp.where(place == width + owner, 1.0, 0.0)
    for t in range(tokens):
        q_rows[t * heads : (t + 1) * heads, 0:width] = q_in[0, t].astype(F32)
    q_packed[0] = jnp.concatenate([q_rows[:, 0:384], q_rows[:, 384:768]], axis=0).astype(BF16)
    pl.semaphore_wait(barrier, len(peers))
    for k in far_z:
        send(q_packed.at[0], q_packed.at[k], qz_send, qz_recv.at[k], along_z(k))

    page_copy.wait()
    length_copy.wait()
    lane = lax.broadcasted_iota(jnp.int32, (8, 128), 1)
    spot = lax.broadcasted_iota(jnp.int32, (64, 64), 0)
    token = lax.broadcasted_iota(jnp.int32, (64, 64), 1)
    last = jnp.where(token < tokens, length[0] - tokens + token - spot, 2**30)

    for c, copy in enumerate(key_copies):
        copy.wait()

        @pl.loop(c * step_keys // 64, (c + 1) * step_keys // 64, unroll=8)
        def _(i):
            at = pl.ds(pl.multiple_of(i * 64, 64), 64)
            mask = jnp.where(pages[0, i] * 64 <= last, 0.0, masked_fill).astype(BF16)
            tails[at, :] = jnp.concatenate([keys[at, latent:width], mask], axis=1)

    for n in range(0, NZ, 2):
        pair = []
        for j in order[n : n + 2]:
            if j > 0:
                done(q_packed.at[j], qz_recv.at[j])
            part = q_packed[j].astype(F32)
            pair.append(jnp.concatenate([part[0:8], part[8:16, 0:256]], axis=1))
        q_all[n * 8 : n * 8 + 16, :] = jnp.concatenate(pair, axis=0).astype(BF16)
        for k in far_x:
            send(
                q_all.at[pl.ds(n * 8, 16)],
                q_all.at[pl.ds(k * block + n * 8, 16)],
                qx_send,
                qx_recv,
                along_x(k),
            )
    done(q_packed.at[pl.ds(1, NZ - 1)], qz_send)

    done(q_all.at[pl.ds(block, rows - block)], qx_recv)

    def columns(value, width):
        return jnp.concatenate([value] * (width // 128), axis=1)

    def score_tile(c, n):
        at = pl.ds(c * step_keys + n * tile_keys, tile_keys)
        wide = jnp.concatenate([keys[at, 0:latent], tails[at, :]], axis=1)
        s = dot(q_all[...], wide, 1) * (score_scale * log2_e)
        scores[c % 2, :, n * tile_keys : (n + 1) * tile_keys] = s
        return functools.reduce(
            jnp.maximum, [s[:, j : j + 128] for j in range(0, tile_keys, 128)]
        )

    tiles = step_keys // tile_keys
    largest = functools.reduce(jnp.maximum, [score_tile(0, n) for n in range(tiles)])
    total = jnp.zeros((rows, 128), F32)
    for c in range(steps):
        top = jnp.broadcast_to(jnp.max(largest, axis=1, keepdims=True), (rows, 128))
        if c == 0:
            tops[c] = jnp.maximum(top, lowest_top)
        else:
            tops[c] = jnp.maximum(top, tops[c - 1])
            shrink = jnp.exp2(tops[c - 1] - tops[c])
            total = total * shrink
        found, pieces = [], []
        for n in range(tiles):
            if c + 1 < steps:
                found.append(score_tile(c + 1, n))
            for low in range(n * tile_keys, (n + 1) * tile_keys, 128):
                p = jnp.exp2((scores[c % 2, :, low : low + 128] - tops[c]).astype(BF16))
                total = total + p.astype(F32)
                probs[:, c * step_keys + low : c * step_keys + low + 128] = p
                pieces.append(p)
        if found:
            largest = functools.reduce(jnp.maximum, found)
        part = dot(jnp.concatenate(pieces, axis=1), keys[pl.ds(c * step_keys, step_keys), 0:half])
        numer[0] = part if c == 0 else numer[0] * columns(shrink, half) + part

    top_column = tops[steps - 1]
    sum_column = jnp.broadcast_to(jnp.sum(total, axis=1, keepdims=True), (rows, 128))
    owner = lax.div(lax.broadcasted_iota(jnp.int32, (8, 128), 1), 8)
    for i in range(NX):
        tile = jnp.zeros((8, 128), F32)
        for v in range(NZ):
            first = i * block + v * 8
            tile = jnp.where(owner == v, top_column[first : first + 8], tile)
            tile = jnp.where(owner == v + 8, sum_column[first : first + 8], tile)
        stat_send[i] = tile
    for k in far_x:
        send(stat_send.at[k], stat_recv.at[k], st_send, st_recv, along_x(-k))

    def send_half(h):
        num_send[h] = numer[h].astype(BF16)
        for k in far_x:
            send(
                num_send.at[h, pl.ds(k * block, block)],
                num_recv.at[h, k],
                nx_send.at[h],
                nx_recv.at[h],
                along_x(-k),
            )

    send_half(0)

    for c in range(steps):
        here = pl.ds(c * step_keys, step_keys)
        part = dot(probs[:, here], keys[here, half:latent])
        if c + 1 < steps:
            part = part * columns(jnp.exp2(tops[c] - tops[steps - 1]), half)
        numer[1] = part if c == 0 else numer[1] + part

    send_half(1)
    done(q_all.at[pl.ds(block, rows - block)], qx_send)

    done(stat_recv.at[pl.ds(1, NX - 1)], st_recv)
    found = [stat_send[0]] + [stat_recv[k] for k in range(1, NX)]
    factors = [[] for _ in found]
    z_stats = []
    for v in range(NZ):
        peaks = [jnp.broadcast_to(f[:, 8 * v : 8 * v + 1], (8, 128)) for f in found]
        top_x = functools.reduce(jnp.maximum, peaks)
        coarse = top_x.astype(BF16).astype(F32)
        top_x = coarse + (top_x - coarse).astype(BF16).astype(F32)
        total_x = jnp.zeros((8, 128), F32)
        for f, t, held in zip(found, peaks, factors):
            held.append(jnp.exp2(t - top_x))
            total_x = total_x + f[:, 64 + 8 * v : 64 + 8 * v + 1] * held[v]
        z_stats.append(jnp.where(lane < 64, top_x, total_x))
        if v > 0:
            coarse = z_stats[v].astype(BF16).astype(F32)
            low_send[order[v], :, 128:256] = jnp.concatenate(
                [coarse, z_stats[v] - coarse], axis=0
            ).astype(BF16)
    factors = [
        jnp.concatenate([jnp.concatenate(held, axis=0)] * (half // 128), axis=1) for held in factors
    ]

    spans = ((0, 256), (256, 384))
    own_half = []
    for h in range(2):
        done(num_recv.at[h, pl.ds(1, NX - 1)], nx_recv.at[h])
        merged = numer[h, 0:block, :] * factors[0]
        for k in range(1, NX):
            merged = merged + num_recv[h, k].astype(F32) * factors[k]
        own_half.append([merged[0:8, j : j + 128] for j in range(0, half, 128)])
        low, high = spans[h]
        for k in far_z:
            part = merged[order.index(k) * 8 : (order.index(k) + 1) * 8]
            low_send[k, :, low : low + 128] = jnp.concatenate(
                [part[:, 0:128], part[:, 128:256]], axis=0
            ).astype(BF16)
            send(
                low_send.at[k, :, low:high],
                low_recv.at[k, :, low:high],
                nz_send.at[h],
                nz_recv.at[h],
                along_z(-k),
            )
    x_columns = own_columns * NZ
    x_lanes = out_group * NZ
    out_copy.wait()
    place = lax.broadcasted_iota(jnp.int32, (1, x_lanes), 1)
    inside = lax.rem(place, out_group)
    wanted = lax.div(place, out_group) * own_columns + inside
    wanted = jnp.where(inside < own_columns, wanted, -(2**20))
    for i in range(NX):
        low = i * x_columns // 128 * 128
        high = min(-(-(i + 1) * x_columns // 128) * 128, w_out.shape[1])
        column = lax.broadcasted_iota(jnp.int32, (high - low, x_lanes), 0)
        pick = jnp.where(column == wanted + (i * x_columns - low), 1.0, 0.0).astype(BF16)
        w_placed[:, i * x_lanes : (i + 1) * x_lanes] = dot(w_out[:, low:high], pick).astype(BF16)

    done(stat_recv.at[pl.ds(1, NX - 1)], st_send)
    for h in range(2):
        done(num_recv.at[h, pl.ds(1, NX - 1)], nx_send.at[h])

    done(low_recv.at[pl.ds(1, NZ - 1), :, 0:256], nz_recv.at[0])
    found = [z_stats[0]]
    for k in range(1, NZ):
        held = low_recv[k, :, 128:256].astype(F32)
        found.append(held[0:8] + held[8:16])
    peaks = [jnp.broadcast_to(f[:, 0:1], (8, 128)) for f in found]
    top_z = functools.reduce(jnp.maximum, peaks)
    factors = [jnp.exp2(t - top_z) for t in peaks]
    total_z = sum(f[:, 64:65] * w for f, w in zip(found, factors))
    attended = []
    for h in range(2):
        if h == 1:
            done(low_recv.at[pl.ds(1, NZ - 1), :, 256:384], nz_recv.at[1])
        merged = [own * factors[0] for own in own_half[h]]
        for k in range(1, NZ):
            held = low_recv[k, :, spans[h][0] : spans[h][0] + 128].astype(F32)
            for j in range(2):
                merged[j] = merged[j] + held[j * 8 : (j + 1) * 8] * factors[k]
        attended += [m / total_z for m in merged]
    attended = jnp.concatenate(attended, axis=1)
    head = lax.rem(lax.broadcasted_iota(jnp.int32, attended.shape, 0), heads)
    spread = [jnp.where(head == i, attended, 0.0) for i in range(heads)]
    up_copy.wait()
    values = dot(
        jnp.concatenate(spread, axis=1).astype(BF16), w_up[...].reshape(heads * latent, -1)
    )

    own = pl.ds(pl.multiple_of(g * 8, 8), 8)
    head_values[own, :] = values.astype(BF16).astype(F32)
    for k in far_g:
        send(head_values.at[own], head_values.at[own], v_send, v_recv, along_g(k))
    others = head_values.at[pl.ds(0, (NG - 1) * 8)]
    done(low_recv.at[pl.ds(1, NZ - 1), :, 0:256], nz_send.at[0])
    done(low_recv.at[pl.ds(1, NZ - 1), :, 256:384], nz_send.at[1])
    done(others, v_recv)
    wide = [head_values[pl.ds(i, tokens * NG, stride=heads), :] for i in range(heads)]
    terms = dot(jnp.concatenate(wide, axis=1).astype(BF16), w_placed[...])

    for i in range(NX):
        term_send[i] = terms[:, i * x_lanes : (i + 1) * x_lanes].astype(BF16)
    for k in far_x:
        send(term_send.at[lax.rem(x + k, NX)], term_recv.at[k], tx_send, tx_recv, along_x(k))
    done(others, v_send)
    summed = term_send[x].astype(F32)
    done(term_recv.at[pl.ds(1, NX - 1)], tx_recv)
    for k in range(1, NX):
        summed = summed + term_recv[k].astype(F32)
    for i in range(x_lanes // 128):
        last_send[i] = summed[:, i * 128 : (i + 1) * 128].astype(BF16)
    per_tile = 128 // out_group
    for k in far_z:
        send(
            last_send.at[lax.div(lax.rem(z + k, NZ), per_tile)],
            last_recv.at[k],
            tz_send,
            tz_recv,
            along_z(k),
        )
    done(term_recv.at[pl.ds(1, NX - 1)], tx_send)
    final = last_send[lax.div(z, per_tile)].astype(F32)
    done(last_recv.at[pl.ds(1, NZ - 1)], tz_recv)
    for k in range(1, NZ):
        final = final + last_recv[k].astype(F32)
    place = lax.rem(z, per_tile)
    chosen = final
    for i in range(1, per_tile):
        chosen = jnp.where(place == i, pltpu.roll(final, 128 - i * out_group, 1), chosen)
    result[...] = chosen.astype(BF16)
    done(last_recv.at[pl.ds(1, NZ - 1)], tz_send)


def body(sizes, queries, cache, slot_page, lengths, w_uv, w_out):
    NX, NZ, NG, own_columns = sizes
    tokens, heads, width = queries.shape[1:]
    latent = w_uv.shape[1]
    half = latent // 2
    key_rows = cache.shape[1] * cache.shape[2]
    rows = NX * NZ * 8
    block = NZ * 8
    x_lanes = NZ * out_group
    sem = pltpu.SemaphoreType.DMA
    scratch = [
        pltpu.VMEM(queries.shape, BF16),
        pltpu.VMEM((8, 768), F32),
        pltpu.VMEM((NZ, 16, 384), BF16),
        pltpu.VMEM((rows, 640), BF16),
        pltpu.VMEM((key_rows, width), BF16),
        pltpu.SMEM(slot_page.shape, jnp.int32),
        pltpu.SMEM(lengths.shape, jnp.int32),
        pltpu.VMEM(w_uv.shape, BF16),
        pltpu.VMEM(w_out.shape, BF16),
        pltpu.VMEM((w_out.shape[0], NX * x_lanes), BF16),
        pltpu.VMEM((key_rows, 128), BF16),
        pltpu.VMEM((2, rows, step_keys), F32),
        pltpu.VMEM((rows, key_rows), BF16),
        pltpu.VMEM((key_rows // step_keys, rows, 128), F32),
        pltpu.VMEM((2, rows, half), F32),
        pltpu.VMEM((2, rows, half), BF16),
        pltpu.VMEM((2, NX, block, half), BF16),
        pltpu.VMEM((NX, 8, 128), F32),
        pltpu.VMEM((NX, 8, 128), F32),
        pltpu.VMEM((NZ, 16, 384), BF16),
        pltpu.VMEM((NZ, 16, 384), BF16),
        pltpu.VMEM((NG * 8, 128), F32),
        pltpu.VMEM((NX, tokens * NG, x_lanes), BF16),
        pltpu.VMEM((NX, tokens * NG, x_lanes), BF16),
        pltpu.VMEM((x_lanes // 128, tokens * NG, 128), BF16),
        pltpu.VMEM((NZ, tokens * NG, 128), BF16),
        sem((5,)),
        sem((key_rows // step_keys,)),
        sem,
        sem((NZ,)),
        sem,
        sem,
        sem,
        sem,
        sem((2,)),
        sem((2,)),
        sem((2,)),
        sem((2,)),
        sem,
        sem,
        sem,
        sem,
        sem,
        sem,
    ]
    result = pl.pallas_call(
        functools.partial(kernel, sizes),
        out_shape=jax.ShapeDtypeStruct((tokens * NG, 128), BF16),
        in_specs=[pl.BlockSpec(memory_space=pltpu.HBM)] * 6,
        out_specs=pl.BlockSpec(memory_space=pltpu.VMEM),
        scratch_shapes=scratch,
        compiler_params=pltpu.CompilerParams(
            collective_id=0, has_side_effects=True, vmem_limit_bytes=55220 * 1024
        ),
    )(queries, cache.reshape(key_rows, width), slot_page, lengths, w_uv, w_out)
    return result[:, 0:own_columns].reshape(NG, tokens, own_columns)


def solution(mesh, NX=4):
    NG, pages = mesh.shape["group"], mesh.shape["page"]
    in_specs = (
        P("group", None, "page", None),
        P("group", "page", None, None),
        P("group", "page"),
        P("group"),
        P("page", None, None),
        P("page", "group"),
    )
    out_specs = P(None, None, ("group", "page"))

    def step(queries, cache, slot_page, lengths, w_uv, w_out):
        sizes = (NX, pages // NX, NG, w_out.shape[1] // pages)
        return body(sizes, queries, cache, slot_page, lengths, w_uv, w_out)

    return jax.shard_map(step, mesh=mesh, in_specs=in_specs, out_specs=out_specs, check_vma=False)
```

```python
import functools

import jax
import jax.numpy as jnp
from jax import lax
from jax.experimental import pallas as pl
from jax.experimental.pallas import tpu as pltpu
from jax.sharding import PartitionSpec as P

MESH = pl.DeviceIdType.MESH
F32 = jnp.float32
BF16 = jnp.bfloat16
score_scale = 192.0 ** (-0.5)
log2_e = 1.4426950408889634
masked_fill = -(2.0**99)
lowest_top = -(2.0**20)
out_group = 32
step_keys = 512
tile_keys = 256


def dot(a, b, contract_b=0):
    return lax.dot_general(a, b, (((1,), (contract_b,)), ((), ())), preferred_element_type=F32)


def kernel(
    sizes,
    q_hbm,
    k_hbm,
    page_hbm,
    length_hbm,
    up_hbm,
    out_hbm,
    result,
    q_in,
    q_rows,
    q_packed,
    q_all,
    keys,
    pages,
    length,
    w_up,
    w_out,
    w_placed,
    tails,
    scores,
    tops,
    numer,
    num_send,
    num_recv,
    stat_send,
    stat_recv,
    low_send,
    low_recv,
    head_values,
    term_send,
    term_recv,
    last_send,
    last_recv,
    local_sem,
    key_sem,
    qz_send,
    qz_recv,
    qx_send,
    qx_recv,
    st_send,
    st_recv,
    nx_send,
    nx_recv,
    nz_send,
    nz_recv,
    v_send,
    v_recv,
    tx_send,
    tx_recv,
    tz_send,
    tz_recv,
):
    NX, NZ, NG, own_columns = sizes
    width = q_in.shape[-1]
    latent = w_up.shape[1]
    half = latent // 2
    key_rows = keys.shape[0]
    rows = q_all.shape[0]
    block = rows // NX
    steps = key_rows // step_keys
    tokens, heads = q_in.shape[1], q_in.shape[2]

    g = lax.axis_index("group")
    page = lax.axis_index("page")
    x, z = lax.div(page, NZ), lax.rem(page, NZ)

    def along_x(k):
        return {"page": lax.rem(x + k + NX, NX) * NZ + z}

    def along_z(k):
        return {"page": x * NZ + lax.rem(z + k + NZ, NZ)}

    def along_g(k):
        return {"group": lax.rem(g + k + NG, NG)}

    def send(source, target, send_sem, recv_sem, device):
        copy = pltpu.make_async_remote_copy(
            src_ref=source,
            dst_ref=target,
            send_sem=send_sem,
            recv_sem=recv_sem,
            device_id=device,
            device_id_type=MESH,
        )
        copy.start()
        return copy

    def done(region, sem):
        pltpu.make_async_copy(region, region, sem).wait()

    far_z = sorted(range(1, NZ), key=lambda k: -min(k, NZ - k))
    order = [0] + far_z[::-1]
    far_g = sorted(range(1, NG), key=lambda k: -min(k, NG - k))
    far_x = sorted(range(1, NX), key=lambda k: -min(k, NX - k))

    def local(source, target, sem):
        copy = pltpu.make_async_copy(source, target, sem)
        copy.start()
        return copy

    q_copy = local(q_hbm, q_in, local_sem.at[0])
    barrier = pltpu.get_barrier_semaphore()
    peers = [along_z(k) for k in far_z] + [along_x(k) for k in far_x] + [along_g(k) for k in far_g]
    for peer in peers:
        pl.semaphore_signal(barrier, inc=1, device_id=peer, device_id_type=MESH)
    page_copy = local(page_hbm, pages, local_sem.at[1])
    length_copy = local(length_hbm, length, local_sem.at[2])
    out_copy = local(out_hbm, w_out, local_sem.at[3])
    key_copies = [
        local(
            k_hbm.at[pl.ds(c * step_keys, step_keys)],
            keys.at[pl.ds(c * step_keys, step_keys)],
            key_sem.at[c],
        )
        for c in range(steps)
    ]
    up_copy = local(up_hbm, w_up, local_sem.at[4])

    q_copy.wait()
    place = lax.broadcasted_iota(jnp.int32, (8, 256), 1) + 512
    owner = lax.broadcasted_iota(jnp.int32, (8, 256), 0) // heads
    q_rows[:, 512:768] = jnp.where(place == width + owner, 1.0, 0.0)
    for t in range(tokens):
        q_rows[t * heads : (t + 1) * heads, 0:width] = q_in[0, t].astype(F32)
    q_packed[0] = jnp.concatenate([q_rows[:, 0:384], q_rows[:, 384:768]], axis=0).astype(BF16)
    pl.semaphore_wait(barrier, len(peers))
    for k in far_z:
        send(q_packed.at[0], q_packed.at[k], qz_send, qz_recv.at[k], along_z(k))

    page_copy.wait()
    length_copy.wait()
    lane = lax.broadcasted_iota(jnp.int32, (8, 128), 1)
    spot = lax.broadcasted_iota(jnp.int32, (64, 64), 0)
    token = lax.broadcasted_iota(jnp.int32, (64, 64), 1)
    last = jnp.where(token < tokens, length[0] - tokens + token - spot, 2**30)

    for c, copy in enumerate(key_copies):
        copy.wait()

        @pl.loop(c * step_keys // 64, (c + 1) * step_keys // 64, unroll=8)
        def _(i):
            at = pl.ds(pl.multiple_of(i * 64, 64), 64)
            mask = jnp.where(pages[0, i] * 64 <= last, 0.0, masked_fill).astype(BF16)
            tails[at, :] = jnp.concatenate([keys[at, latent:width], mask], axis=1)

    for n in range(0, NZ, 2):
        pair = []
        for j in order[n : n + 2]:
            if j > 0:
                done(q_packed.at[j], qz_recv.at[j])
            part = q_packed[j].astype(F32)
            pair.append(jnp.concatenate([part[0:8], part[8:16, 0:256]], axis=1))
        q_all[n * 8 : n * 8 + 16, :] = jnp.concatenate(pair, axis=0).astype(BF16)
        for k in far_x:
            send(
                q_all.at[pl.ds(n * 8, 16)],
                q_all.at[pl.ds(k * block + n * 8, 16)],
                qx_send,
                qx_recv,
                along_x(k),
            )
    done(q_packed.at[pl.ds(1, NZ - 1)], qz_send)

    done(q_all.at[pl.ds(block, rows - block)], qx_recv)

    def columns(value, width):
        return jnp.concatenate([value] * (width // 128), axis=1)

    def score_tile(c, n):
        at = pl.ds(c * step_keys + n * tile_keys, tile_keys)
        wide = jnp.concatenate([keys[at, 0:latent], tails[at, :]], axis=1)
        s = dot(q_all[...], wide, 1) * (score_scale * log2_e)
        scores[c % 2, :, n * tile_keys : (n + 1) * tile_keys] = s
        return functools.reduce(
            jnp.maximum, [s[:, j : j + 128] for j in range(0, tile_keys, 128)]
        )

    tiles = step_keys // tile_keys
    largest = functools.reduce(jnp.maximum, [score_tile(0, n) for n in range(tiles)])
    total = jnp.zeros((rows, 128), F32)
    for c in range(steps):
        top = jnp.broadcast_to(jnp.max(largest, axis=1, keepdims=True), (rows, 128))
        if c == 0:
            tops[c] = jnp.maximum(top, lowest_top)
        else:
            tops[c] = jnp.maximum(top, tops[c - 1])
            shrink = jnp.exp2(tops[c - 1] - tops[c])
            total = total * shrink
        found, pieces = [], []
        for n in range(tiles):
            if c + 1 < steps:
                found.append(score_tile(c + 1, n))
            for low in range(n * tile_keys, (n + 1) * tile_keys, 128):
                p = jnp.exp2((scores[c % 2, :, low : low + 128] - tops[c]).astype(BF16))
                total = total + p.astype(F32)
                pieces.append(p)
        if found:
            largest = functools.reduce(jnp.maximum, found)
        here = pl.ds(c * step_keys, step_keys)
        part = dot(jnp.concatenate(pieces, axis=1), keys[here, 0:latent])
        for h in range(2):
            own = part[:, h * half : (h + 1) * half]
            numer[h] = own if c == 0 else numer[h] * columns(shrink, half) + own

    top_column = tops[steps - 1]
    sum_column = jnp.broadcast_to(jnp.sum(total, axis=1, keepdims=True), (rows, 128))
    owner = lax.div(lax.broadcasted_iota(jnp.int32, (8, 128), 1), 8)
    for i in range(NX):
        tile = jnp.zeros((8, 128), F32)
        for v in range(NZ):
            first = i * block + v * 8
            tile = jnp.where(owner == v, top_column[first : first + 8], tile)
            tile = jnp.where(owner == v + 8, sum_column[first : first + 8], tile)
        stat_send[i] = tile
    for k in far_x:
        send(stat_send.at[k], stat_recv.at[k], st_send, st_recv, along_x(-k))

    def send_half(h):
        num_send[h] = numer[h].astype(BF16)
        for k in far_x:
            send(
                num_send.at[h, pl.ds(k * block, block)],
                num_recv.at[h, k],
                nx_send.at[h],
                nx_recv.at[h],
                along_x(-k),
            )

    send_half(0)

    send_half(1)
    done(q_all.at[pl.ds(block, rows - block)], qx_send)

    done(stat_recv.at[pl.ds(1, NX - 1)], st_recv)
    found = [stat_send[0]] + [stat_recv[k] for k in range(1, NX)]
    factors = [[] for _ in found]
    z_stats = []
    for v in range(NZ):
        peaks = [jnp.broadcast_to(f[:, 8 * v : 8 * v + 1], (8, 128)) for f in found]
        top_x = functools.reduce(jnp.maximum, peaks)
        coarse = top_x.astype(BF16).astype(F32)
        top_x = coarse + (top_x - coarse).astype(BF16).astype(F32)
        total_x = jnp.zeros((8, 128), F32)
        for f, t, held in zip(found, peaks, factors):
            held.append(jnp.exp2(t - top_x))
            total_x = total_x + f[:, 64 + 8 * v : 64 + 8 * v + 1] * held[v]
        z_stats.append(jnp.where(lane < 64, top_x, total_x))
        if v > 0:
            coarse = z_stats[v].astype(BF16).astype(F32)
            low_send[order[v], :, 128:256] = jnp.concatenate(
                [coarse, z_stats[v] - coarse], axis=0
            ).astype(BF16)
    factors = [
        jnp.concatenate([jnp.concatenate(held, axis=0)] * (half // 128), axis=1) for held in factors
    ]

    spans = ((0, 256), (256, 384))
    own_half = []
    for h in range(2):
        done(num_recv.at[h, pl.ds(1, NX - 1)], nx_recv.at[h])
        merged = numer[h, 0:block, :] * factors[0]
        for k in range(1, NX):
            merged = merged + num_recv[h, k].astype(F32) * factors[k]
        own_half.append([merged[0:8, j : j + 128] for j in range(0, half, 128)])
        low, high = spans[h]
        for k in far_z:
            part = merged[order.index(k) * 8 : (order.index(k) + 1) * 8]
            low_send[k, :, low : low + 128] = jnp.concatenate(
                [part[:, 0:128], part[:, 128:256]], axis=0
            ).astype(BF16)
            send(
                low_send.at[k, :, low:high],
                low_recv.at[k, :, low:high],
                nz_send.at[h],
                nz_recv.at[h],
                along_z(-k),
            )
    x_columns = own_columns * NZ
    x_lanes = out_group * NZ
    out_copy.wait()
    place = lax.broadcasted_iota(jnp.int32, (1, x_lanes), 1)
    inside = lax.rem(place, out_group)
    wanted = lax.div(place, out_group) * own_columns + inside
    wanted = jnp.where(inside < own_columns, wanted, -(2**20))
    for i in range(NX):
        low = i * x_columns // 128 * 128
        high = min(-(-(i + 1) * x_columns // 128) * 128, w_out.shape[1])
        column = lax.broadcasted_iota(jnp.int32, (high - low, x_lanes), 0)
        pick = jnp.where(column == wanted + (i * x_columns - low), 1.0, 0.0).astype(BF16)
        w_placed[:, i * x_lanes : (i + 1) * x_lanes] = dot(w_out[:, low:high], pick).astype(BF16)

    done(stat_recv.at[pl.ds(1, NX - 1)], st_send)
    for h in range(2):
        done(num_recv.at[h, pl.ds(1, NX - 1)], nx_send.at[h])

    done(low_recv.at[pl.ds(1, NZ - 1), :, 0:256], nz_recv.at[0])
    found = [z_stats[0]]
    for k in range(1, NZ):
        held = low_recv[k, :, 128:256].astype(F32)
        found.append(held[0:8] + held[8:16])
    peaks = [jnp.broadcast_to(f[:, 0:1], (8, 128)) for f in found]
    top_z = functools.reduce(jnp.maximum, peaks)
    factors = [jnp.exp2(t - top_z) for t in peaks]
    total_z = sum(f[:, 64:65] * w for f, w in zip(found, factors))
    attended = []
    for h in range(2):
        if h == 1:
            done(low_recv.at[pl.ds(1, NZ - 1), :, 256:384], nz_recv.at[1])
        merged = [own * factors[0] for own in own_half[h]]
        for k in range(1, NZ):
            held = low_recv[k, :, spans[h][0] : spans[h][0] + 128].astype(F32)
            for j in range(2):
                merged[j] = merged[j] + held[j * 8 : (j + 1) * 8] * factors[k]
        attended += [m / total_z for m in merged]
    attended = jnp.concatenate(attended, axis=1)
    head = lax.rem(lax.broadcasted_iota(jnp.int32, attended.shape, 0), heads)
    spread = [jnp.where(head == i, attended, 0.0) for i in range(heads)]
    up_copy.wait()
    values = dot(
        jnp.concatenate(spread, axis=1).astype(BF16), w_up[...].reshape(heads * latent, -1)
    )

    own = pl.ds(pl.multiple_of(g * 8, 8), 8)
    head_values[own, :] = values.astype(BF16).astype(F32)
    for k in far_g:
        send(head_values.at[own], head_values.at[own], v_send, v_recv, along_g(k))
    others = head_values.at[pl.ds(0, (NG - 1) * 8)]
    done(low_recv.at[pl.ds(1, NZ - 1), :, 0:256], nz_send.at[0])
    done(low_recv.at[pl.ds(1, NZ - 1), :, 256:384], nz_send.at[1])
    done(others, v_recv)
    wide = [head_values[pl.ds(i, tokens * NG, stride=heads), :] for i in range(heads)]
    terms = dot(jnp.concatenate(wide, axis=1).astype(BF16), w_placed[...])

    for i in range(NX):
        term_send[i] = terms[:, i * x_lanes : (i + 1) * x_lanes].astype(BF16)
    for k in far_x:
        send(term_send.at[lax.rem(x + k, NX)], term_recv.at[k], tx_send, tx_recv, along_x(k))
    done(others, v_send)
    summed = term_send[x].astype(F32)
    done(term_recv.at[pl.ds(1, NX - 1)], tx_recv)
    for k in range(1, NX):
        summed = summed + term_recv[k].astype(F32)
    for i in range(x_lanes // 128):
        last_send[i] = summed[:, i * 128 : (i + 1) * 128].astype(BF16)
    per_tile = 128 // out_group
    for k in far_z:
        send(
            last_send.at[lax.div(lax.rem(z + k, NZ), per_tile)],
            last_recv.at[k],
            tz_send,
            tz_recv,
            along_z(k),
        )
    done(term_recv.at[pl.ds(1, NX - 1)], tx_send)
    final = last_send[lax.div(z, per_tile)].astype(F32)
    done(last_recv.at[pl.ds(1, NZ - 1)], tz_recv)
    for k in range(1, NZ):
        final = final + last_recv[k].astype(F32)
    place = lax.rem(z, per_tile)
    chosen = final
    for i in range(1, per_tile):
        chosen = jnp.where(place == i, pltpu.roll(final, 128 - i * out_group, 1), chosen)
    result[...] = chosen.astype(BF16)
    done(last_recv.at[pl.ds(1, NZ - 1)], tz_send)


def body(sizes, queries, cache, slot_page, lengths, w_uv, w_out):
    NX, NZ, NG, own_columns = sizes
    tokens, heads, width = queries.shape[1:]
    latent = w_uv.shape[1]
    half = latent // 2
    key_rows = cache.shape[1] * cache.shape[2]
    rows = NX * NZ * 8
    block = NZ * 8
    x_lanes = NZ * out_group
    sem = pltpu.SemaphoreType.DMA
    scratch = [
        pltpu.VMEM(queries.shape, BF16),
        pltpu.VMEM((8, 768), F32),
        pltpu.VMEM((NZ, 16, 384), BF16),
        pltpu.VMEM((rows, 640), BF16),
        pltpu.VMEM((key_rows, width), BF16),
        pltpu.SMEM(slot_page.shape, jnp.int32),
        pltpu.SMEM(lengths.shape, jnp.int32),
        pltpu.VMEM(w_uv.shape, BF16),
        pltpu.VMEM(w_out.shape, BF16),
        pltpu.VMEM((w_out.shape[0], NX * x_lanes), BF16),
        pltpu.VMEM((key_rows, 128), BF16),
        pltpu.VMEM((2, rows, step_keys), F32),
        pltpu.VMEM((key_rows // step_keys, rows, 128), F32),
        pltpu.VMEM((2, rows, half), F32),
        pltpu.VMEM((2, rows, half), BF16),
        pltpu.VMEM((2, NX, block, half), BF16),
        pltpu.VMEM((NX, 8, 128), F32),
        pltpu.VMEM((NX, 8, 128), F32),
        pltpu.VMEM((NZ, 16, 384), BF16),
        pltpu.VMEM((NZ, 16, 384), BF16),
        pltpu.VMEM((NG * 8, 128), F32),
        pltpu.VMEM((NX, tokens * NG, x_lanes), BF16),
        pltpu.VMEM((NX, tokens * NG, x_lanes), BF16),
        pltpu.VMEM((x_lanes // 128, tokens * NG, 128), BF16),
        pltpu.VMEM((NZ, tokens * NG, 128), BF16),
        sem((5,)),
        sem((key_rows // step_keys,)),
        sem,
        sem((NZ,)),
        sem,
        sem,
        sem,
        sem,
        sem((2,)),
        sem((2,)),
        sem((2,)),
        sem((2,)),
        sem,
        sem,
        sem,
        sem,
        sem,
        sem,
    ]
    result = pl.pallas_call(
        functools.partial(kernel, sizes),
        out_shape=jax.ShapeDtypeStruct((tokens * NG, 128), BF16),
        in_specs=[pl.BlockSpec(memory_space=pltpu.HBM)] * 6,
        out_specs=pl.BlockSpec(memory_space=pltpu.VMEM),
        scratch_shapes=scratch,
        compiler_params=pltpu.CompilerParams(
            collective_id=0, has_side_effects=True, vmem_limit_bytes=55220 * 1024
        ),
    )(queries, cache.reshape(key_rows, width), slot_page, lengths, w_uv, w_out)
    return result[:, 0:own_columns].reshape(NG, tokens, own_columns)


def solution(mesh, NX=4):
    NG, pages = mesh.shape["group"], mesh.shape["page"]
    in_specs = (
        P("group", None, "page", None),
        P("group", "page", None, None),
        P("group", "page"),
        P("group"),
        P("page", None, None),
        P("page", "group"),
    )
    out_specs = P(None, None, ("group", "page"))

    def step(queries, cache, slot_page, lengths, w_uv, w_out):
        sizes = (NX, pages // NX, NG, w_out.shape[1] // pages)
        return body(sizes, queries, cache, slot_page, lengths, w_uv, w_out)

    return jax.shard_map(step, mesh=mesh, in_specs=in_specs, out_specs=out_specs, check_vma=False)
```

```python
import functools

import jax
import jax.numpy as jnp
from jax import lax
from jax.experimental import pallas as pl
from jax.experimental.pallas import tpu as pltpu
from jax.sharding import PartitionSpec as P

MESH = pl.DeviceIdType.MESH
F32 = jnp.float32
BF16 = jnp.bfloat16
score_scale = 192.0 ** (-0.5)
log2_e = 1.4426950408889634
masked_fill = -(2.0**99)
lowest_top = -(2.0**20)
out_group = 32
step_keys = 512
tile_keys = 256


def dot(a, b, contract_b=0):
    return lax.dot_general(a, b, (((1,), (contract_b,)), ((), ())), preferred_element_type=F32)


def kernel(
    sizes,
    q_hbm,
    k_hbm,
    page_hbm,
    length_hbm,
    up_hbm,
    out_hbm,
    result,
    q_in,
    q_rows,
    q_packed,
    q_all,
    keys,
    pages,
    length,
    w_up,
    w_out,
    w_placed,
    tails,
    scores,
    tops,
    numer,
    num_send,
    num_recv,
    stat_send,
    stat_recv,
    low_send,
    low_recv,
    head_values,
    term_send,
    term_recv,
    last_send,
    last_recv,
    local_sem,
    key_sem,
    qz_send,
    qz_recv,
    qx_send,
    qx_recv,
    st_send,
    st_recv,
    nx_send,
    nx_recv,
    nz_send,
    nz_recv,
    v_send,
    v_recv,
    tx_send,
    tx_recv,
    tz_send,
    tz_recv,
):
    NX, NZ, NG, own_columns = sizes
    width = q_in.shape[-1]
    latent = w_up.shape[1]
    half = latent // 2
    key_rows = keys.shape[0]
    rows = q_all.shape[0]
    block = rows // NX
    steps = key_rows // step_keys
    tokens, heads = q_in.shape[1], q_in.shape[2]

    g = lax.axis_index("group")
    page = lax.axis_index("page")
    x, z = lax.div(page, NZ), lax.rem(page, NZ)

    def along_x(k):
        return {"page": lax.rem(x + k + NX, NX) * NZ + z}

    def along_z(k):
        return {"page": x * NZ + lax.rem(z + k + NZ, NZ)}

    def along_g(k):
        return {"group": lax.rem(g + k + NG, NG)}

    def send(source, target, send_sem, recv_sem, device):
        copy = pltpu.make_async_remote_copy(
            src_ref=source,
            dst_ref=target,
            send_sem=send_sem,
            recv_sem=recv_sem,
            device_id=device,
            device_id_type=MESH,
        )
        copy.start()
        return copy

    def done(region, sem):
        pltpu.make_async_copy(region, region, sem).wait()

    far_z = sorted(range(1, NZ), key=lambda k: -min(k, NZ - k))
    order = [0] + far_z[::-1]
    far_g = sorted(range(1, NG), key=lambda k: -min(k, NG - k))
    far_x = sorted(range(1, NX), key=lambda k: -min(k, NX - k))

    def local(source, target, sem):
        copy = pltpu.make_async_copy(source, target, sem)
        copy.start()
        return copy

    q_copy = local(q_hbm, q_in, local_sem.at[0])
    barrier = pltpu.get_barrier_semaphore()
    peers = [along_z(k) for k in far_z] + [along_x(k) for k in far_x] + [along_g(k) for k in far_g]
    for peer in peers:
        pl.semaphore_signal(barrier, inc=1, device_id=peer, device_id_type=MESH)
    page_copy = local(page_hbm, pages, local_sem.at[1])
    length_copy = local(length_hbm, length, local_sem.at[2])
    out_copy = local(out_hbm, w_out, local_sem.at[3])
    key_copies = [
        local(
            k_hbm.at[pl.ds(c * step_keys, step_keys)],
            keys.at[pl.ds(c * step_keys, step_keys)],
            key_sem.at[c],
        )
        for c in range(steps)
    ]
    up_copy = local(up_hbm, w_up, local_sem.at[4])

    q_copy.wait()
    place = lax.broadcasted_iota(jnp.int32, (8, 256), 1) + 512
    owner = lax.broadcasted_iota(jnp.int32, (8, 256), 0) // heads
    q_rows[:, 512:768] = jnp.where(place == width + owner, 1.0, 0.0)
    for t in range(tokens):
        q_rows[t * heads : (t + 1) * heads, 0:width] = q_in[0, t].astype(F32)
    q_packed[0] = jnp.concatenate([q_rows[:, 0:384], q_rows[:, 384:768]], axis=0).astype(BF16)
    pl.semaphore_wait(barrier, len(peers))
    for k in far_z:
        send(q_packed.at[0], q_packed.at[k], qz_send, qz_recv.at[k], along_z(k))

    page_copy.wait()
    length_copy.wait()
    lane = lax.broadcasted_iota(jnp.int32, (8, 128), 1)
    spot = lax.broadcasted_iota(jnp.int32, (64, 64), 0)
    token = lax.broadcasted_iota(jnp.int32, (64, 64), 1)
    last = jnp.where(token < tokens, length[0] - tokens + token - spot, 2**30)

    for c, copy in enumerate(key_copies):
        copy.wait()

        @pl.loop(c * step_keys // 64, (c + 1) * step_keys // 64, unroll=8)
        def _(i):
            at = pl.ds(pl.multiple_of(i * 64, 64), 64)
            mask = jnp.where(pages[0, i] * 64 <= last, 0.0, masked_fill).astype(BF16)
            tails[at, :] = jnp.concatenate([keys[at, latent:width], mask], axis=1)

    for n in range(0, NZ, 2):
        pair = []
        for j in order[n : n + 2]:
            if j > 0:
                done(q_packed.at[j], qz_recv.at[j])
            part = q_packed[j].astype(F32)
            pair.append(jnp.concatenate([part[0:8], part[8:16, 0:256]], axis=1))
        q_all[n * 8 : n * 8 + 16, :] = jnp.concatenate(pair, axis=0).astype(BF16)
        for k in far_x:
            send(
                q_all.at[pl.ds(n * 8, 16)],
                q_all.at[pl.ds(k * block + n * 8, 16)],
                qx_send,
                qx_recv,
                along_x(k),
            )
    done(q_packed.at[pl.ds(1, NZ - 1)], qz_send)

    done(q_all.at[pl.ds(block, rows - block)], qx_recv)

    def columns(value, width):
        return jnp.concatenate([value] * (width // 128), axis=1)

    def score_tile(c, n):
        at = pl.ds(c * step_keys + n * tile_keys, tile_keys)
        wide = jnp.concatenate([keys[at, 0:latent], tails[at, :]], axis=1)
        s = dot(q_all[...], wide, 1) * (score_scale * log2_e)
        scores[c % 2, :, n * tile_keys : (n + 1) * tile_keys] = s
        return functools.reduce(
            jnp.maximum, [s[:, j : j + 128] for j in range(0, tile_keys, 128)]
        )

    tiles = step_keys // tile_keys
    largest = functools.reduce(jnp.maximum, [score_tile(0, n) for n in range(tiles)])
    total = jnp.zeros((rows, 128), F32)
    for c in range(steps):
        top = jnp.broadcast_to(jnp.max(largest, axis=1, keepdims=True), (rows, 128))
        if c == 0:
            tops[c] = jnp.maximum(top, lowest_top)
        else:
            tops[c] = jnp.maximum(top, tops[c - 1])
            shrink = jnp.exp2(tops[c - 1] - tops[c])
            total = total * shrink
        found, pieces = [], []
        for n in range(tiles):
            if c + 1 < steps:
                found.append(score_tile(c + 1, n))
            for low in range(n * tile_keys, (n + 1) * tile_keys, 128):
                p = jnp.exp2((scores[c % 2, :, low : low + 128] - tops[c]).astype(BF16))
                total = total + p.astype(F32)
                pieces.append(p)
        if found:
            largest = functools.reduce(jnp.maximum, found)
        here = pl.ds(c * step_keys, step_keys)
        part = dot(jnp.concatenate(pieces, axis=1), keys[here, 0:latent])
        for h in range(2):
            own = part[:, h * half : (h + 1) * half]
            numer[h] = own if c == 0 else numer[h] * columns(shrink, half) + own

    def send_half(h):
        num_send[h] = numer[h].astype(BF16)
        for k in far_x:
            send(
                num_send.at[h, pl.ds(k * block, block)],
                num_recv.at[h, k],
                nx_send.at[h],
                nx_recv.at[h],
                along_x(-k),
            )

    send_half(0)
    top_column = tops[steps - 1]
    sum_column = jnp.broadcast_to(jnp.sum(total, axis=1, keepdims=True), (rows, 128))
    owner = lax.div(lax.broadcasted_iota(jnp.int32, (8, 128), 1), 8)
    for i in range(NX):
        tile = jnp.zeros((8, 128), F32)
        for v in range(NZ):
            first = i * block + v * 8
            tile = jnp.where(owner == v, top_column[first : first + 8], tile)
            tile = jnp.where(owner == v + 8, sum_column[first : first + 8], tile)
        stat_send[i] = tile
    for k in far_x:
        send(stat_send.at[k], stat_recv.at[k], st_send, st_recv, along_x(-k))


    send_half(1)
    done(q_all.at[pl.ds(block, rows - block)], qx_send)

    done(stat_recv.at[pl.ds(1, NX - 1)], st_recv)
    found = [stat_send[0]] + [stat_recv[k] for k in range(1, NX)]
    factors = [[] for _ in found]
    z_stats = []
    for v in range(NZ):
        peaks = [jnp.broadcast_to(f[:, 8 * v : 8 * v + 1], (8, 128)) for f in found]
        top_x = functools.reduce(jnp.maximum, peaks)
        coarse = top_x.astype(BF16).astype(F32)
        top_x = coarse + (top_x - coarse).astype(BF16).astype(F32)
        total_x = jnp.zeros((8, 128), F32)
        for f, t, held in zip(found, peaks, factors):
            held.append(jnp.exp2(t - top_x))
            total_x = total_x + f[:, 64 + 8 * v : 64 + 8 * v + 1] * held[v]
        z_stats.append(jnp.where(lane < 64, top_x, total_x))
        if v > 0:
            coarse = z_stats[v].astype(BF16).astype(F32)
            low_send[order[v], :, 128:256] = jnp.concatenate(
                [coarse, z_stats[v] - coarse], axis=0
            ).astype(BF16)
    factors = [
        jnp.concatenate([jnp.concatenate(held, axis=0)] * (half // 128), axis=1) for held in factors
    ]

    spans = ((0, 256), (256, 384))
    own_half = []
    for h in range(2):
        done(num_recv.at[h, pl.ds(1, NX - 1)], nx_recv.at[h])
        merged = numer[h, 0:block, :] * factors[0]
        for k in range(1, NX):
            merged = merged + num_recv[h, k].astype(F32) * factors[k]
        own_half.append([merged[0:8, j : j + 128] for j in range(0, half, 128)])
        low, high = spans[h]
        for k in far_z:
            part = merged[order.index(k) * 8 : (order.index(k) + 1) * 8]
            low_send[k, :, low : low + 128] = jnp.concatenate(
                [part[:, 0:128], part[:, 128:256]], axis=0
            ).astype(BF16)
            send(
                low_send.at[k, :, low:high],
                low_recv.at[k, :, low:high],
                nz_send.at[h],
                nz_recv.at[h],
                along_z(-k),
            )
    x_columns = own_columns * NZ
    x_lanes = out_group * NZ
    out_copy.wait()
    place = lax.broadcasted_iota(jnp.int32, (1, x_lanes), 1)
    inside = lax.rem(place, out_group)
    wanted = lax.div(place, out_group) * own_columns + inside
    wanted = jnp.where(inside < own_columns, wanted, -(2**20))
    for i in range(NX):
        low = i * x_columns // 128 * 128
        high = min(-(-(i + 1) * x_columns // 128) * 128, w_out.shape[1])
        column = lax.broadcasted_iota(jnp.int32, (high - low, x_lanes), 0)
        pick = jnp.where(column == wanted + (i * x_columns - low), 1.0, 0.0).astype(BF16)
        w_placed[:, i * x_lanes : (i + 1) * x_lanes] = dot(w_out[:, low:high], pick).astype(BF16)

    done(stat_recv.at[pl.ds(1, NX - 1)], st_send)
    for h in range(2):
        done(num_recv.at[h, pl.ds(1, NX - 1)], nx_send.at[h])

    done(low_recv.at[pl.ds(1, NZ - 1), :, 0:256], nz_recv.at[0])
    found = [z_stats[0]]
    for k in range(1, NZ):
        held = low_recv[k, :, 128:256].astype(F32)
        found.append(held[0:8] + held[8:16])
    peaks = [jnp.broadcast_to(f[:, 0:1], (8, 128)) for f in found]
    top_z = functools.reduce(jnp.maximum, peaks)
    factors = [jnp.exp2(t - top_z) for t in peaks]
    total_z = sum(f[:, 64:65] * w for f, w in zip(found, factors))
    attended = []
    for h in range(2):
        if h == 1:
            done(low_recv.at[pl.ds(1, NZ - 1), :, 256:384], nz_recv.at[1])
        merged = [own * factors[0] for own in own_half[h]]
        for k in range(1, NZ):
            held = low_recv[k, :, spans[h][0] : spans[h][0] + 128].astype(F32)
            for j in range(2):
                merged[j] = merged[j] + held[j * 8 : (j + 1) * 8] * factors[k]
        attended += [m / total_z for m in merged]
    attended = jnp.concatenate(attended, axis=1)
    head = lax.rem(lax.broadcasted_iota(jnp.int32, attended.shape, 0), heads)
    spread = [jnp.where(head == i, attended, 0.0) for i in range(heads)]
    up_copy.wait()
    values = dot(
        jnp.concatenate(spread, axis=1).astype(BF16), w_up[...].reshape(heads * latent, -1)
    )

    own = pl.ds(pl.multiple_of(g * 8, 8), 8)
    head_values[own, :] = values.astype(BF16).astype(F32)
    for k in far_g:
        send(head_values.at[own], head_values.at[own], v_send, v_recv, along_g(k))
    others = head_values.at[pl.ds(0, (NG - 1) * 8)]
    done(low_recv.at[pl.ds(1, NZ - 1), :, 0:256], nz_send.at[0])
    done(low_recv.at[pl.ds(1, NZ - 1), :, 256:384], nz_send.at[1])
    done(others, v_recv)
    wide = [head_values[pl.ds(i, tokens * NG, stride=heads), :] for i in range(heads)]
    terms = dot(jnp.concatenate(wide, axis=1).astype(BF16), w_placed[...])

    for i in range(NX):
        term_send[i] = terms[:, i * x_lanes : (i + 1) * x_lanes].astype(BF16)
    for k in far_x:
        send(term_send.at[lax.rem(x + k, NX)], term_recv.at[k], tx_send, tx_recv, along_x(k))
    done(others, v_send)
    summed = term_send[x].astype(F32)
    done(term_recv.at[pl.ds(1, NX - 1)], tx_recv)
    for k in range(1, NX):
        summed = summed + term_recv[k].astype(F32)
    for i in range(x_lanes // 128):
        last_send[i] = summed[:, i * 128 : (i + 1) * 128].astype(BF16)
    per_tile = 128 // out_group
    for k in far_z:
        send(
            last_send.at[lax.div(lax.rem(z + k, NZ), per_tile)],
            last_recv.at[k],
            tz_send,
            tz_recv,
            along_z(k),
        )
    done(term_recv.at[pl.ds(1, NX - 1)], tx_send)
    final = last_send[lax.div(z, per_tile)].astype(F32)
    done(last_recv.at[pl.ds(1, NZ - 1)], tz_recv)
    for k in range(1, NZ):
        final = final + last_recv[k].astype(F32)
    place = lax.rem(z, per_tile)
    chosen = final
    for i in range(1, per_tile):
        chosen = jnp.where(place == i, pltpu.roll(final, 128 - i * out_group, 1), chosen)
    result[...] = chosen.astype(BF16)
    done(last_recv.at[pl.ds(1, NZ - 1)], tz_send)


def body(sizes, queries, cache, slot_page, lengths, w_uv, w_out):
    NX, NZ, NG, own_columns = sizes
    tokens, heads, width = queries.shape[1:]
    latent = w_uv.shape[1]
    half = latent // 2
    key_rows = cache.shape[1] * cache.shape[2]
    rows = NX * NZ * 8
    block = NZ * 8
    x_lanes = NZ * out_group
    sem = pltpu.SemaphoreType.DMA
    scratch = [
        pltpu.VMEM(queries.shape, BF16),
        pltpu.VMEM((8, 768), F32),
        pltpu.VMEM((NZ, 16, 384), BF16),
        pltpu.VMEM((rows, 640), BF16),
        pltpu.VMEM((key_rows, width), BF16),
        pltpu.SMEM(slot_page.shape, jnp.int32),
        pltpu.SMEM(lengths.shape, jnp.int32),
        pltpu.VMEM(w_uv.shape, BF16),
        pltpu.VMEM(w_out.shape, BF16),
        pltpu.VMEM((w_out.shape[0], NX * x_lanes), BF16),
        pltpu.VMEM((key_rows, 128), BF16),
        pltpu.VMEM((2, rows, step_keys), F32),
        pltpu.VMEM((key_rows // step_keys, rows, 128), F32),
        pltpu.VMEM((2, rows, half), F32),
        pltpu.VMEM((2, rows, half), BF16),
        pltpu.VMEM((2, NX, block, half), BF16),
        pltpu.VMEM((NX, 8, 128), F32),
        pltpu.VMEM((NX, 8, 128), F32),
        pltpu.VMEM((NZ, 16, 384), BF16),
        pltpu.VMEM((NZ, 16, 384), BF16),
        pltpu.VMEM((NG * 8, 128), F32),
        pltpu.VMEM((NX, tokens * NG, x_lanes), BF16),
        pltpu.VMEM((NX, tokens * NG, x_lanes), BF16),
        pltpu.VMEM((x_lanes // 128, tokens * NG, 128), BF16),
        pltpu.VMEM((NZ, tokens * NG, 128), BF16),
        sem((5,)),
        sem((key_rows // step_keys,)),
        sem,
        sem((NZ,)),
        sem,
        sem,
        sem,
        sem,
        sem((2,)),
        sem((2,)),
        sem((2,)),
        sem((2,)),
        sem,
        sem,
        sem,
        sem,
        sem,
        sem,
    ]
    result = pl.pallas_call(
        functools.partial(kernel, sizes),
        out_shape=jax.ShapeDtypeStruct((tokens * NG, 128), BF16),
        in_specs=[pl.BlockSpec(memory_space=pltpu.HBM)] * 6,
        out_specs=pl.BlockSpec(memory_space=pltpu.VMEM),
        scratch_shapes=scratch,
        compiler_params=pltpu.CompilerParams(
            collective_id=0, has_side_effects=True, vmem_limit_bytes=55220 * 1024
        ),
    )(queries, cache.reshape(key_rows, width), slot_page, lengths, w_uv, w_out)
    return result[:, 0:own_columns].reshape(NG, tokens, own_columns)


def solution(mesh, NX=4):
    NG, pages = mesh.shape["group"], mesh.shape["page"]
    in_specs = (
        P("group", None, "page", None),
        P("group", "page", None, None),
        P("group", "page"),
        P("group"),
        P("page", None, None),
        P("page", "group"),
    )
    out_specs = P(None, None, ("group", "page"))

    def step(queries, cache, slot_page, lengths, w_uv, w_out):
        sizes = (NX, pages // NX, NG, w_out.shape[1] // pages)
        return body(sizes, queries, cache, slot_page, lengths, w_uv, w_out)

    return jax.shard_map(step, mesh=mesh, in_specs=in_specs, out_specs=out_specs, check_vma=False)
```
